32 devices in a mesh: batch: 8 (over z, x), chan: 4 (over y, core).
Axes of the slice: x: 2, y: 2, z: 4, core: 2. Of those that a mesh axis runs over, the one named last changes fastest.
Arguments:
- inputs: bfloat16 [4, 64, 14, 14, 1024], P(None, 'batch', None, None, 'chan'), may hold values from -6 to 6
- weight_in: bfloat16 [1024, 512], P(None, 'chan'), may hold values from -0.1875 to 0.1875
- kernel_one: bfloat16 [3, 3, 512, 512], P(None, None, None, 'chan'), may hold values from -0.09375 to 0.09375
- weight_out: bfloat16 [512, 2048], P(None, 'chan'), may hold values from -0.25 to 0.25
- weight_skip: bfloat16 [1024, 2048], P(None, 'chan'), may hold values from -0.1875 to 0.1875
- second_in: bfloat16 [2048, 512], P(None, 'chan'), may hold values from -0.125 to 0.125
- kernel_two: bfloat16 [3, 3, 512, 512], P(None, None, None, 'chan'), may hold values from -0.09375 to 0.09375
- second_out: bfloat16 [512, 2048], P(None, 'chan'), may hold values from -0.25 to 0.25
- norm_reduce: float32 [2, 512], P(None, 'chan'), may hold values from 0.3 to 1.5
- norm_kernel: float32 [2, 512], P(None, 'chan'), may hold values from 0.3 to 1.5
- norm_expand: float32 [2, 2048], P(None, 'chan'), may hold values from 0.3 to 1.5
- norm_skip: float32 [2, 2048], P(None, 'chan'), may hold values from 0.3 to 1.5
- later_reduce: float32 [2, 512], P(None, 'chan'), may hold values from 0.3 to 1.5
- later_kernel: float32 [2, 512], P(None, 'chan'), may hold values from 0.3 to 1.5
- later_expand: float32 [2, 2048], P(None, 'chan'), may hold values from 0.3 to 1.5
- widths: int32 [4], replicated, may hold values from 256 to 512, as said below
- depths: int32 [4], replicated, may hold values from 1 to 2, as said below
- counts: int32 [4], replicated, may hold values from 32 to 64, as said below
- cotangent: bfloat16 [4, 64, 7, 7, 2048], P(None, 'batch', None, None, 'chan'), may hold values from -6 to 6
Outputs:
- result: bfloat16 [4, 64, 7, 7, 2048], P(None, 'batch', None, None, 'chan')
- inputs_grad: bfloat16 [4, 64, 14, 14, 1024], P(None, 'batch', None, None, 'chan')
- weight_in_grad: float32 [1024, 512], P('batch', 'chan')
- kernel_one_grad: float32 [3, 3, 512, 512], P(None, None, 'batch', 'chan')
- weight_out_grad: float32 [512, 2048], P('batch', 'chan')
- weight_skip_grad: float32 [1024, 2048], P('batch', 'chan')
- second_in_grad: float32 [2048, 512], P('batch', 'chan')
- kernel_two_grad: float32 [3, 3, 512, 512], P(None, None, 'batch', 'chan')
- second_out_grad: float32 [512, 2048], P('batch', 'chan')
- norm_reduce_grad: float32 [2, 512], P(None, 'chan')
- norm_kernel_grad: float32 [2, 512], P(None, 'chan')
- norm_expand_grad: float32 [2, 2048], P(None, 'chan')
- norm_skip_grad: float32 [2, 2048], P(None, 'chan')
- later_reduce_grad: float32 [2, 512], P(None, 'chan')
- later_kernel_grad: float32 [2, 512], P(None, 'chan')
- later_expand_grad: float32 [2, 2048], P(None, 'chan')
The draws below stay inside these ranges and needn't reach their ends.
Inputs may be any that keep to these rules, and one draw needn't show every extreme that they name: widths[0] is 512 and widths[1] is 512/2 (the largest and smallest subnet). depths[0] is 2 and depths[1] is 1. live images of a subnet are its first counts[s] slots; counts[0] is 64 and counts[1] is 32.
All inputs are finite; a program needn't handle non-finite values.
Results may differ from the reference program's by a relative error of at most 0.025.
Values may be sent and summed in bfloat16 or wider, within the bound.
No kernel may reach another device: no remote copies, remote signals or barrier semaphores. Data moves between devices by JAX's collectives and lax.ppermute only.
A program may use at most 320 MiB of HBM per device.

```python
import jax
import jax.numpy as jnp
from jax import lax

CIN = 1024
MID = 512
COUT = 2048
SUBNETS = 4
HIN = 14
HOUT = 7
IMAGES = 64


def draw_widths(key, part):
    key = jax.random.fold_in(key, 11)
    others = jax.random.randint(key, (SUBNETS - 2,), MID // 2, MID + 1).astype(jnp.int32)
    return jnp.concatenate([jnp.array([MID, MID // 2], jnp.int32), others])


def draw_depths(key, part):
    key = jax.random.fold_in(key, 23)
    others = jax.random.randint(key, (SUBNETS - 2,), 1, 3).astype(jnp.int32)
    return jnp.concatenate([jnp.array([2, 1], jnp.int32), others])


def draw_counts(key, part):
    key = jax.random.fold_in(key, 37)
    others = jax.random.randint(key, (SUBNETS - 2,), IMAGES // 2, IMAGES + 1).astype(jnp.int32)
    return jnp.concatenate([jnp.array([IMAGES, IMAGES // 2], jnp.int32), others])


def levels(stream_key, shape, shards, smallest, high):
    gain, own = 1.0, jax.random.fold_in(stream_key, 6)
    for position, parts in shards:
        steps = jnp.exp(jax.random.uniform(jax.random.fold_in(own, position), (parts,), jnp.float32, smallest / len(shards), high / len(shards)))
        gain = gain * jnp.repeat(steps, shape[position] // parts).reshape([-1 if axis == position else 1 for axis in range(len(shape))])
    return gain


def centred(rng, dims, scale, limit, pieces=(), kind=jnp.bfloat16):
    level = levels(rng, dims, pieces, -0.22, 0.18) if pieces else 1.0
    values = jax.random.normal(rng, dims, jnp.float32) * scale * level
    return jnp.minimum(jnp.maximum(values, -limit), limit).astype(kind)


def setup_inputs(seed: int = 0) -> dict:
    arg_keys = jax.random.split(jax.random.key(seed), 20)
    return {
        "inputs": centred(arg_keys[0], (SUBNETS, IMAGES, HIN, HIN, CIN), 1.0, 6.0, ((1, 8), (4, 4))),
        "weight_in": centred(arg_keys[1], (CIN, MID), CIN ** -0.5, 0.1875, ((1, 4),)),
        "kernel_one": centred(arg_keys[2], (3, 3, MID, MID), (9 * MID) ** -0.5, 0.09375, ((3, 4),)),
        "weight_out": centred(arg_keys[3], (MID, COUT), MID ** -0.5, 0.25, ((1, 4),)),
        "weight_skip": centred(arg_keys[4], (CIN, COUT), CIN ** -0.5, 0.1875, ((1, 4),)),
        "second_in": centred(arg_keys[5], (COUT, MID), COUT ** -0.5, 0.125, ((1, 4),)),
        "kernel_two": centred(arg_keys[6], (3, 3, MID, MID), (9 * MID) ** -0.5, 0.09375, ((3, 4),)),
        "second_out": centred(arg_keys[7], (MID, COUT), MID ** -0.5, 0.25, ((1, 4),)),
        "norm_reduce": jnp.clip(0.3 + 1.2 * jax.random.uniform(arg_keys[8], (2, MID), jnp.float32) ** levels(arg_keys[8], (2, MID), ((1, 4),), -0.2, 0.2), 0.3, 1.5),
        "norm_kernel": jnp.clip(0.3 + 1.2 * jax.random.uniform(arg_keys[9], (2, MID), jnp.float32) ** levels(arg_keys[9], (2, MID), ((1, 4),), -0.2, 0.2), 0.3, 1.5),
        "norm_expand": jnp.clip(0.3 + 1.2 * jax.random.uniform(arg_keys[10], (2, COUT), jnp.float32) ** levels(arg_keys[10], (2, COUT), ((1, 4),), -0.2, 0.2), 0.3, 1.5),
        "norm_skip": jnp.clip(0.3 + 1.2 * jax.random.uniform(arg_keys[11], (2, COUT), jnp.float32) ** levels(arg_keys[11], (2, COUT), ((1, 4),), -0.2, 0.2), 0.3, 1.5),
        "later_reduce": jnp.clip(0.3 + 1.2 * jax.random.uniform(arg_keys[12], (2, MID), jnp.float32) ** levels(arg_keys[12], (2, MID), ((1, 4),), -0.2, 0.2), 0.3, 1.5),
        "later_kernel": jnp.clip(0.3 + 1.2 * jax.random.uniform(arg_keys[13], (2, MID), jnp.float32) ** levels(arg_keys[13], (2, MID), ((1, 4),), -0.2, 0.2), 0.3, 1.5),
        "later_expand": jnp.clip(0.3 + 1.2 * jax.random.uniform(arg_keys[14], (2, COUT), jnp.float32) ** levels(arg_keys[14], (2, COUT), ((1, 4),), -0.2, 0.2), 0.3, 1.5),
        "widths": draw_widths(jax.random.fold_in(arg_keys[19], 71), 0),
        "depths": draw_depths(jax.random.fold_in(arg_keys[19], 71), 0),
        "counts": draw_counts(jax.random.fold_in(arg_keys[19], 71), 0),
        "cotangent": centred(arg_keys[18], (SUBNETS, IMAGES, HOUT, HOUT, COUT), 1.0, 6.0, ((1, 8), (4, 4))),
    }


epsilon = 1e-05

@jax.custom_vjp
def low(v):
    return lax.optimization_barrier(v.astype(jnp.bfloat16)).astype(jnp.float32)

@jax.custom_vjp
def low_back(v):
    return v

def low_keep(v):
    return (low(v), None)

def low_pass(kept, grad):
    return (grad,)

def back_keep(v):
    return (v, None)

def back_low(kept, grad):
    return (low(grad),)
low.defvjp(low_keep, low_pass)
low_back.defvjp(back_keep, back_low)

def pointwise(active, weight):
    return jnp.einsum('ihwc,cd->ihwd', active, weight, precision=lax.Precision.HIGHEST)

def spatial(active, kernel, stride):
    return lax.conv_general_dilated(active, kernel, (stride, stride), ((1, 1), (1, 1)), dimension_numbers=('NHWC', 'HWIO', 'NHWC'), precision=lax.Precision.HIGHEST)

def norm_apply(values, keep_mask, affine, pixels):
    average = lax.optimization_barrier(jnp.sum(values * keep_mask, axis=(0, 1, 2))) / pixels
    centered = values - average
    variance = lax.optimization_barrier(jnp.sum(keep_mask * centered * centered, axis=(0, 1, 2))) / pixels
    return keep_mask * (affine[0] * centered * lax.rsqrt(variance + epsilon) + affine[1])

def subnet(image_in, width, depth, count, weight_in, kernel_one, weight_out, weight_skip, second_in, kernel_two, second_out, norm_reduce, norm_kernel, norm_expand, norm_skip, later_reduce, later_kernel, later_expand):
    live = (jnp.arange(IMAGES, dtype=jnp.int32) < count).astype(jnp.float32)[:, None, None, None]
    width_live = (jnp.arange(MID, dtype=jnp.int32) < width).astype(jnp.float32)
    inner = live * width_live
    big_pixels = count.astype(jnp.float32) * (HIN * HIN)
    small_pixels = count.astype(jnp.float32) * (HOUT * HOUT)
    conv_a = low_back(pointwise(image_in, weight_in))
    act_a = low_back(low(jax.nn.silu(norm_apply(conv_a, inner, norm_reduce, big_pixels))))
    conv_b = low_back(low(spatial(act_a, kernel_one, 2)))
    act_b = low(jax.nn.silu(norm_apply(conv_b, inner, norm_kernel, small_pixels)))
    conv_c = low_back(pointwise(act_b, weight_out))
    conv_s = low_back(pointwise(image_in[:, ::2, ::2, :], weight_skip))
    first = jax.nn.silu(norm_apply(conv_c, live, norm_expand, small_pixels) + norm_apply(conv_s, live, norm_skip, small_pixels))
    first_low = low(first)
    conv_d = low_back(pointwise(first_low, second_in))
    act_d = low_back(low(jax.nn.silu(norm_apply(conv_d, inner, later_reduce, small_pixels))))
    conv_e = low_back(low(spatial(act_d, kernel_two, 1)))
    act_e = low(jax.nn.silu(norm_apply(conv_e, inner, later_kernel, small_pixels)))
    conv_f = low_back(pointwise(act_e, second_out))
    second = jax.nn.silu(norm_apply(conv_f, live, later_expand, small_pixels) + first)
    depth_on = (depth == 2).astype(jnp.float32)
    return first + depth_on * (second - first)

def reference(inputs, weight_in, kernel_one, weight_out, weight_skip, second_in, kernel_two, second_out, norm_reduce, norm_kernel, norm_expand, norm_skip, later_reduce, later_kernel, later_expand, widths, depths, counts, cotangent):
    floats = tuple((array.astype(jnp.float32) for array in (inputs, weight_in, kernel_one, weight_out, weight_skip, second_in, kernel_two, second_out, norm_reduce, norm_kernel, norm_expand, norm_skip, later_reduce, later_kernel, later_expand)))

    def forward(image_all, *params):
        outcomes = []
        for member in range(SUBNETS):
            outcomes.append(jax.checkpoint(subnet)(image_all[member], widths[member], depths[member], counts[member], *params))
        return jnp.stack(outcomes)
    result, pullback = jax.vjp(forward, *floats)
    grads = pullback(cotangent.astype(jnp.float32))
    return (result.astype(jnp.bfloat16), grads[0].astype(jnp.bfloat16), grads[1], grads[2], grads[3], grads[4], grads[5], grads[6], grads[7], grads[8], grads[9], grads[10], grads[11], grads[12], grads[13], grads[14])
```

```python
import jax
import jax.numpy as jnp
from jax import lax
from jax.experimental import pallas as pl
from jax.experimental.pallas import tpu as pltpu
from jax.sharding import PartitionSpec as P

EPS = 1e-05
F32 = jnp.float32
BF = jnp.bfloat16
MID = 512
Q = 4
R = 392
NT = (((1,), (1,)), ((), ()))
TN = (((0,), (0,)), ((), ()))
VMEM_LIMIT = 48 * 1024 * 1024


def call(body, grid, ins, outs, scratch=(), flops=0, moved=0):
    in_specs = []
    for item in ins:
        if item[1] is None:
            in_specs.append(pl.BlockSpec(memory_space=pltpu.SMEM))
        else:
            in_specs.append(pl.BlockSpec(item[1], item[2]))
    return pl.pallas_call(
        body,
        grid=grid,
        in_specs=in_specs,
        out_specs=[pl.BlockSpec(item[2], item[3]) for item in outs],
        out_shape=[jax.ShapeDtypeStruct(item[0], item[1]) for item in outs],
        scratch_shapes=list(scratch),
        compiler_params=pltpu.CompilerParams(vmem_limit_bytes=VMEM_LIMIT),
        cost_estimate=pl.CostEstimate(flops=int(flops), bytes_accessed=int(moved), transcendentals=0),
    )(*[item[0] for item in ins])


def whole(array):
    zeros = (0,) * array.ndim
    return (array, array.shape, lambda i: zeros)


def bands():
    return [slice(56 * h, 56 * h + 56) for h in range(7)]


def tall(value):
    return value.reshape(7, 8, value.shape[-1])


def dot(left, right, dims=(((1,), (0,)), ((), ()))):
    return lax.dot_general(left, right, dims, preferred_element_type=F32)


def mean_inv(sums, pixels):
    total = jnp.sum(sums, axis=0)
    mean = total[:, :MID] / pixels
    var = jnp.maximum(total[:, MID : 2 * MID] / pixels - mean * mean, 0.0)
    return mean, lax.rsqrt(var + EPS)


def forward_coef(sums, affine, mask, pixels):
    mean, inv = mean_inv(sums, pixels)
    scale = affine[0:1] * inv
    return mask * scale, mask * (affine[1:2] - mean * scale), mean, inv


def backward_coef(sums, grad_sums, which, affine, mask, pixels):
    mean, inv = mean_inv(sums, pixels)
    total = jnp.sum(grad_sums, axis=0)
    first = total[:, :MID] / pixels
    second = total[:, which * MID : (which + 1) * MID] / pixels
    scale = affine[0:1] * inv
    slope = -scale * second * inv
    return mask * scale, mask * slope, mask * (-scale * first - slope * mean)


def silu(u):
    return u * jax.nn.sigmoid(u)


def silu_both(u):
    s = jax.nn.sigmoid(u)
    return u * s, s * (1.0 + u * (1.0 - s))


def silu_slope(u):
    s = jax.nn.sigmoid(u)
    return s * (1.0 + u * (1.0 - s))


def fold(acc, value):
    return acc + jnp.sum(tall(value), axis=0)


def put_sums(ref, parts):
    row = jnp.concatenate([jnp.sum(part, axis=0, keepdims=True) for part in parts], axis=1)
    ref[...] = jnp.broadcast_to(row[None], ref.shape)


def value_sums(out_ref, pieces, live):
    first = jnp.zeros((8, MID), F32)
    second = jnp.zeros((8, MID), F32)
    for value in pieces:
        first = fold(first, value)
        second = fold(second, value * value)
    put_sums(out_ref, [first * live, second * live])


def rows_in(inputs):
    subnets, images, size, _, width = inputs.shape
    cut = inputs.reshape(subnets, images, size // 2, 2, size // 2, 2, width)
    return jnp.transpose(cut, (0, 3, 5, 2, 4, 1, 6)).reshape(subnets, 4, R, width)


def rows_out(rows, subnets):
    cut = rows.reshape(subnets, 2, 2, 7, 7, 8, rows.shape[3])
    return jnp.transpose(cut, (0, 5, 3, 1, 4, 2, 6)).reshape(subnets, 8, 14, 14, rows.shape[3])


def small_in(maps):
    return jnp.transpose(maps, (0, 2, 3, 1, 4)).reshape(maps.shape[0], R, maps.shape[4])


def small_out(rows, subnets):
    return jnp.transpose(rows.reshape(subnets, 7, 7, 8, rows.shape[2]), (0, 3, 1, 2, 4))


def lanes(ref):
    return jnp.concatenate([ref[j] for j in range(ref.shape[0])], axis=1)


def stage_a(slabs, weight, live, nb):
    nch, width = slabs.shape[0], slabs.shape[3]
    cin = nch * width

    def body(x_ref, w_ref, live_ref, a_ref, s_ref, sums):
        p = pl.program_id(0)
        x = jnp.concatenate([x_ref[k, 0] for k in range(nch)], axis=1)
        w = lanes(w_ref)
        value = dot(x, w)
        a_ref[0] = value

        @pl.when(p == 0)
        def _():
            sums[...] = jnp.zeros_like(sums)

        first = jnp.zeros((8, MID), F32)
        second = jnp.zeros((8, MID), F32)
        for band in bands():
            piece = value[band]
            first = fold(first, piece)
            second = fold(second, piece * piece)
        sums[0] += first
        sums[1] += second

        @pl.when(p == 3)
        def _():
            put_sums(s_ref, [sums[0] * live_ref[...], sums[1] * live_ref[...]])

    return call(
        body,
        (4,),
        [(slabs, (nch, 1, R, width), lambda i: (0, i, 0, 0)), whole(weight), whole(live)],
        [
            ((4, R, MID), F32, (1, R, MID), lambda i: (i, 0, 0)),
            ((nb, 1, 2 * MID), F32, (nb, 1, 2 * MID), lambda i: (0, 0, 0)),
        ],
        [pltpu.VMEM((2, 8, MID), F32)],
        flops=2 * 4 * R * cin * MID,
        moved=4 * R * (2 * cin + 4 * MID) + 2 * cin * MID,
    )


def stage_skip(slabs, weight, live, nb):
    nch, width = slabs.shape[0], slabs.shape[3]
    cin = nch * width

    def body(x_ref, w_ref, live_ref, o_ref, s_ref):
        x = jnp.concatenate([x_ref[k, 0] for k in range(nch)], axis=1)
        value = dot(x, w_ref[0])
        o_ref[...] = value
        value_sums(s_ref, [value[band] for band in bands()], live_ref[...])

    return call(
        body,
        (Q,),
        [
            (slabs, (nch, 1, R, width), lambda i: (0, 0, 0, 0)),
            (weight, (1, cin, MID), lambda i: (i, 0, 0)),
            whole(live),
        ],
        [
            ((R, Q * MID), F32, (R, MID), lambda i: (0, i)),
            ((nb, 1, Q * 2 * MID), F32, (nb, 1, 2 * MID), lambda i: (0, 0, i)),
        ],
        flops=2 * R * cin * Q * MID,
        moved=2 * R * cin + Q * MID * (2 * cin + 4 * R),
    )


def stage_conv_one(conv_a, sums_a, affine, inner, live, kernel, table, nb):
    def body(t_ref, a_ref, s_ref, g_ref, inner_ref, live_ref, k_ref, cols_ref, b_ref, o_ref, pad, acc):
        i = pl.program_id(0)

        @pl.when(i == 0)
        def _():
            scale, shift, _, _ = forward_coef(s_ref[...], g_ref[...], inner_ref[...], t_ref[0])
            pad[1, :, 0] = jnp.zeros((2, 8, 8, MID), F32)
            pad[:, 1, :, 0] = jnp.zeros((2, 8, 8, MID), F32)
            for p in range(4):
                for h, band in enumerate(bands()):
                    u = tall(a_ref[p, band]) * scale + shift
                    pad[p // 2, p % 2, h + 1, 1:8] = silu(u)

        hp = jnp.where(i == 1, 0, 1)
        h0 = jnp.minimum(i, 1)
        taps = []
        for dw in range(3):
            wp = 0 if dw == 1 else 1
            w0 = 0 if dw == 0 else 1
            tap = pad[hp, wp, pl.ds(h0, 7), w0 : w0 + 7].reshape(R, MID).astype(BF)
            cols_ref[:, dw * MID : (dw + 1) * MID] = tap
            taps.append(tap)
        value = sum(dot(taps[dw], jnp.concatenate([k_ref[j, dw] for j in range(Q)], axis=1)) for dw in range(3))

        @pl.when(i == 0)
        def _():
            acc[...] = value

        @pl.when(i > 0)
        def _():
            acc[...] += value

        @pl.when(i == 2)
        def _():
            low = acc[...].astype(BF).astype(F32)
            b_ref[...] = low
            value_sums(o_ref, [low[band] for band in bands()], live_ref[...])

    return call(
        body,
        (3,),
        [
            (table, None),
            whole(conv_a),
            whole(sums_a),
            whole(affine),
            whole(inner),
            whole(live),
            (kernel, (Q, 3, MID, MID // Q), lambda i: (0, i, 0, 0)),
        ],
        [
            ((R, 9 * MID), BF, (R, 3 * MID), lambda i: (0, i)),
            ((R, MID), F32, (R, MID), lambda i: (0, 0)),
            ((nb, 1, 2 * MID), F32, (nb, 1, 2 * MID), lambda i: (0, 0, 0)),
        ],
        [pltpu.VMEM((2, 2, 8, 8, 8, MID), F32), pltpu.VMEM((R, MID), F32)],
        flops=2 * R * 9 * MID * MID,
        moved=4 * 4 * R * MID + 2 * R * 9 * MID + 2 * 9 * MID * MID,
    )


def stage_conv_two(conv_d, sums_d, affine, inner, live, kernel, table, nb):
    def body(t_ref, d_ref, s_ref, g_ref, inner_ref, live_ref, k_ref, cols_ref, e_ref, o_ref, pad, acc):
        i = pl.program_id(0)

        @pl.when(i == 0)
        def _():
            scale, shift, _, _ = forward_coef(s_ref[...], g_ref[...], inner_ref[...], t_ref[1])
            pad[...] = jnp.zeros_like(pad)
            for h, band in enumerate(bands()):
                u = tall(d_ref[band]) * scale + shift
                pad[h + 1, 1:8] = silu(u)

        taps = []
        for dw in range(3):
            tap = pad[pl.ds(i, 7), dw : dw + 7].reshape(R, MID).astype(BF)
            cols_ref[:, dw * MID : (dw + 1) * MID] = tap
            taps.append(tap)
        value = sum(dot(taps[dw], jnp.concatenate([k_ref[j, dw] for j in range(Q)], axis=1)) for dw in range(3))

        @pl.when(i == 0)
        def _():
            acc[...] = value

        @pl.when(i > 0)
        def _():
            acc[...] += value

        @pl.when(i == 2)
        def _():
            low = acc[...].astype(BF).astype(F32)
            e_ref[...] = low
            value_sums(o_ref, [low[band] for band in bands()], live_ref[...])

    return call(
        body,
        (3,),
        [
            (table, None),
            whole(conv_d),
            whole(sums_d),
            whole(affine),
            whole(inner),
            whole(live),
            (kernel, (Q, 3, MID, MID // Q), lambda i: (0, i, 0, 0)),
        ],
        [
            ((R, 9 * MID), BF, (R, 3 * MID), lambda i: (0, i)),
            ((R, MID), F32, (R, MID), lambda i: (0, 0)),
            ((nb, 1, 2 * MID), F32, (nb, 1, 2 * MID), lambda i: (0, 0, 0)),
        ],
        [pltpu.VMEM((9, 9, 8, MID), F32), pltpu.VMEM((R, MID), F32)],
        flops=2 * R * 9 * MID * MID,
        moved=4 * R * MID + 2 * R * 9 * MID + 2 * 9 * MID * MID,
    )


def stage_expand(conv, sums, affine, inner, live, weight, table, nb):
    def body(t_ref, b_ref, s_ref, g_ref, inner_ref, live_ref, w_ref, act_ref, o_ref, sum_ref, wide):
        i = pl.program_id(0)

        @pl.when(i == 0)
        def _():
            scale, shift, _, _ = forward_coef(s_ref[...], g_ref[...], inner_ref[...], t_ref[1])
            for band in bands():
                u = tall(b_ref[band]) * scale + shift
                wide[band] = silu(u).reshape(56, MID)
            act_ref[...] = wide[...].astype(BF)

        value = dot(act_ref[...], w_ref[0])
        o_ref[...] = value
        value_sums(sum_ref, [value[band] for band in bands()], live_ref[...])

    return call(
        body,
        (Q,),
        [
            (table, None),
            whole(conv),
            whole(sums),
            whole(affine),
            whole(inner),
            whole(live),
            (weight, (1, MID, MID), lambda i: (i, 0, 0)),
        ],
        [
            ((R, MID), BF, (R, MID), lambda i: (0, 0)),
            ((R, Q * MID), F32, (R, MID), lambda i: (0, i)),
            ((nb, 1, Q * 2 * MID), F32, (nb, 1, 2 * MID), lambda i: (0, 0, i)),
        ],
        [pltpu.VMEM((R, MID), F32)],
        flops=2 * R * MID * Q * MID,
        moved=4 * R * MID * (Q + 1) + 2 * MID * MID * Q,
    )


def chunk(array, parts=1):
    return (array, (array.shape[0], parts * MID), lambda i: (0, i))


def sum_chunk(array, parts=2):
    return (array, (array.shape[0], 1, parts * MID), lambda i: (0, 0, i))


def stage_join(conv_c, sums_c, affine_c, conv_s, sums_s, affine_s, live, weight, table, nb):
    def body(t_ref, c_ref, sc_ref, gc_ref, v_ref, sv_ref, gv_ref, live_ref, w_ref, f_ref, low_ref, d_ref, o_ref, acc):
        i = pl.program_id(0)
        live = live_ref[...]
        scale_c, shift_c, _, _ = forward_coef(sc_ref[...], gc_ref[...], live, t_ref[1])
        scale_s, shift_s, _, _ = forward_coef(sv_ref[...], gv_ref[...], live, t_ref[1])
        shift = shift_c + shift_s
        for band in bands():
            u = tall(c_ref[band]) * scale_c + tall(v_ref[band]) * scale_s + shift
            f_ref[band] = silu(u).reshape(56, MID)
        low = f_ref[...].astype(BF)
        low_ref[...] = low
        value = dot(low, lanes(w_ref))

        @pl.when(i == 0)
        def _():
            acc[...] = value

        @pl.when(i > 0)
        def _():
            acc[...] += value

        @pl.when(i == Q - 1)
        def _():
            total = acc[...]
            d_ref[...] = total
            value_sums(o_ref, [total[band] for band in bands()], live)

    return call(
        body,
        (Q,),
        [
            (table, None),
            chunk(conv_c),
            sum_chunk(sums_c),
            chunk(affine_c),
            chunk(conv_s),
            sum_chunk(sums_s),
            chunk(affine_s),
            whole(live),
            (weight, (Q, MID, MID // Q), lambda i: (0, i, 0)),
        ],
        [
            ((R, Q * MID), F32, (R, MID), lambda i: (0, i)),
            ((R, Q * MID), BF, (R, MID), lambda i: (0, i)),
            ((R, MID), F32, (R, MID), lambda i: (0, 0)),
            ((nb, 1, 2 * MID), F32, (nb, 1, 2 * MID), lambda i: (0, 0, 0)),
        ],
        [pltpu.VMEM((R, MID), F32)],
        flops=2 * R * MID * Q * MID,
        moved=14 * R * MID * Q + 2 * MID * MID * Q,
    )


def stage_result(conv_f, sums_f, affine, first, cotangent, live, table, nb):
    nch, width = cotangent.shape[0], cotangent.shape[2]
    per = nch // Q

    def body(t_ref, f_ref, s_ref, g_ref, y_ref, ct_ref, live_ref, r_ref, gs_ref, o_ref, wide):
        live = live_ref[...]
        on = t_ref[2]
        scale, shift, mean, inv = forward_coef(s_ref[...], g_ref[...], live, t_ref[1])
        ct = jnp.concatenate([ct_ref[k] for k in range(per)], axis=1).astype(F32)
        first_sum = jnp.zeros((8, MID), F32)
        second_sum = jnp.zeros((8, MID), F32)
        for band in bands():
            v = tall(f_ref[band])
            y = tall(y_ref[band])
            u = v * scale + shift + y
            second, slope = silu_both(u)
            wide[band] = (y + on * (second - y)).reshape(56, MID)
            grad = on * tall(ct[band]) * slope
            gs_ref[band] = grad.reshape(56, MID)
            first_sum = first_sum + jnp.sum(grad, axis=0)
            second_sum = second_sum + jnp.sum(grad * (v - mean), axis=0)
        result = wide[...].astype(BF)
        for k in range(per):
            r_ref[k] = result[:, k * width : (k + 1) * width]
        put_sums(o_ref, [first_sum * live, second_sum * live * inv])

    return call(
        body,
        (Q,),
        [
            (table, None),
            chunk(conv_f),
            sum_chunk(sums_f),
            chunk(affine),
            chunk(first),
            (cotangent, (per, R, width), lambda i: (i, 0, 0)),
            whole(live),
        ],
        [
            ((nch, R, width), BF, (per, R, width), lambda i: (i, 0, 0)),
            ((R, Q * MID), F32, (R, MID), lambda i: (0, i)),
            ((nb, 1, Q * 2 * MID), F32, (nb, 1, 2 * MID), lambda i: (0, 0, i)),
        ],
        [pltpu.VMEM((R, MID), F32)],
        moved=16 * R * Q * MID,
    )


def finish_inner(grad, conv_ref, sums, affine, mask, pixels, out_put, sum_ref):
    scale, shift, mean, inv = forward_coef(sums, affine, mask, pixels)
    first = jnp.zeros((8, MID), F32)
    second = jnp.zeros((8, MID), F32)
    for band in bands():
        v = tall(conv_ref[band])
        gy = mask * (tall(grad[band]) * silu_slope(v * scale + shift))
        out_put(band, gy.reshape(56, MID))
        first = first + jnp.sum(gy, axis=0)
        second = second + jnp.sum(gy * (v - mean), axis=0)
    put_sums(sum_ref, [first, second * inv])


def stage_back_f(gs, conv_f, sums_f, grad_f, affine_f, live, weight, conv_e, sums_e, affine_e, inner, table, nb):
    def body(
        t_ref, gs_ref, f_ref, sf_ref, gf_ref, af_ref, live_ref, w_ref, e_ref, se_ref, ae_ref, inner_ref,
        low_ref, gy_ref, o_ref, acc, wide,
    ):
        i = pl.program_id(0)
        a, b, c = backward_coef(sf_ref[...], gf_ref[...], 1, af_ref[...], live_ref[...], t_ref[1])
        for band in bands():
            wide[band] = (tall(gs_ref[band]) * a + tall(f_ref[band]) * b + c).reshape(56, MID)
        low = wide[...].astype(BF)
        low_ref[...] = low
        value = dot(low, w_ref[0], NT)

        @pl.when(i == 0)
        def _():
            acc[...] = value

        @pl.when(i > 0)
        def _():
            acc[...] += value

        @pl.when(i == Q - 1)
        def _():
            def put(band, piece):
                gy_ref[band] = piece

            finish_inner(acc, e_ref, se_ref[...], ae_ref[...], inner_ref[...], t_ref[1], put, o_ref)

    return call(
        body,
        (Q,),
        [
            (table, None),
            chunk(gs),
            chunk(conv_f),
            sum_chunk(sums_f),
            sum_chunk(grad_f),
            chunk(affine_f),
            whole(live),
            (weight, (1, MID, MID), lambda i: (i, 0, 0)),
            whole(conv_e),
            whole(sums_e),
            whole(affine_e),
            whole(inner),
        ],
        [
            ((R, Q * MID), BF, (R, MID), lambda i: (0, i)),
            ((R, MID), F32, (R, MID), lambda i: (0, 0)),
            ((nb, 1, 2 * MID), F32, (nb, 1, 2 * MID), lambda i: (0, 0, 0)),
        ],
        [pltpu.VMEM((R, MID), F32), pltpu.VMEM((R, MID), F32)],
        flops=2 * R * MID * Q * MID,
        moved=10 * R * MID * Q + 2 * MID * MID * Q,
    )


def stage_back_two(gy_e, conv_e, sums_e, grad_e, affine_e, kernel, conv_d, sums_d, affine_d, inner, table, nb):
    def body(
        t_ref, gy_ref, e_ref, se_ref, ge_ref, ae_ref, k_ref, d_ref, sd_ref, ad_ref, inner_ref,
        low_ref, out_ref, o_ref, pad, acc, wide,
    ):
        i = pl.program_id(0)

        @pl.when(i == 0)
        def _():
            a, b, c = backward_coef(se_ref[...], ge_ref[...], 1, ae_ref[...], inner_ref[...], t_ref[1])
            pad[...] = jnp.zeros_like(pad)
            for h, band in enumerate(bands()):
                value = tall(gy_ref[band]) * a + tall(e_ref[band]) * b + c
                wide[band] = value.reshape(56, MID)
                pad[h + 1, 1:8] = value
            low_ref[...] = wide[...].astype(BF)

        total = None
        for dw in range(3):
            tap = pad[pl.ds(2 - i, 7), 2 - dw : 9 - dw].reshape(R, MID).astype(BF)
            part = dot(tap, jnp.concatenate([k_ref[j, dw] for j in range(Q)], axis=1), NT)
            total = part if total is None else total + part

        @pl.when(i == 0)
        def _():
            acc[...] = total

        @pl.when(i > 0)
        def _():
            acc[...] += total

        @pl.when(i == 2)
        def _():
            low = acc[...].astype(BF).astype(F32)

            def put(band, piece):
                out_ref[band] = piece

            finish_inner(low, d_ref, sd_ref[...], ad_ref[...], inner_ref[...], t_ref[1], put, o_ref)

    return call(
        body,
        (3,),
        [
            (table, None),
            whole(gy_e),
            whole(conv_e),
            whole(sums_e),
            whole(grad_e),
            whole(affine_e),
            (kernel, (Q, 3, MID, MID // Q), lambda i: (0, i, 0, 0)),
            whole(conv_d),
            whole(sums_d),
            whole(affine_d),
            whole(inner),
        ],
        [
            ((R, MID), BF, (R, MID), lambda i: (0, 0)),
            ((R, MID), F32, (R, MID), lambda i: (0, 0)),
            ((nb, 1, 2 * MID), F32, (nb, 1, 2 * MID), lambda i: (0, 0, 0)),
        ],
        [pltpu.VMEM((9, 9, 8, MID), F32), pltpu.VMEM((R, MID), F32), pltpu.VMEM((R, MID), F32)],
        flops=2 * R * 9 * MID * MID,
        moved=16 * R * MID + 2 * 9 * MID * MID,
    )


def stage_back_join(
    gy_d, conv_d, sums_d, grad_d, affine_d, inner, weight, cotangent, gs, conv_c, sums_c, affine_c, conv_s, sums_s,
    affine_s, live, table, nb,
):
    nch, width = cotangent.shape[0], cotangent.shape[2]
    per = nch // Q

    def body(
        t_ref, gy_ref, d_ref, sd_ref, gd_ref, ad_ref, inner_ref, w_ref, ct_ref, gs_ref, c_ref, sc_ref, ac_ref, v_ref,
        sv_ref, av_ref, live_ref, low_ref, out_ref, o_ref, wide,
    ):
        i = pl.program_id(0)
        live = live_ref[...]

        @pl.when(i == 0)
        def _():
            a, b, c = backward_coef(sd_ref[...], gd_ref[...], 1, ad_ref[...], inner_ref[...], t_ref[1])
            for band in bands():
                wide[band] = (tall(gy_ref[band]) * a + tall(d_ref[band]) * b + c).reshape(56, MID)
            low_ref[...] = wide[...].astype(BF)

        back = dot(low_ref[...], lanes(w_ref), NT)
        ct = jnp.concatenate([ct_ref[k] for k in range(per)], axis=1).astype(F32)
        scale_c, shift_c, mean_c, inv_c = forward_coef(sc_ref[...], ac_ref[...], live, t_ref[1])
        scale_s, shift_s, mean_s, inv_s = forward_coef(sv_ref[...], av_ref[...], live, t_ref[1])
        shift = shift_c + shift_s
        off = 1.0 - t_ref[2]
        one = jnp.zeros((8, MID), F32)
        two = jnp.zeros((8, MID), F32)
        three = jnp.zeros((8, MID), F32)
        for band in bands():
            c = tall(c_ref[band])
            v = tall(v_ref[band])
            u = c * scale_c + v * scale_s + shift
            grad = off * tall(ct[band]) + tall(gs_ref[band]) + tall(back[band])
            grad = live * (grad * silu_slope(u))
            out_ref[band] = grad.reshape(56, MID)
            one = one + jnp.sum(grad, axis=0)
            two = two + jnp.sum(grad * (c - mean_c), axis=0)
            three = three + jnp.sum(grad * (v - mean_s), axis=0)
        put_sums(o_ref, [one, two * inv_c, three * inv_s])

    return call(
        body,
        (Q,),
        [
            (table, None),
            whole(gy_d),
            whole(conv_d),
            whole(sums_d),
            whole(grad_d),
            whole(affine_d),
            whole(inner),
            (weight, (Q, MID, MID // Q), lambda i: (0, i, 0)),
            (cotangent, (per, R, width), lambda i: (i, 0, 0)),
            chunk(gs),
            chunk(conv_c),
            sum_chunk(sums_c),
            chunk(affine_c),
            chunk(conv_s),
            sum_chunk(sums_s),
            chunk(affine_s),
            whole(live),
        ],
        [
            ((R, MID), BF, (R, MID), lambda i: (0, 0)),
            ((R, Q * MID), F32, (R, MID), lambda i: (0, i)),
            ((nb, 1, Q * 3 * MID), F32, (nb, 1, 3 * MID), lambda i: (0, 0, i)),
        ],
        [pltpu.VMEM((R, MID), F32)],
        flops=2 * R * MID * Q * MID,
        moved=18 * R * MID * Q + 2 * MID * MID * Q,
    )


def stage_back_first(
    grad, sums_g, conv_c, sums_c, affine_c, conv_s, sums_s, affine_s, live, weight, conv_b, sums_b, affine_b, inner,
    table, nb,
):
    def body(
        t_ref, g_ref, sg_ref, c_ref, sc_ref, ac_ref, v_ref, sv_ref, av_ref, live_ref, w_ref, b_ref, sb_ref, ab_ref,
        inner_ref, lowc_ref, lows_ref, out_ref, o_ref, acc, wide,
    ):
        i = pl.program_id(0)
        live = live_ref[...]
        a, b, c = backward_coef(sv_ref[...], sg_ref[...], 2, av_ref[...], live, t_ref[1])
        for band in bands():
            wide[band] = (tall(g_ref[band]) * a + tall(v_ref[band]) * b + c).reshape(56, MID)
        lows_ref[...] = wide[...].astype(BF)
        a, b, c = backward_coef(sc_ref[...], sg_ref[...], 1, ac_ref[...], live, t_ref[1])
        for band in bands():
            wide[band] = (tall(g_ref[band]) * a + tall(c_ref[band]) * b + c).reshape(56, MID)
        low = wide[...].astype(BF)
        lowc_ref[...] = low
        value = dot(low, w_ref[0], NT)

        @pl.when(i == 0)
        def _():
            acc[...] = value

        @pl.when(i > 0)
        def _():
            acc[...] += value

        @pl.when(i == Q - 1)
        def _():
            def put(band, piece):
                out_ref[band] = piece

            finish_inner(acc, b_ref, sb_ref[...], ab_ref[...], inner_ref[...], t_ref[1], put, o_ref)

    return call(
        body,
        (Q,),
        [
            (table, None),
            chunk(grad),
            sum_chunk(sums_g, 3),
            chunk(conv_c),
            sum_chunk(sums_c),
            chunk(affine_c),
            chunk(conv_s),
            sum_chunk(sums_s),
            chunk(affine_s),
            whole(live),
            (weight, (1, MID, MID), lambda i: (i, 0, 0)),
            whole(conv_b),
            whole(sums_b),
            whole(affine_b),
            whole(inner),
        ],
        [
            ((R, Q * MID), BF, (R, MID), lambda i: (0, i)),
            ((R, Q * MID), BF, (R, MID), lambda i: (0, i)),
            ((R, MID), F32, (R, MID), lambda i: (0, 0)),
            ((nb, 1, 2 * MID), F32, (nb, 1, 2 * MID), lambda i: (0, 0, 0)),
        ],
        [pltpu.VMEM((R, MID), F32), pltpu.VMEM((R, MID), F32)],
        flops=2 * R * MID * Q * MID,
        moved=16 * R * MID * Q + 2 * MID * MID * Q,
    )


def stage_back_skip(low, weight):
    cin = weight.shape[1]

    def body(g_ref, w_ref, o_ref):
        i = pl.program_id(0)
        value = dot(g_ref[...], w_ref[0], NT)

        @pl.when(i == 0)
        def _():
            o_ref[...] = value

        @pl.when(i > 0)
        def _():
            o_ref[...] += value

    return call(
        body,
        (Q,),
        [chunk(low), (weight, (1, cin, MID), lambda i: (i, 0, 0))],
        [((R, cin), F32, (R, cin), lambda i: (0, 0))],
        flops=2 * R * cin * Q * MID,
        moved=4 * R * cin + 2 * R * Q * MID + 2 * cin * Q * MID,
    )[0]


def stage_back_one(gy_b, conv_b, sums_b, grad_b, affine_b, kernel, conv_a, sums_a, affine_a, inner, table, nb):
    def body(
        t_ref, gy_ref, b_ref, sb_ref, gb_ref, ab_ref, k_ref, a_ref, sa_ref, aa_ref, inner_ref,
        low_ref, out_ref, o_ref, pad, acc, wide,
    ):
        i = pl.program_id(0)

        @pl.when(i == 0)
        def _():
            a, b, c = backward_coef(sb_ref[...], gb_ref[...], 1, ab_ref[...], inner_ref[...], t_ref[1])
            pad[7] = jnp.zeros((8, 8, MID), F32)
            pad[:, 7] = jnp.zeros((8, 8, MID), F32)
            for h, band in enumerate(bands()):
                value = tall(gy_ref[band]) * a + tall(b_ref[band]) * b + c
                wide[band] = value.reshape(56, MID)
                pad[h, 0:7] = value
            low_ref[...] = wide[...].astype(BF)

        h0 = jnp.where(i == 0, 1, 0)
        near = pad[pl.ds(h0, 7), 0:7].reshape(R, MID).astype(BF)
        far = pad[pl.ds(h0, 7), 1:8].reshape(R, MID).astype(BF)
        k = [jnp.concatenate([k_ref[j, dw] for j in range(Q)], axis=1) for dw in range(3)]
        even = dot(near, k[1], NT)
        odd = dot(far, k[0], NT) + dot(near, k[2], NT)

        @pl.when(i == 0)
        def _():
            acc[2] = even
            acc[3] = odd

        @pl.when(i == 1)
        def _():
            acc[0] = even
            acc[1] = odd

        @pl.when(i == 2)
        def _():
            acc[2] += even
            acc[3] += odd
            mask = inner_ref[...]
            scale, shift, mean, inv = forward_coef(sa_ref[...], aa_ref[...], mask, t_ref[0])
            first = jnp.zeros((8, MID), F32)
            second = jnp.zeros((8, MID), F32)
            for p in range(4):
                wide[...] = acc[p].astype(BF).astype(F32)
                for band in bands():
                    v = tall(a_ref[p, band])
                    gy = mask * (tall(wide[band]) * silu_slope(v * scale + shift))
                    out_ref[p, band] = gy.reshape(56, MID)
                    first = first + jnp.sum(gy, axis=0)
                    second = second + jnp.sum(gy * (v - mean), axis=0)
            put_sums(o_ref, [first, second * inv])

    return call(
        body,
        (3,),
        [
            (table, None),
            whole(gy_b),
            whole(conv_b),
            whole(sums_b),
            whole(grad_b),
            whole(affine_b),
            (kernel, (Q, 3, MID, MID // Q), lambda i: (0, i, 0, 0)),
            whole(conv_a),
            whole(sums_a),
            whole(affine_a),
            whole(inner),
        ],
        [
            ((R, MID), BF, (R, MID), lambda i: (0, 0)),
            ((4, R, MID), F32, (4, R, MID), lambda i: (0, 0, 0)),
            ((nb, 1, 2 * MID), F32, (nb, 1, 2 * MID), lambda i: (0, 0, 0)),
        ],
        [pltpu.VMEM((8, 8, 8, MID), F32), pltpu.VMEM((4, R, MID), F32), pltpu.VMEM((R, MID), F32)],
        flops=2 * R * 9 * MID * MID,
        moved=32 * R * MID + 2 * 9 * MID * MID,
    )


def stage_back_in(gy_a, conv_a, sums_a, grad_a, affine_a, weight, skip_grad, inner, table, nch):
    cin = weight.shape[1]
    width = cin // nch

    def body(t_ref, gy_ref, a_ref, sa_ref, ga_ref, aa_ref, w_ref, s_ref, inner_ref, low_ref, out_ref, wide):
        i = pl.program_id(0)
        a, b, c = backward_coef(sa_ref[...], ga_ref[...], 1, aa_ref[...], inner_ref[...], t_ref[0])
        for band in bands():
            wide[band] = (tall(gy_ref[0, band]) * a + tall(a_ref[0, band]) * b + c).reshape(56, MID)
        low = wide[...].astype(BF)
        low_ref[0] = low
        value = dot(low, lanes(w_ref), NT)

        @pl.when(i == 0)
        def _():
            both = (value + s_ref[...]).astype(BF)
            for k in range(nch):
                out_ref[k, 0] = both[:, k * width : (k + 1) * width]

        @pl.when(i > 0)
        def _():
            both = value.astype(BF)
            for k in range(nch):
                out_ref[k, 0] = both[:, k * width : (k + 1) * width]

    return call(
        body,
        (4,),
        [
            (table, None),
            (gy_a, (1, R, MID), lambda i: (i, 0, 0)),
            (conv_a, (1, R, MID), lambda i: (i, 0, 0)),
            whole(sums_a),
            whole(grad_a),
            whole(affine_a),
            whole(weight),
            whole(skip_grad),
            whole(inner),
        ],
        [
            ((4, R, MID), BF, (1, R, MID), lambda i: (i, 0, 0)),
            ((nch, 4, R, width), BF, (nch, 1, R, width), lambda i: (0, i, 0, 0)),
        ],
        [pltpu.VMEM((R, MID), F32)],
        flops=2 * 4 * R * cin * MID,
        moved=4 * R * (10 * MID + 2 * cin) + 2 * cin * MID + 4 * R * cin,
    )


def after(value, *others):
    return lax.optimization_barrier((value,) + others)[0]


NEAR = [(i, i ^ 1) for i in range(Q)]
FAR = [(i, i ^ 2) for i in range(Q)]


def gather_far(part, nch):
    return lax.ppermute(part, "chan", FAR) if nch == Q else None


def gather_far_slices(parts, nb, nch):
    if nch != Q:
        return [None] * len(parts)
    b = lax.axis_index("batch")
    slices = [lax.dynamic_index_in_dim(part.reshape(nb, -1, part.shape[-1]), b, 0, keepdims=False) for part in parts]
    return [lax.ppermute(piece, "chan", FAR) for piece in slices]


def share(piece, shape, nb):
    got = lax.all_to_all(jnp.broadcast_to(piece[None], (nb,) + piece.shape), "batch", 0, 0)
    return got.reshape(shape)


def gather_rest(part, other, nch):
    if nch == Q:
        c = lax.axis_index("chan")
        parts = [part, lax.ppermute(part, "chan", NEAR), other, lax.ppermute(other, "chan", NEAR)]
        return place(parts, c)
    full = lax.all_gather(part, "chan", axis=part.ndim - 1, tiled=True)
    cut = full.reshape(full.shape[:-1] + (Q, full.shape[-1] // Q))
    return jnp.moveaxis(cut, -2, 0)


def place(parts, c):
    shape = parts[0].shape
    cuts = shape[0] // 3 if len(shape) == 3 else 1
    block = (3,) + shape[1:] if len(shape) == 3 else shape
    rest = (0,) * (len(shape) - 1)

    def body(c_ref, *refs):
        k = pl.program_id(0)
        out = refs[Q]
        for j in range(Q):

            @pl.when(k == j)
            def _():
                out[0] = refs[j][...]

    def spec(j):
        def index(k, i, c_ref):
            return (jnp.where(k == j, i, jnp.where(k < j, 0, cuts - 1)),) + rest

        return pl.BlockSpec(block, index)

    grid_spec = pltpu.PrefetchScalarGridSpec(
        num_scalar_prefetch=1,
        grid=(Q, cuts),
        in_specs=[spec(j) for j in range(Q)],
        out_specs=pl.BlockSpec((1,) + block, lambda k, i, c_ref: (jnp.bitwise_xor(c_ref[0], k), i) + rest),
    )
    return pl.pallas_call(
        body,
        grid_spec=grid_spec,
        out_shape=jax.ShapeDtypeStruct((Q,) + shape, parts[0].dtype),
        compiler_params=pltpu.CompilerParams(vmem_limit_bytes=VMEM_LIMIT),
        cost_estimate=pl.CostEstimate(flops=0, bytes_accessed=4 * Q * parts[0].size, transcendentals=0),
    )(c.reshape(1).astype(jnp.int32), *parts)


def to_subnets(blocks, groups):
    if groups > 1:
        images = 8 // groups
        shape = blocks.shape
        cut = blocks.reshape(shape[:-2] + (49, groups, images, shape[-1]))
        cut = jnp.moveaxis(cut, -3, 1)
        cut = jnp.pad(cut, [(0, 0)] * (cut.ndim - 2) + [(0, 8 - images), (0, 0)])
        blocks = cut.reshape((shape[0] * groups,) + shape[1:])
    return lax.all_to_all(blocks, "chan", 0, 0)


def from_subnets(blocks, groups):
    back = lax.all_to_all(blocks, "chan", 0, 0)
    if groups > 1:
        images = 8 // groups
        shape = back.shape
        cut = back.reshape((shape[0] // groups, groups) + shape[1:-2] + (49, 8, shape[-1]))[..., :images, :]
        cut = jnp.moveaxis(cut, 1, -3)
        back = cut.reshape((shape[0] // groups,) + shape[1:-2] + (R, shape[-1]))
    return back


def make_sync(groups, nch):
    def sync(sums):
        got = lax.all_to_all(sums, "batch", 0, 0)
        if groups > 1:
            pairs = [[g * groups + k for k in range(groups)] for g in range(nch // groups)]
            got = lax.psum(got, "chan", axis_index_groups=pairs)
        return got

    return sync


def weight_product(left, grad, columns, plus, width, apart):
    phases, rows = grad.shape[0], grad.shape[1]
    if left.ndim == 2:
        depth = left.shape[1]
        step = {4608: 1536, 2048: 1024}.get(depth, 512)
        left_spec = pl.BlockSpec((rows, step), lambda i, c: (0, i))
    else:
        step = left.shape[3]
        depth = left.shape[0] * step
        left_spec = pl.BlockSpec((1, phases, rows, step), lambda i, c: (i, 0, 0, 0))
    flat = left.ndim == 2

    def body(c_ref, l_ref, one_ref, two_ref, *refs):
        value = None
        for p in range(phases):
            piece = dot(
                l_ref[...] if flat else l_ref[0, p], jnp.concatenate([one_ref[p], two_ref[p]], axis=1), TN
            )
            value = piece if value is None else value + piece
        halves = [value[:, :width], value[:, width:]]
        outs = refs
        if plus is not None:
            halves = [halves[k] + refs[0][k].astype(F32) for k in range(2)]
            outs = refs[1:]
        for k in range(2):
            if apart:
                outs[k][...] = halves[k].astype(BF)
            else:
                outs[0][k] = halves[k].astype(BF)

    def grad_spec(k):
        return pl.BlockSpec((phases, rows, width), lambda i, c: (0, 0, c[k]))

    pair = pl.BlockSpec((2, step, width), lambda i, c: (0, i, 0))
    single = pl.BlockSpec((step, width), lambda i, c: (i, 0))
    grid_spec = pltpu.PrefetchScalarGridSpec(
        num_scalar_prefetch=1,
        grid=(depth // step,),
        in_specs=[left_spec, grad_spec(0), grad_spec(1)] + ([] if plus is None else [pair]),
        out_specs=[single, single] if apart else pair,
    )
    one = jax.ShapeDtypeStruct((depth, width), BF)
    return pl.pallas_call(
        body,
        grid_spec=grid_spec,
        out_shape=[one, one] if apart else jax.ShapeDtypeStruct((2, depth, width), BF),
        compiler_params=pltpu.CompilerParams(vmem_limit_bytes=VMEM_LIMIT),
        cost_estimate=pl.CostEstimate(
            flops=4 * phases * rows * depth * width,
            bytes_accessed=2 * (phases * rows * (depth + 2 * width) + 4 * depth * width),
            transcendentals=0,
        ),
    )(columns, left, grad, grad, *([] if plus is None else [plus]))


class Reduce:
    def __init__(self, nb, nch, left, grad, lead=()):
        self.nb, self.nch, self.left, self.lead = nb, nch, left, lead
        self.grad = grad if grad.ndim == 3 else grad[None]
        self.width = self.grad.shape[2] // nch
        self.depth = left.shape[1] if left.ndim == 2 else left.shape[0] * left.shape[3]
        self.quick = nch == Q

    def first(self):
        if not self.quick:
            left = self.left
            if left.ndim == 4:
                left = jnp.transpose(left[:, : self.grad.shape[0]], (1, 2, 0, 3)).reshape(-1, self.depth)
            full = dot(left, self.grad.reshape(-1, self.grad.shape[2]), TN).astype(BF)
            self.value = lax.psum_scatter(full, "chan", scatter_dimension=1, tiled=True)
            return []
        c = lax.axis_index("chan").astype(jnp.int32)
        self.value = weight_product(self.left, self.grad, jnp.stack([c ^ 1, c ^ 3]), None, self.width, False)
        return [self.value]

    def near(self, held=None):
        if self.quick:
            self.value = lax.ppermute(held[0], "chan", NEAR)

    def second(self):
        if not self.quick:
            return []
        c = lax.axis_index("chan").astype(jnp.int32)
        out = weight_product(self.left, self.grad, jnp.stack([c, c ^ 2]), self.value, self.width, True)
        return list(out)

    def far(self, held=None):
        if self.quick:
            self.own = held[0]
            self.value = lax.ppermute(held[1], "chan", FAR)

    def third(self):
        part = self.value
        if self.quick:
            part = (self.own.astype(F32) + self.value.astype(F32)).astype(BF)
        if self.lead:
            part = jnp.moveaxis(part.reshape(self.lead + (self.nb, -1, self.width)), len(self.lead), 0)
        else:
            part = part.reshape(self.nb, self.depth // self.nb, self.width)
        return [part]

    def batch(self, held):
        self.value = lax.all_to_all(held[0], "batch", 0, 0)

    def total(self):
        return jnp.sum(self.value.astype(F32), axis=0)


def slot(value, *groups):
    flat = [array for group in groups for array in group]
    held = lax.optimization_barrier((value, *flat))
    out = []
    at = 1
    for group in groups:
        out.append(list(held[at : at + len(group)]))
        at += len(group)
    return [held[0]] + out


def body(
    inputs, weight_in, kernel_one, weight_out, weight_skip, second_in, kernel_two, second_out, norm_reduce,
    norm_kernel, norm_expand, norm_skip, later_reduce, later_kernel, later_expand, widths, depths, counts, cotangent,
    *, nb, nch,
):
    subnets, per = inputs.shape[0], inputs.shape[1]
    groups = nch // subnets
    images = per // groups
    chan = lax.axis_index("chan")
    member, half = chan // groups, chan % groups
    slots = jnp.arange(8, dtype=jnp.int32)
    ids = lax.axis_index("batch") * per + half * images + slots
    count = counts[member]
    live_image = jnp.logical_and(slots < images, ids < count).astype(F32)[:, None]
    live = jnp.broadcast_to(live_image, (8, MID))
    inner = live * (jnp.arange(MID, dtype=jnp.int32) < widths[member]).astype(F32)[None, :]
    high, low = inputs.shape[2], cotangent.shape[2]
    table = jnp.stack(
        [
            count.astype(F32) * (high * high),
            count.astype(F32) * (low * low),
            (depths[member] == 2).astype(F32),
        ]
    )
    sync = make_sync(groups, nch)

    small = (norm_reduce, norm_kernel, later_reduce, later_kernel)
    large = (norm_expand, norm_skip, later_expand)
    joined = jnp.concatenate(small + large, axis=1)
    spread = lax.all_to_all(jnp.broadcast_to(joined[None], (nch,) + joined.shape), "chan", 0, 0)
    at = 0
    full = []
    for part in small + large:
        piece = lax.slice_in_dim(spread, at, at + part.shape[1], axis=2)
        full.append(jnp.moveaxis(piece, 0, 1).reshape(2, -1))
        at += part.shape[1]
    aff_a, aff_b, aff_d, aff_e, aff_c, aff_s, aff_f = full

    flat_one = kernel_one.reshape((9,) + kernel_one.shape[2:])
    flat_two = kernel_two.reshape((9,) + kernel_two.shape[2:])
    rows = rows_in(inputs)
    far = gather_far(weight_in, nch)
    late = [weight_skip, flat_two, second_out]
    pieces = gather_far_slices(late, nb, nch)
    if nch == Q:
        rows = after(rows, far, *pieces)
    w_in = gather_rest(weight_in, far, nch)
    slabs = to_subnets(rows, groups)
    if nch == Q:
        pieces = [share(piece, part.shape, nb) for piece, part in zip(pieces, late)]
    far_one = gather_far(after(flat_one, slabs), nch)

    conv_a, sums = stage_a(slabs, w_in, live, nb)
    sums_a = sync(sums)
    w_skip = gather_rest(weight_skip, pieces[0], nch)
    sums_a, (w_skip,) = slot(sums_a, [w_skip])
    conv_s, sums = stage_skip(slabs, w_skip, live, nb)
    sums_s = sync(sums)
    k_one = gather_rest(flat_one, far_one, nch)
    far_out = gather_far(after(weight_out, k_one), nch)
    cols_a, conv_b, sums = stage_conv_one(conv_a, sums_a, aff_a, inner, live, k_one, table, nb)
    sums_b = sync(sums)
    w_out = gather_rest(weight_out, far_out, nch)
    far_in = gather_far(after(second_in, w_out), nch)
    act_b, conv_c, sums = stage_expand(conv_b, sums_b, aff_b, inner, live, w_out, table, nb)
    sums_c = sync(sums)
    k_two = gather_rest(flat_two, pieces[1], nch)
    s_in = gather_rest(second_in, far_in, nch)
    sums_c, (s_in,) = slot(sums_c, [s_in])
    first, first_low, conv_d, sums = stage_join(
        conv_c, sums_c, aff_c, conv_s, sums_s, aff_s, live, s_in, table, nb
    )
    cot = to_subnets(after(small_in(cotangent), sums), groups)
    sums_d = sync(sums)
    sums_d, (k_two,) = slot(sums_d, [k_two])
    cols_d, conv_e, sums = stage_conv_two(conv_d, sums_d, aff_d, inner, live, k_two, table, nb)
    sums_e = sync(sums)
    s_out = gather_rest(second_out, pieces[2], nch)
    sums_e, (s_out,) = slot(sums_e, [s_out])
    act_e, conv_f, sums = stage_expand(conv_e, sums_e, aff_e, inner, live, s_out, table, nb)
    sums_f = sync(sums)
    result, grad_sum, sums = stage_result(conv_f, sums_f, aff_f, first, cot, live, table, nb)
    grads_f = sync(sums)
    result = small_out(from_subnets(result, groups), subnets)

    low_f, gy_e, sums = stage_back_f(
        grad_sum, conv_f, sums_f, grads_f, aff_f, live, s_out, conv_e, sums_e, aff_e, inner, table, nb
    )
    grads_e = sync(sums)
    d_sout = Reduce(nb, nch, act_e, low_f)
    grads_e, x = slot(grads_e, d_sout.first())
    d_sout.near(x)
    low_e, gy_d, sums = stage_back_two(
        gy_e, conv_e, sums_e, grads_e, aff_e, k_two, conv_d, sums_d, aff_d, inner, table, nb
    )
    grads_d = sync(sums)
    d_two = Reduce(nb, nch, cols_d, low_e, (9,))
    grads_d, x, y = slot(grads_d, d_sout.second(), d_two.first())
    d_sout.far(x)
    d_two.near(y)
    low_d, grad_one, sums = stage_back_join(
        gy_d, conv_d, sums_d, grads_d, aff_d, inner, s_in, cot, grad_sum, conv_c, sums_c, aff_c, conv_s, sums_s,
        aff_s, live, table, nb,
    )
    grads_j = sync(sums)
    d_sin = Reduce(nb, nch, first_low, low_d)
    grads_j, x, y, z = slot(grads_j, d_sout.third(), d_two.second(), d_sin.first())
    d_sout.batch(x)
    d_two.far(y)
    d_sin.near(z)
    low_c, low_s, gy_b, sums = stage_back_first(
        grad_one, grads_j, conv_c, sums_c, aff_c, conv_s, sums_s, aff_s, live, w_out, conv_b, sums_b, aff_b, inner,
        table, nb,
    )
    grads_b = sync(sums)
    d_out = Reduce(nb, nch, act_b, low_c)
    d_skip = Reduce(nb, nch, slabs, low_s)
    skip_grad = stage_back_skip(low_s, w_skip)
    grads_b, x, y, z = slot(grads_b, d_sin.second(), d_out.first(), d_skip.first())
    d_sin.far(x)
    d_out.near(y)
    d_skip.near(z)
    low_b, gy_a, sums = stage_back_one(
        gy_b, conv_b, sums_b, grads_b, aff_b, k_one, conv_a, sums_a, aff_a, inner, table, nb
    )
    grads_a = sync(sums)
    d_one = Reduce(nb, nch, cols_a, low_b, (9,))
    grads_a, x, y, z, v, w, (skip_grad,) = slot(
        grads_a, d_two.third(), d_sin.third(), d_out.second(), d_skip.second(), d_one.first(), [skip_grad]
    )
    d_two.batch(x)
    d_sin.batch(y)
    d_out.far(z)
    d_skip.far(v)
    d_one.near(w)
    low_a, grad_in = stage_back_in(gy_a, conv_a, sums_a, grads_a, aff_a, w_in, skip_grad, inner, table, nch)
    d_in = Reduce(nb, nch, slabs, low_a)
    inputs_grad = rows_out(from_subnets(grad_in, groups), subnets)
    d_one.far(d_one.second())
    d_out.batch(d_out.third())
    d_skip.batch(d_skip.third())
    d_in.near(d_in.first())
    d_in.far(d_in.second())
    d_one.batch(d_one.third())
    d_in.batch(d_in.third())
    weight_in_grad, kernel_one_grad, weight_out_grad = d_in.total(), d_one.total(), d_out.total()
    weight_skip_grad, second_in_grad = d_skip.total(), d_sin.total()
    kernel_two_grad, second_out_grad = d_two.total(), d_sout.total()

    def pair(sums, parts, which):
        total = jnp.sum(sums, axis=0).reshape(-1, parts, MID)
        both = jnp.stack([total[:, which].reshape(-1), total[:, 0].reshape(-1)])
        return both.reshape(2, nch, -1)

    norm_parts = [
        pair(grads_a, 2, 1), pair(grads_b, 2, 1), pair(grads_j, 3, 1), pair(grads_j, 3, 2), pair(grads_d, 2, 1),
        pair(grads_e, 2, 1), pair(grads_f, 2, 1),
    ]
    joined = jnp.moveaxis(jnp.concatenate(norm_parts, axis=2), 1, 0)
    mine = jnp.sum(lax.all_to_all(joined, "chan", 0, 0), axis=0) / groups
    norm_grads = []
    at = 0
    for part in norm_parts:
        norm_grads.append(mine[:, at : at + part.shape[2]])
        at += part.shape[2]

    shape = (3, 3, MID // nb, MID // nch)
    return (
        result, inputs_grad, weight_in_grad, kernel_one_grad.reshape(shape), weight_out_grad, weight_skip_grad,
        second_in_grad, kernel_two_grad.reshape(shape), second_out_grad, *norm_grads,
    )


def solution(mesh):
    nb, nch = mesh.shape["batch"], mesh.shape["chan"]
    maps = P(None, "batch", None, None, "chan")
    cols = P(None, "chan")
    taps = P(None, None, None, "chan")
    in_specs = (maps, cols, taps, cols, cols, cols, taps, cols) + (cols,) * 7 + (P(), P(), P(), maps)
    both = P("batch", "chan")
    split = P(None, None, "batch", "chan")
    out_specs = (maps, maps, both, split, both, both, both, split, both) + (cols,) * 7

    def run(*args):
        return body(*args, nb=nb, nch=nch)

    return jax.shard_map(run, mesh=mesh, in_specs=in_specs, out_specs=out_specs, check_vma=False)
```

```python
import jax
import jax.numpy as jnp
from jax import lax
from jax.experimental import pallas as pl
from jax.experimental.pallas import tpu as pltpu
from jax.sharding import PartitionSpec as P

EPS = 1e-05
F32 = jnp.float32
BF = jnp.bfloat16
MID = 512
Q = 4
R = 392
NT = (((1,), (1,)), ((), ()))
TN = (((0,), (0,)), ((), ()))
VMEM_LIMIT = 60 * 1024 * 1024


def call(body, grid, ins, outs, scratch=(), flops=0, moved=0):
    in_specs = []
    for item in ins:
        if item[1] is None:
            in_specs.append(pl.BlockSpec(memory_space=pltpu.SMEM))
        else:
            in_specs.append(pl.BlockSpec(item[1], item[2]))
    return pl.pallas_call(
        body,
        grid=grid,
        in_specs=in_specs,
        out_specs=[pl.BlockSpec(item[2], item[3]) for item in outs],
        out_shape=[jax.ShapeDtypeStruct(item[0], item[1]) for item in outs],
        scratch_shapes=list(scratch),
        compiler_params=pltpu.CompilerParams(vmem_limit_bytes=VMEM_LIMIT),
        cost_estimate=pl.CostEstimate(flops=int(flops), bytes_accessed=int(moved), transcendentals=0),
    )(*[item[0] for item in ins])


def whole(array):
    zeros = (0,) * array.ndim
    return (array, array.shape, lambda i: zeros)


def bands():
    return [slice(56 * h, 56 * h + 56) for h in range(7)]


def tall(value):
    return value.reshape(7, 8, value.shape[-1])


def dot(left, right, dims=(((1,), (0,)), ((), ()))):
    return lax.dot_general(left, right, dims, preferred_element_type=F32)


def mean_inv(sums, pixels):
    total = jnp.sum(sums, axis=0)
    mean = total[:, :MID] / pixels
    var = jnp.maximum(total[:, MID : 2 * MID] / pixels - mean * mean, 0.0)
    return mean, lax.rsqrt(var + EPS)


def forward_coef(sums, affine, mask, pixels):
    mean, inv = mean_inv(sums, pixels)
    scale = affine[0:1] * inv
    return mask * scale, mask * (affine[1:2] - mean * scale), mean, inv


def backward_coef(sums, grad_sums, which, affine, mask, pixels):
    mean, inv = mean_inv(sums, pixels)
    total = jnp.sum(grad_sums, axis=0)
    first = total[:, :MID] / pixels
    second = total[:, which * MID : (which + 1) * MID] / pixels
    scale = affine[0:1] * inv
    slope = -scale * second * inv
    return mask * scale, mask * slope, mask * (-scale * first - slope * mean)


def silu(u):
    return u * jax.nn.sigmoid(u)


def silu_both(u):
    s = jax.nn.sigmoid(u)
    return u * s, s * (1.0 + u * (1.0 - s))


def silu_slope(u):
    s = jax.nn.sigmoid(u)
    return s * (1.0 + u * (1.0 - s))


def fold(acc, value):
    return acc + jnp.sum(tall(value), axis=0)


def put_sums(ref, parts):
    row = jnp.concatenate([jnp.sum(part, axis=0, keepdims=True) for part in parts], axis=1)
    ref[...] = jnp.broadcast_to(row[None], ref.shape)


def value_sums(out_ref, pieces, live):
    first = jnp.zeros((8, MID), F32)
    second = jnp.zeros((8, MID), F32)
    for value in pieces:
        first = fold(first, value)
        second = fold(second, value * value)
    put_sums(out_ref, [first * live, second * live])


def rows_in(inputs):
    subnets, images, size, _, width = inputs.shape
    cut = inputs.reshape(subnets, images, size // 2, 2, size // 2, 2, width)
    return jnp.transpose(cut, (0, 3, 5, 2, 4, 1, 6)).reshape(subnets, 4, R, width)


def rows_out(rows, subnets):
    cut = rows.reshape(subnets, 2, 2, 7, 7, 8, rows.shape[3])
    return jnp.transpose(cut, (0, 5, 3, 1, 4, 2, 6)).reshape(subnets, 8, 14, 14, rows.shape[3])


def small_in(maps):
    return jnp.transpose(maps, (0, 2, 3, 1, 4)).reshape(maps.shape[0], R, maps.shape[4])


def small_out(rows, subnets):
    return jnp.transpose(rows.reshape(subnets, 7, 7, 8, rows.shape[2]), (0, 3, 1, 2, 4))


def lanes(ref):
    return jnp.concatenate([ref[j] for j in range(ref.shape[0])], axis=1)


def stage_a(slabs, weight, live, nb):
    nch, width = slabs.shape[0], slabs.shape[3]
    cin = nch * width

    def body(x_ref, w_ref, live_ref, a_ref, s_ref, sums):
        p = pl.program_id(0)
        x = jnp.concatenate([x_ref[k, 0] for k in range(nch)], axis=1)
        w = lanes(w_ref)
        value = dot(x, w)
        a_ref[0] = value

        @pl.when(p == 0)
        def _():
            sums[...] = jnp.zeros_like(sums)

        first = jnp.zeros((8, MID), F32)
        second = jnp.zeros((8, MID), F32)
        for band in bands():
            piece = value[band]
            first = fold(first, piece)
            second = fold(second, piece * piece)
        sums[0] += first
        sums[1] += second

        @pl.when(p == 3)
        def _():
            put_sums(s_ref, [sums[0] * live_ref[...], sums[1] * live_ref[...]])

    return call(
        body,
        (4,),
        [(slabs, (nch, 1, R, width), lambda i: (0, i, 0, 0)), whole(weight), whole(live)],
        [
            ((4, R, MID), F32, (1, R, MID), lambda i: (i, 0, 0)),
            ((nb, 1, 2 * MID), F32, (nb, 1, 2 * MID), lambda i: (0, 0, 0)),
        ],
        [pltpu.VMEM((2, 8, MID), F32)],
        flops=2 * 4 * R * cin * MID,
        moved=4 * R * (2 * cin + 4 * MID) + 2 * cin * MID,
    )


def stage_skip(slabs, weight, live, nb):
    nch, width = slabs.shape[0], slabs.shape[3]
    cin = nch * width

    def body(x_ref, w_ref, live_ref, o_ref, s_ref):
        x = jnp.concatenate([x_ref[k, 0] for k in range(nch)], axis=1)
        value = dot(x, w_ref[0])
        o_ref[...] = value
        value_sums(s_ref, [value[band] for band in bands()], live_ref[...])

    return call(
        body,
        (Q,),
        [
            (slabs, (nch, 1, R, width), lambda i: (0, 0, 0, 0)),
            (weight, (1, cin, MID), lambda i: (i, 0, 0)),
            whole(live),
        ],
        [
            ((R, Q * MID), F32, (R, MID), lambda i: (0, i)),
            ((nb, 1, Q * 2 * MID), F32, (nb, 1, 2 * MID), lambda i: (0, 0, i)),
        ],
        flops=2 * R * cin * Q * MID,
        moved=2 * R * cin + Q * MID * (2 * cin + 4 * R),
    )


def stage_conv_one(conv_a, sums_a, affine, inner, live, kernel, table, nb):
    def body(t_ref, a_ref, s_ref, g_ref, inner_ref, live_ref, k_ref, cols_ref, b_ref, o_ref, pad, acc):
        i = pl.program_id(0)

        @pl.when(i == 0)
        def _():
            scale, shift, _, _ = forward_coef(s_ref[...], g_ref[...], inner_ref[...], t_ref[0])
            pad[1, :, 0] = jnp.zeros((2, 8, 8, MID), F32)
            pad[:, 1, :, 0] = jnp.zeros((2, 8, 8, MID), F32)
            for p in range(4):
                for h, band in enumerate(bands()):
                    u = tall(a_ref[p, band]) * scale + shift
                    pad[p // 2, p % 2, h + 1, 1:8] = silu(u)

        hp = jnp.where(i == 1, 0, 1)
        h0 = jnp.minimum(i, 1)
        taps = []
        for dw in range(3):
            wp = 0 if dw == 1 else 1
            w0 = 0 if dw == 0 else 1
            tap = pad[hp, wp, pl.ds(h0, 7), w0 : w0 + 7].reshape(R, MID).astype(BF)
            cols_ref[:, dw * MID : (dw + 1) * MID] = tap
            taps.append(tap)
        value = sum(dot(taps[dw], jnp.concatenate([k_ref[j, dw] for j in range(Q)], axis=1)) for dw in range(3))

        @pl.when(i == 0)
        def _():
            acc[...] = value

        @pl.when(i > 0)
        def _():
            acc[...] += value

        @pl.when(i == 2)
        def _():
            low = acc[...].astype(BF).astype(F32)
            b_ref[...] = low
            value_sums(o_ref, [low[band] for band in bands()], live_ref[...])

    return call(
        body,
        (3,),
        [
            (table, None),
            whole(conv_a),
            whole(sums_a),
            whole(affine),
            whole(inner),
            whole(live),
            (kernel, (Q, 3, MID, MID // Q), lambda i: (0, i, 0, 0)),
        ],
        [
            ((R, 9 * MID), BF, (R, 3 * MID), lambda i: (0, i)),
            ((R, MID), F32, (R, MID), lambda i: (0, 0)),
            ((nb, 1, 2 * MID), F32, (nb, 1, 2 * MID), lambda i: (0, 0, 0)),
        ],
        [pltpu.VMEM((2, 2, 8, 8, 8, MID), F32), pltpu.VMEM((R, MID), F32)],
        flops=2 * R * 9 * MID * MID,
        moved=4 * 4 * R * MID + 2 * R * 9 * MID + 2 * 9 * MID * MID,
    )


def stage_conv_two(conv_d, sums_d, affine, inner, live, kernel, table, nb):
    def body(t_ref, d_ref, s_ref, g_ref, inner_ref, live_ref, k_ref, cols_ref, e_ref, o_ref, pad, acc):
        i = pl.program_id(0)

        @pl.when(i == 0)
        def _():
            scale, shift, _, _ = forward_coef(s_ref[...], g_ref[...], inner_ref[...], t_ref[1])
            pad[...] = jnp.zeros_like(pad)
            for h, band in enumerate(bands()):
                u = tall(d_ref[band]) * scale + shift
                pad[h + 1, 1:8] = silu(u)

        taps = []
        for dw in range(3):
            tap = pad[pl.ds(i, 7), dw : dw + 7].reshape(R, MID).astype(BF)
            cols_ref[:, dw * MID : (dw + 1) * MID] = tap
            taps.append(tap)
        value = sum(dot(taps[dw], jnp.concatenate([k_ref[j, dw] for j in range(Q)], axis=1)) for dw in range(3))

        @pl.when(i == 0)
        def _():
            acc[...] = value

        @pl.when(i > 0)
        def _():
            acc[...] += value

        @pl.when(i == 2)
        def _():
            low = acc[...].astype(BF).astype(F32)
            e_ref[...] = low
            value_sums(o_ref, [low[band] for band in bands()], live_ref[...])

    return call(
        body,
        (3,),
        [
            (table, None),
            whole(conv_d),
            whole(sums_d),
            whole(affine),
            whole(inner),
            whole(live),
            (kernel, (Q, 3, MID, MID // Q), lambda i: (0, i, 0, 0)),
        ],
        [
            ((R, 9 * MID), BF, (R, 3 * MID), lambda i: (0, i)),
            ((R, MID), F32, (R, MID), lambda i: (0, 0)),
            ((nb, 1, 2 * MID), F32, (nb, 1, 2 * MID), lambda i: (0, 0, 0)),
        ],
        [pltpu.VMEM((9, 9, 8, MID), F32), pltpu.VMEM((R, MID), F32)],
        flops=2 * R * 9 * MID * MID,
        moved=4 * R * MID + 2 * R * 9 * MID + 2 * 9 * MID * MID,
    )


def stage_expand(conv, sums, affine, inner, live, weight, table, nb, beside=None):
    parts = 2 if beside is None else 4

    def body(t_ref, b_ref, s_ref, g_ref, inner_ref, live_ref, w_ref, *refs):
        act_ref, o_ref, sum_ref, wide = refs[-4:]
        i = pl.program_id(0)

        @pl.when(i == 0)
        def _():
            scale, shift, _, _ = forward_coef(s_ref[...], g_ref[...], inner_ref[...], t_ref[1])
            for band in bands():
                u = tall(b_ref[band]) * scale + shift
                wide[band] = silu(u).reshape(56, MID)
            act_ref[...] = wide[...].astype(BF)

        value = dot(act_ref[...], w_ref[0])
        o_ref[...] = value
        value_sums(sum_ref.at[:, :, : 2 * MID], [value[band] for band in bands()], live_ref[...])
        if beside is not None:
            sum_ref[:, :, 2 * MID :] = refs[0][...]

    return call(
        body,
        (Q,),
        [
            (table, None),
            whole(conv),
            whole(sums),
            whole(affine),
            whole(inner),
            whole(live),
            (weight, (1, MID, MID), lambda i: (i, 0, 0)),
        ]
        + ([] if beside is None else [sum_chunk(beside)]),
        [
            ((R, MID), BF, (R, MID), lambda i: (0, 0)),
            ((R, Q * MID), F32, (R, MID), lambda i: (0, i)),
            ((nb, 1, Q * parts * MID), F32, (nb, 1, parts * MID), lambda i: (0, 0, i)),
        ],
        [pltpu.VMEM((R, MID), F32)],
        flops=2 * R * MID * Q * MID,
        moved=4 * R * MID * (Q + 1) + 2 * MID * MID * Q,
    )


def chunk(array, parts=1):
    return (array, (array.shape[0], parts * MID), lambda i: (0, i))


def sum_chunk(array, parts=2):
    return (array, (array.shape[0], 1, parts * MID), lambda i: (0, 0, i))


def stage_join(conv_c, sums_c, affine_c, conv_s, affine_s, live, weight, table, nb):
    def body(t_ref, c_ref, sc_ref, gc_ref, v_ref, gv_ref, live_ref, w_ref, f_ref, low_ref, d_ref, o_ref, acc):
        i = pl.program_id(0)
        live = live_ref[...]
        scale_c, shift_c, _, _ = forward_coef(sc_ref[...], gc_ref[...], live, t_ref[1])
        scale_s, shift_s, _, _ = forward_coef(sc_ref[:, :, 2 * MID :], gv_ref[...], live, t_ref[1])
        shift = shift_c + shift_s
        for band in bands():
            u = tall(c_ref[band]) * scale_c + tall(v_ref[band]) * scale_s + shift
            f_ref[band] = silu(u).reshape(56, MID)
        low = f_ref[...].astype(BF)
        low_ref[...] = low
        value = dot(low, lanes(w_ref))

        @pl.when(i == 0)
        def _():
            acc[...] = value

        @pl.when(i > 0)
        def _():
            acc[...] += value

        @pl.when(i == Q - 1)
        def _():
            total = acc[...]
            d_ref[...] = total
            value_sums(o_ref, [total[band] for band in bands()], live)

    return call(
        body,
        (Q,),
        [
            (table, None),
            chunk(conv_c),
            sum_chunk(sums_c, 4),
            chunk(affine_c),
            chunk(conv_s),
            chunk(affine_s),
            whole(live),
            (weight, (Q, MID, MID // Q), lambda i: (0, i, 0)),
        ],
        [
            ((R, Q * MID), F32, (R, MID), lambda i: (0, i)),
            ((R, Q * MID), BF, (R, MID), lambda i: (0, i)),
            ((R, MID), F32, (R, MID), lambda i: (0, 0)),
            ((nb, 1, 2 * MID), F32, (nb, 1, 2 * MID), lambda i: (0, 0, 0)),
        ],
        [pltpu.VMEM((R, MID), F32)],
        flops=2 * R * MID * Q * MID,
        moved=14 * R * MID * Q + 2 * MID * MID * Q,
    )


def stage_result(conv_f, sums_f, affine, first, cotangent, live, table, nb):
    nch, width = cotangent.shape[0], cotangent.shape[2]
    per = nch // Q

    def body(t_ref, f_ref, s_ref, g_ref, y_ref, ct_ref, live_ref, r_ref, gs_ref, o_ref, wide):
        live = live_ref[...]
        on = t_ref[2]
        scale, shift, mean, inv = forward_coef(s_ref[...], g_ref[...], live, t_ref[1])
        ct = jnp.concatenate([ct_ref[k] for k in range(per)], axis=1).astype(F32)
        first_sum = jnp.zeros((8, MID), F32)
        second_sum = jnp.zeros((8, MID), F32)
        for band in bands():
            v = tall(f_ref[band])
            y = tall(y_ref[band])
            u = v * scale + shift + y
            second, slope = silu_both(u)
            wide[band] = (y + on * (second - y)).reshape(56, MID)
            grad = on * tall(ct[band]) * slope
            gs_ref[band] = grad.reshape(56, MID)
            first_sum = first_sum + jnp.sum(grad, axis=0)
            second_sum = second_sum + jnp.sum(grad * (v - mean), axis=0)
        result = wide[...].astype(BF)
        for k in range(per):
            r_ref[k] = result[:, k * width : (k + 1) * width]
        put_sums(o_ref, [first_sum * live, second_sum * live * inv])

    return call(
        body,
        (Q,),
        [
            (table, None),
            chunk(conv_f),
            sum_chunk(sums_f),
            chunk(affine),
            chunk(first),
            (cotangent, (per, R, width), lambda i: (i, 0, 0)),
            whole(live),
        ],
        [
            ((nch, R, width), BF, (per, R, width), lambda i: (i, 0, 0)),
            ((R, Q * MID), F32, (R, MID), lambda i: (0, i)),
            ((nb, 1, Q * 2 * MID), F32, (nb, 1, 2 * MID), lambda i: (0, 0, i)),
        ],
        [pltpu.VMEM((R, MID), F32)],
        moved=16 * R * Q * MID,
    )


def finish_inner(grad, conv_ref, sums, affine, mask, pixels, out_put, sum_ref):
    scale, shift, mean, inv = forward_coef(sums, affine, mask, pixels)
    first = jnp.zeros((8, MID), F32)
    second = jnp.zeros((8, MID), F32)
    for band in bands():
        v = tall(conv_ref[band])
        gy = mask * (tall(grad[band]) * silu_slope(v * scale + shift))
        out_put(band, gy.reshape(56, MID))
        first = first + jnp.sum(gy, axis=0)
        second = second + jnp.sum(gy * (v - mean), axis=0)
    put_sums(sum_ref, [first, second * inv])


def stage_back_f(gs, conv_f, sums_f, grad_f, affine_f, live, weight, conv_e, sums_e, affine_e, inner, table, nb):
    def body(
        t_ref, gs_ref, f_ref, sf_ref, gf_ref, af_ref, live_ref, w_ref, e_ref, se_ref, ae_ref, inner_ref,
        low_ref, gy_ref, o_ref, acc, wide,
    ):
        i = pl.program_id(0)
        a, b, c = backward_coef(sf_ref[...], gf_ref[...], 1, af_ref[...], live_ref[...], t_ref[1])
        for band in bands():
            wide[band] = (tall(gs_ref[band]) * a + tall(f_ref[band]) * b + c).reshape(56, MID)
        low = wide[...].astype(BF)
        low_ref[...] = low
        value = dot(low, w_ref[0], NT)

        @pl.when(i == 0)
        def _():
            acc[...] = value

        @pl.when(i > 0)
        def _():
            acc[...] += value

        @pl.when(i == Q - 1)
        def _():
            def put(band, piece):
                gy_ref[band] = piece

            finish_inner(acc, e_ref, se_ref[...], ae_ref[...], inner_ref[...], t_ref[1], put, o_ref)

    return call(
        body,
        (Q,),
        [
            (table, None),
            chunk(gs),
            chunk(conv_f),
            sum_chunk(sums_f),
            sum_chunk(grad_f),
            chunk(affine_f),
            whole(live),
            (weight, (1, MID, MID), lambda i: (i, 0, 0)),
            whole(conv_e),
            whole(sums_e),
            whole(affine_e),
            whole(inner),
        ],
        [
            ((R, Q * MID), BF, (R, MID), lambda i: (0, i)),
            ((R, MID), F32, (R, MID), lambda i: (0, 0)),
            ((nb, 1, 2 * MID), F32, (nb, 1, 2 * MID), lambda i: (0, 0, 0)),
        ],
        [pltpu.VMEM((R, MID), F32), pltpu.VMEM((R, MID), F32)],
        flops=2 * R * MID * Q * MID,
        moved=10 * R * MID * Q + 2 * MID * MID * Q,
    )


def stage_back_two(gy_e, conv_e, sums_e, grad_e, affine_e, kernel, conv_d, sums_d, affine_d, inner, table, nb):
    def body(
        t_ref, gy_ref, e_ref, se_ref, ge_ref, ae_ref, k_ref, d_ref, sd_ref, ad_ref, inner_ref,
        low_ref, out_ref, o_ref, pad, acc, wide,
    ):
        i = pl.program_id(0)

        @pl.when(i == 0)
        def _():
            a, b, c = backward_coef(se_ref[...], ge_ref[...], 1, ae_ref[...], inner_ref[...], t_ref[1])
            pad[...] = jnp.zeros_like(pad)
            for h, band in enumerate(bands()):
                value = tall(gy_ref[band]) * a + tall(e_ref[band]) * b + c
                wide[band] = value.reshape(56, MID)
                pad[h + 1, 1:8] = value
            low_ref[...] = wide[...].astype(BF)

        total = None
        for dw in range(3):
            tap = pad[pl.ds(2 - i, 7), 2 - dw : 9 - dw].reshape(R, MID).astype(BF)
            part = dot(tap, jnp.concatenate([k_ref[j, dw] for j in range(Q)], axis=1), NT)
            total = part if total is None else total + part

        @pl.when(i == 0)
        def _():
            acc[...] = total

        @pl.when(i > 0)
        def _():
            acc[...] += total

        @pl.when(i == 2)
        def _():
            low = acc[...].astype(BF).astype(F32)

            def put(band, piece):
                out_ref[band] = piece

            finish_inner(low, d_ref, sd_ref[...], ad_ref[...], inner_ref[...], t_ref[1], put, o_ref)

    return call(
        body,
        (3,),
        [
            (table, None),
            whole(gy_e),
            whole(conv_e),
            whole(sums_e),
            whole(grad_e),
            whole(affine_e),
            (kernel, (Q, 3, MID, MID // Q), lambda i: (0, i, 0, 0)),
            whole(conv_d),
            whole(sums_d),
            whole(affine_d),
            whole(inner),
        ],
        [
            ((R, MID), BF, (R, MID), lambda i: (0, 0)),
            ((R, MID), F32, (R, MID), lambda i: (0, 0)),
            ((nb, 1, 2 * MID), F32, (nb, 1, 2 * MID), lambda i: (0, 0, 0)),
        ],
        [pltpu.VMEM((9, 9, 8, MID), F32), pltpu.VMEM((R, MID), F32), pltpu.VMEM((R, MID), F32)],
        flops=2 * R * 9 * MID * MID,
        moved=16 * R * MID + 2 * 9 * MID * MID,
    )


def stage_back_join(
    gy_d, conv_d, sums_d, grad_d, affine_d, inner, weight, cotangent, gs, conv_c, sums_c, affine_c, conv_s,
    affine_s, live, table, nb,
):
    nch, width = cotangent.shape[0], cotangent.shape[2]
    per = nch // Q

    def body(
        t_ref, gy_ref, d_ref, sd_ref, gd_ref, ad_ref, inner_ref, w_ref, ct_ref, gs_ref, c_ref, sc_ref, ac_ref, v_ref,
        av_ref, live_ref, low_ref, out_ref, o_ref, wide,
    ):
        i = pl.program_id(0)
        live = live_ref[...]

        @pl.when(i == 0)
        def _():
            a, b, c = backward_coef(sd_ref[...], gd_ref[...], 1, ad_ref[...], inner_ref[...], t_ref[1])
            for band in bands():
                wide[band] = (tall(gy_ref[band]) * a + tall(d_ref[band]) * b + c).reshape(56, MID)
            low_ref[...] = wide[...].astype(BF)

        back = dot(low_ref[...], lanes(w_ref), NT)
        ct = jnp.concatenate([ct_ref[k] for k in range(per)], axis=1).astype(F32)
        scale_c, shift_c, mean_c, inv_c = forward_coef(sc_ref[...], ac_ref[...], live, t_ref[1])
        scale_s, shift_s, mean_s, inv_s = forward_coef(sc_ref[:, :, 2 * MID :], av_ref[...], live, t_ref[1])
        shift = shift_c + shift_s
        off = 1.0 - t_ref[2]
        one = jnp.zeros((8, MID), F32)
        two = jnp.zeros((8, MID), F32)
        three = jnp.zeros((8, MID), F32)
        for band in bands():
            c = tall(c_ref[band])
            v = tall(v_ref[band])
            u = c * scale_c + v * scale_s + shift
            grad = off * tall(ct[band]) + tall(gs_ref[band]) + tall(back[band])
            grad = live * (grad * silu_slope(u))
            out_ref[band] = grad.reshape(56, MID)
            one = one + jnp.sum(grad, axis=0)
            two = two + jnp.sum(grad * (c - mean_c), axis=0)
            three = three + jnp.sum(grad * (v - mean_s), axis=0)
        put_sums(o_ref, [one, two * inv_c, three * inv_s])

    return call(
        body,
        (Q,),
        [
            (table, None),
            whole(gy_d),
            whole(conv_d),
            whole(sums_d),
            whole(grad_d),
            whole(affine_d),
            whole(inner),
            (weight, (Q, MID, MID // Q), lambda i: (0, i, 0)),
            (cotangent, (per, R, width), lambda i: (i, 0, 0)),
            chunk(gs),
            chunk(conv_c),
            sum_chunk(sums_c, 4),
            chunk(affine_c),
            chunk(conv_s),
            chunk(affine_s),
            whole(live),
        ],
        [
            ((R, MID), BF, (R, MID), lambda i: (0, 0)),
            ((R, Q * MID), F32, (R, MID), lambda i: (0, i)),
            ((nb, 1, Q * 3 * MID), F32, (nb, 1, 3 * MID), lambda i: (0, 0, i)),
        ],
        [pltpu.VMEM((R, MID), F32)],
        flops=2 * R * MID * Q * MID,
        moved=18 * R * MID * Q + 2 * MID * MID * Q,
    )


def stage_back_first(
    grad, sums_g, conv_c, sums_c, affine_c, conv_s, affine_s, live, weight, conv_b, sums_b, affine_b, inner,
    table, nb,
):
    def body(
        t_ref, g_ref, sg_ref, c_ref, sc_ref, ac_ref, v_ref, av_ref, live_ref, w_ref, b_ref, sb_ref, ab_ref,
        inner_ref, lowc_ref, lows_ref, out_ref, o_ref, acc, wide,
    ):
        i = pl.program_id(0)
        live = live_ref[...]
        a, b, c = backward_coef(sc_ref[:, :, 2 * MID :], sg_ref[...], 2, av_ref[...], live, t_ref[1])
        for band in bands():
            wide[band] = (tall(g_ref[band]) * a + tall(v_ref[band]) * b + c).reshape(56, MID)
        lows_ref[...] = wide[...].astype(BF)
        a, b, c = backward_coef(sc_ref[...], sg_ref[...], 1, ac_ref[...], live, t_ref[1])
        for band in bands():
            wide[band] = (tall(g_ref[band]) * a + tall(c_ref[band]) * b + c).reshape(56, MID)
        low = wide[...].astype(BF)
        lowc_ref[...] = low
        value = dot(low, w_ref[0], NT)

        @pl.when(i == 0)
        def _():
            acc[...] = value

        @pl.when(i > 0)
        def _():
            acc[...] += value

        @pl.when(i == Q - 1)
        def _():
            def put(band, piece):
                out_ref[band] = piece

            finish_inner(acc, b_ref, sb_ref[...], ab_ref[...], inner_ref[...], t_ref[1], put, o_ref)

    return call(
        body,
        (Q,),
        [
            (table, None),
            chunk(grad),
            sum_chunk(sums_g, 3),
            chunk(conv_c),
            sum_chunk(sums_c, 4),
            chunk(affine_c),
            chunk(conv_s),
            chunk(affine_s),
            whole(live),
            (weight, (1, MID, MID), lambda i: (i, 0, 0)),
            whole(conv_b),
            whole(sums_b),
            whole(affine_b),
            whole(inner),
        ],
        [
            ((R, Q * MID), BF, (R, MID), lambda i: (0, i)),
            ((R, Q * MID), BF, (R, MID), lambda i: (0, i)),
            ((R, MID), F32, (R, MID), lambda i: (0, 0)),
            ((nb, 1, 2 * MID), F32, (nb, 1, 2 * MID), lambda i: (0, 0, 0)),
        ],
        [pltpu.VMEM((R, MID), F32), pltpu.VMEM((R, MID), F32)],
        flops=2 * R * MID * Q * MID,
        moved=16 * R * MID * Q + 2 * MID * MID * Q,
    )


def stage_back_skip(low, weight):
    cin = weight.shape[1]

    def body(g_ref, w_ref, o_ref):
        i = pl.program_id(0)
        value = dot(g_ref[...], w_ref[0], NT)

        @pl.when(i == 0)
        def _():
            o_ref[...] = value

        @pl.when(i > 0)
        def _():
            o_ref[...] += value

    return call(
        body,
        (Q,),
        [chunk(low), (weight, (1, cin, MID), lambda i: (i, 0, 0))],
        [((R, cin), F32, (R, cin), lambda i: (0, 0))],
        flops=2 * R * cin * Q * MID,
        moved=4 * R * cin + 2 * R * Q * MID + 2 * cin * Q * MID,
    )[0]


def stage_back_one(gy_b, conv_b, sums_b, grad_b, affine_b, kernel, conv_a, sums_a, affine_a, inner, table, nb):
    def body(
        t_ref, gy_ref, b_ref, sb_ref, gb_ref, ab_ref, k_ref, a_ref, sa_ref, aa_ref, inner_ref,
        low_ref, out_ref, o_ref, pad, acc, wide,
    ):
        i = pl.program_id(0)

        @pl.when(i == 0)
        def _():
            a, b, c = backward_coef(sb_ref[...], gb_ref[...], 1, ab_ref[...], inner_ref[...], t_ref[1])
            pad[7] = jnp.zeros((8, 8, MID), F32)
            pad[:, 7] = jnp.zeros((8, 8, MID), F32)
            for h, band in enumerate(bands()):
                value = tall(gy_ref[band]) * a + tall(b_ref[band]) * b + c
                wide[band] = value.reshape(56, MID)
                pad[h, 0:7] = value
            low_ref[...] = wide[...].astype(BF)

        h0 = jnp.where(i == 0, 1, 0)
        near = pad[pl.ds(h0, 7), 0:7].reshape(R, MID).astype(BF)
        far = pad[pl.ds(h0, 7), 1:8].reshape(R, MID).astype(BF)
        k = [jnp.concatenate([k_ref[j, dw] for j in range(Q)], axis=1) for dw in range(3)]
        even = dot(near, k[1], NT)
        odd = dot(far, k[0], NT) + dot(near, k[2], NT)

        @pl.when(i == 0)
        def _():
            acc[2] = even
            acc[3] = odd

        @pl.when(i == 1)
        def _():
            acc[0] = even
            acc[1] = odd

        @pl.when(i == 2)
        def _():
            acc[2] += even
            acc[3] += odd
            mask = inner_ref[...]
            scale, shift, mean, inv = forward_coef(sa_ref[...], aa_ref[...], mask, t_ref[0])
            first = jnp.zeros((8, MID), F32)
            second = jnp.zeros((8, MID), F32)
            for p in range(4):
                wide[...] = acc[p].astype(BF).astype(F32)
                for band in bands():
                    v = tall(a_ref[p, band])
                    gy = mask * (tall(wide[band]) * silu_slope(v * scale + shift))
                    out_ref[p, band] = gy.reshape(56, MID)
                    first = first + jnp.sum(gy, axis=0)
                    second = second + jnp.sum(gy * (v - mean), axis=0)
            put_sums(o_ref, [first, second * inv])

    return call(
        body,
        (3,),
        [
            (table, None),
            whole(gy_b),
            whole(conv_b),
            whole(sums_b),
            whole(grad_b),
            whole(affine_b),
            (kernel, (Q, 3, MID, MID // Q), lambda i: (0, i, 0, 0)),
            whole(conv_a),
            whole(sums_a),
            whole(affine_a),
            whole(inner),
        ],
        [
            ((R, MID), BF, (R, MID), lambda i: (0, 0)),
            ((4, R, MID), F32, (4, R, MID), lambda i: (0, 0, 0)),
            ((nb, 1, 2 * MID), F32, (nb, 1, 2 * MID), lambda i: (0, 0, 0)),
        ],
        [pltpu.VMEM((8, 8, 8, MID), F32), pltpu.VMEM((4, R, MID), F32), pltpu.VMEM((R, MID), F32)],
        flops=2 * R * 9 * MID * MID,
        moved=32 * R * MID + 2 * 9 * MID * MID,
    )


def stage_back_in(gy_a, conv_a, sums_a, grad_a, affine_a, weight, skip_grad, inner, table, nch):
    cin = weight.shape[1]
    width = cin // nch

    def body(t_ref, gy_ref, a_ref, sa_ref, ga_ref, aa_ref, w_ref, s_ref, inner_ref, low_ref, out_ref, wide):
        i = pl.program_id(0)
        a, b, c = backward_coef(sa_ref[...], ga_ref[...], 1, aa_ref[...], inner_ref[...], t_ref[0])
        for band in bands():
            wide[band] = (tall(gy_ref[0, band]) * a + tall(a_ref[0, band]) * b + c).reshape(56, MID)
        low = wide[...].astype(BF)
        low_ref[0] = low
        value = dot(low, lanes(w_ref), NT)

        @pl.when(i == 0)
        def _():
            both = (value + s_ref[...]).astype(BF)
            for k in range(nch):
                out_ref[k, 0] = both[:, k * width : (k + 1) * width]

        @pl.when(i > 0)
        def _():
            both = value.astype(BF)
            for k in range(nch):
                out_ref[k, 0] = both[:, k * width : (k + 1) * width]

    return call(
        body,
        (4,),
        [
            (table, None),
            (gy_a, (1, R, MID), lambda i: (i, 0, 0)),
            (conv_a, (1, R, MID), lambda i: (i, 0, 0)),
            whole(sums_a),
            whole(grad_a),
            whole(affine_a),
            whole(weight),
            whole(skip_grad),
            whole(inner),
        ],
        [
            ((4, R, MID), BF, (1, R, MID), lambda i: (i, 0, 0)),
            ((nch, 4, R, width), BF, (nch, 1, R, width), lambda i: (0, i, 0, 0)),
        ],
        [pltpu.VMEM((R, MID), F32)],
        flops=2 * 4 * R * cin * MID,
        moved=4 * R * (10 * MID + 2 * cin) + 2 * cin * MID + 4 * R * cin,
    )


def after(value, *others):
    return lax.optimization_barrier((value,) + others)[0]


NEAR = [(i, i ^ 1) for i in range(Q)]
FAR = [(i, i ^ 2) for i in range(Q)]


def gather_far(part, nch):
    return lax.ppermute(part, "chan", FAR) if nch == Q else None


def gather_rest(part, other, nch, *when):
    if nch == Q:
        c = lax.axis_index("chan")
        part, other = lax.optimization_barrier((part, other) + when)[:2]
        parts = [part, lax.ppermute(part, "chan", NEAR), other, lax.ppermute(other, "chan", NEAR)]
        return place(parts, c)
    full = lax.all_gather(part, "chan", axis=part.ndim - 1, tiled=True)
    cut = full.reshape(full.shape[:-1] + (Q, full.shape[-1] // Q))
    return jnp.moveaxis(cut, -2, 0)


def place(parts, c):
    shape = parts[0].shape
    block = (3,) + shape[1:] if shape[0] == 9 else shape
    cuts = shape[0] // block[0]
    rest = (0,) * (len(shape) - 1)

    def body(c_ref, *refs):
        k = pl.program_id(0)
        out = refs[Q]
        for j in range(Q):

            @pl.when(k == j)
            def _():
                out[0] = refs[j][...]

    def spec(j):
        def index(k, i, c_ref):
            return (jnp.where(k == j, i, jnp.where(k < j, 0, cuts - 1)),) + rest

        return pl.BlockSpec(block, index)

    grid_spec = pltpu.PrefetchScalarGridSpec(
        num_scalar_prefetch=1,
        grid=(Q, cuts),
        in_specs=[spec(j) for j in range(Q)],
        out_specs=pl.BlockSpec((1,) + block, lambda k, i, c_ref: (jnp.bitwise_xor(c_ref[0], k), i) + rest),
    )
    return pl.pallas_call(
        body,
        grid_spec=grid_spec,
        out_shape=jax.ShapeDtypeStruct((Q,) + shape, parts[0].dtype),
        compiler_params=pltpu.CompilerParams(vmem_limit_bytes=VMEM_LIMIT),
        cost_estimate=pl.CostEstimate(flops=0, bytes_accessed=4 * Q * parts[0].size, transcendentals=0),
    )(c.reshape(1).astype(jnp.int32), *parts)


def exchange(pick, nch):
    c = lax.axis_index("chan")
    parts = [pick(c)]
    for k in (3, 2, 1):
        parts.insert(1, lax.ppermute(pick(jnp.bitwise_xor(c, k)), "chan", [(i, i ^ k) for i in range(Q)]))
    return place(parts, c)


def to_subnets(maps, order, groups, nch, *tokens):
    if groups == 1:

        def pick(member):
            part = order(lax.dynamic_index_in_dim(maps, member, 0, keepdims=True))[0]
            return after(part, *tokens) if tokens else part

        return exchange(pick, nch)
    blocks = order(maps)
    images = 8 // groups
    shape = blocks.shape
    cut = blocks.reshape(shape[:-2] + (49, groups, images, shape[-1]))
    cut = jnp.moveaxis(cut, -3, 1)
    cut = jnp.pad(cut, [(0, 0)] * (cut.ndim - 2) + [(0, 8 - images), (0, 0)])
    blocks = cut.reshape((shape[0] * groups,) + shape[1:])
    return lax.all_to_all(blocks, "chan", 0, 0)


def from_subnets(blocks, groups, nch):
    if groups == 1:
        return exchange(lambda member: lax.dynamic_index_in_dim(blocks, member, 0, keepdims=False), nch)
    back = lax.all_to_all(blocks, "chan", 0, 0)
    images = 8 // groups
    shape = back.shape
    cut = back.reshape((shape[0] // groups, groups) + shape[1:-2] + (49, 8, shape[-1]))[..., :images, :]
    cut = jnp.moveaxis(cut, 1, -3)
    return cut.reshape((shape[0] // groups,) + shape[1:-2] + (R, shape[-1]))


def make_sync(groups, nch):
    def sync(sums):
        got = lax.all_to_all(sums, "batch", 0, 0)
        if groups > 1:
            pairs = [[g * groups + k for k in range(groups)] for g in range(nch // groups)]
            got = lax.psum(got, "chan", axis_index_groups=pairs)
        return got

    return sync


def weight_product(pairs, columns, plus, width, apart):
    every = columns is None
    depths = [left.shape[1] if left.ndim == 2 else left.shape[0] * left.shape[3] for left, _ in pairs]
    depth = sum(depths)
    if len(pairs) > 1 or pairs[0][0].ndim == 4:
        step = min(256, pairs[-1][0].shape[-1])
    else:
        step = {4608: 1536, 2048: 1024}.get(depth, 512)
    starts = [sum(depths[:m]) // step for m in range(len(pairs) + 1)]

    def local(i, m):
        return jnp.clip(i - starts[m], 0, starts[m + 1] - starts[m] - 1)

    args, specs = [], []
    for m, (left, grad) in enumerate(pairs):
        phases, rows = grad.shape[0], grad.shape[1]
        args.append(left)
        if left.ndim == 2:
            specs.append(pl.BlockSpec((rows, step), lambda i, c, m=m: (0, local(i, m))))
        else:
            specs.append(pl.BlockSpec((1, phases, rows, step), lambda i, c, m=m: (local(i, m), 0, 0, 0)))
        if every:
            args.append(grad)
            specs.append(pl.BlockSpec(grad.shape, lambda i, c: (0, 0, 0)))
        else:
            for k in range(2):
                args.append(grad)
                specs.append(pl.BlockSpec((phases, rows, width), lambda i, c, k=k: (0, 0, c[k])))
    each = 2 if every else 3
    pair = pl.BlockSpec((2, step, width), lambda i, c: (0, i, 0))
    if plus is not None:
        args.append(plus)
        specs.append(pair)

    def one(m, refs, more, outs):
        left, grad = pairs[m]
        l_ref = refs[0]
        value = None
        for p in range(grad.shape[0]):
            right = refs[1][p] if every else jnp.concatenate([refs[1][p], refs[2][p]], axis=1)
            piece = dot(l_ref[...] if left.ndim == 2 else l_ref[0, p], right, TN)
            value = piece if value is None else value + piece
        for k in range(Q if every else 2):
            part = value[:, k * width : (k + 1) * width]
            if more is not None:
                part = part + more[k].astype(F32)
            if apart:
                outs[k][...] = part.astype(BF)
            else:
                outs[0][k] = part.astype(BF)

    def body(c_ref, *refs):
        ins, outs = refs[: len(args)], refs[len(args) :]
        more = ins[-1] if plus is not None else None
        if len(pairs) == 1:
            one(0, ins, more, outs)
            return
        i = pl.program_id(0)
        for m in range(len(pairs)):

            @pl.when(jnp.logical_and(i >= starts[m], i < starts[m + 1]))
            def _(m=m):
                one(m, ins[each * m : each * m + each], more, outs)

    single = pl.BlockSpec((step, width), lambda i, c: (i, 0))
    block = jax.ShapeDtypeStruct((depth, width), BF)
    if every:
        out_specs = pl.BlockSpec((Q, step, width), lambda i, c: (0, i, 0))
        out_shape = jax.ShapeDtypeStruct((Q, depth, width), BF)
    elif apart:
        out_specs, out_shape = [single, single], [block, block]
    else:
        out_specs, out_shape = pair, jax.ShapeDtypeStruct((2, depth, width), BF)
    flops = sum(4 * left.size * width for left, _ in pairs)
    return pl.pallas_call(
        body,
        grid_spec=pltpu.PrefetchScalarGridSpec(
            num_scalar_prefetch=1, grid=(depth // step,), in_specs=specs, out_specs=out_specs
        ),
        out_shape=out_shape,
        compiler_params=pltpu.CompilerParams(vmem_limit_bytes=VMEM_LIMIT),
        cost_estimate=pl.CostEstimate(
            flops=flops, bytes_accessed=sum(2 * left.size for left, _ in pairs) + 8 * depth * width, transcendentals=0
        ),
    )(jnp.zeros((1,), jnp.int32) if every else columns, *args)


class Reduce:
    def __init__(self, nb, nch, *pairs, lead=()):
        self.nb, self.nch, self.lead = nb, nch, lead
        self.pairs = [(left, grad if grad.ndim == 3 else grad[None]) for left, grad in pairs]
        self.width = self.pairs[0][1].shape[2] // nch
        self.depths = [left.shape[1] if left.ndim == 2 else left.shape[0] * left.shape[3] for left, _ in pairs]
        self.depth = sum(self.depths)
        self.quick = nch == Q

    def first(self):
        if not self.quick:
            parts = []
            for (left, grad), depth in zip(self.pairs, self.depths):
                if left.ndim == 4:
                    left = jnp.transpose(left[:, : grad.shape[0]], (1, 2, 0, 3)).reshape(-1, depth)
                parts.append(dot(left, grad.reshape(-1, grad.shape[2]), TN).astype(BF))
            full = jnp.concatenate(parts, axis=0)
            self.terms = [lax.psum_scatter(full, "chan", scatter_dimension=1, tiled=True)]
            return []
        c = lax.axis_index("chan").astype(jnp.int32)
        self.value = weight_product(self.pairs, jnp.stack([c ^ 1, c ^ 3]), None, self.width, False)
        return [self.value]

    def near(self, held=None):
        if self.quick:
            self.value = lax.ppermute(held[0], "chan", NEAR)

    def second(self):
        if not self.quick:
            return []
        c = lax.axis_index("chan").astype(jnp.int32)
        out = weight_product(self.pairs, jnp.stack([c, c ^ 2]), self.value, self.width, True)
        return list(out)

    def far(self, held=None):
        if self.quick:
            self.terms = [held[0], lax.ppermute(held[1], "chan", FAR)]

    def direct(self):
        if not self.quick:
            return self.first()
        value = weight_product(self.pairs, None, None, self.width, False)
        got = lax.all_to_all(value, "chan", 0, 0)
        self.terms = [got[k] for k in range(Q)]

    def blocks(self, part):
        if self.lead:
            part = jnp.moveaxis(part.reshape(self.lead + (self.nb, -1, self.width)), len(self.lead), 0)
            return part.reshape(self.nb, -1, self.width)
        outs = []
        at = 0
        for depth in self.depths:
            piece = part[at : at + depth].reshape(self.nb, depth // self.nb, self.width)
            if self.quick and self.width > 128:
                piece = piece.reshape(self.nb, -1, self.width // 128, 128)
                piece = jnp.transpose(piece, (0, 2, 1, 3)).reshape(self.nb, -1, 128)
            outs.append(piece)
            at += depth
        return jnp.concatenate(outs, axis=1) if len(outs) > 1 else outs[0]

    def results(self, total):
        outs = []
        at = 0
        for depth in self.depths:
            rows = depth // self.nb * (self.width // 128 if self.quick else 1)
            piece = total[at : at + rows]
            if self.quick and self.width > 128:
                piece = piece.reshape(self.width // 128, -1, 128)
                piece = jnp.transpose(piece, (1, 0, 2)).reshape(-1, self.width)
            outs.append(piece)
            at += rows
        return outs


def joined_blocks(group, which=None):
    parts = []
    for member in group:
        both = [member.blocks(part) for part in member.terms]
        if which is not None:
            both = [part.reshape((4, 2) + part.shape[1:]) for part in both]
            both = [lax.dynamic_index_in_dim(part, which, 1, keepdims=False) for part in both]
        total = both[0].astype(F32)
        for part in both[1:]:
            total = total + part.astype(F32)
        parts.append(total)
    return jnp.concatenate(parts, axis=1) if len(parts) > 1 else parts[0]


class BatchSum:
    def __init__(self, group, nb, nch):
        self.group, self.nb = group, nb
        self.quick = nch == Q and nb == 8
        b = lax.axis_index("batch")
        self.x, self.z = b % 2, b // 2

    def hold(self, when):
        for member in self.group:
            held = lax.optimization_barrier(tuple(member.terms) + tuple(when))
            member.terms = list(held[: len(member.terms)])

    def along_x(self, *when):
        if when:
            self.hold(when)
        if self.quick:
            send = joined_blocks(self.group, 1 - self.x).astype(BF)
            self.got = lax.ppermute(send, "batch", [(i, i ^ 1) for i in range(8)])

    def along_z(self, *when):
        if self.quick:
            got = after(self.got, *when) if when else self.got
            keep = (joined_blocks(self.group, self.x) + got.astype(F32)).astype(BF)
            lines = [[2 * k + x for k in range(4)] for x in range(2)]
            got = lax.all_to_all(keep, "batch", 0, 0, axis_index_groups=lines)
            total = jnp.sum(got.astype(F32), axis=0)
        outs = []
        at = 0
        for member in self.group:
            if self.quick:
                rows = member.depth // self.nb * (member.width // 128)
                part = total[at : at + rows]
                at += rows
            else:
                part = joined_blocks([member]).astype(BF)
                got = lax.psum_scatter(part, "batch", scatter_dimension=0, tiled=True)
                part = got.reshape(part.shape[1:]).astype(F32)
            outs += member.results(part)
        return outs


def slot(value, *groups):
    flat = [array for group in groups for array in group]
    held = lax.optimization_barrier((value, *flat))
    out = []
    at = 1
    for group in groups:
        out.append(list(held[at : at + len(group)]))
        at += len(group)
    return [held[0]] + out


def body(
    inputs, weight_in, kernel_one, weight_out, weight_skip, second_in, kernel_two, second_out, norm_reduce,
    norm_kernel, norm_expand, norm_skip, later_reduce, later_kernel, later_expand, widths, depths, counts, cotangent,
    *, nb, nch,
):
    subnets, per = inputs.shape[0], inputs.shape[1]
    groups = nch // subnets
    images = per // groups
    chan = lax.axis_index("chan")
    member, half = chan // groups, chan % groups
    slots = jnp.arange(8, dtype=jnp.int32)
    ids = lax.axis_index("batch") * per + half * images + slots
    count = counts[member]
    live_image = jnp.logical_and(slots < images, ids < count).astype(F32)[:, None]
    live = jnp.broadcast_to(live_image, (8, MID))
    inner = live * (jnp.arange(MID, dtype=jnp.int32) < widths[member]).astype(F32)[None, :]
    high, low = inputs.shape[2], cotangent.shape[2]
    table = jnp.stack(
        [
            count.astype(F32) * (high * high),
            count.astype(F32) * (low * low),
            (depths[member] == 2).astype(F32),
        ]
    )
    sync = make_sync(groups, nch)

    small = (norm_reduce, norm_kernel, later_reduce, later_kernel)
    large = (norm_expand, norm_skip, later_expand)
    joined = jnp.concatenate(small + large, axis=1)
    spread = lax.all_to_all(jnp.broadcast_to(joined[None], (nch,) + joined.shape), "chan", 0, 0)
    at = 0
    full = []
    for part in small + large:
        piece = lax.slice_in_dim(spread, at, at + part.shape[1], axis=2)
        full.append(jnp.moveaxis(piece, 0, 1).reshape(2, -1))
        at += part.shape[1]
    flat_one = kernel_one.reshape((9,) + kernel_one.shape[2:])
    flat_two = kernel_two.reshape((9,) + kernel_two.shape[2:])
    far = gather_far(weight_in, nch)
    slabs = to_subnets(inputs, rows_in, groups, nch, *([far] if nch == Q else []))
    slabs, full = slot(slabs, full)
    aff_a, aff_b, aff_d, aff_e, aff_c, aff_s, aff_f = full
    w_in = gather_rest(weight_in, far, nch)
    far_one = gather_far(after(flat_one, slabs), nch)

    conv_a, sums = stage_a(slabs, w_in, live, nb)
    far_out = gather_far(after(weight_out, sums), nch)
    far_skip = gather_far(after(weight_skip, sums), nch)
    sums_a = sync(sums)
    k_one = gather_rest(flat_one, far_one, nch, sums_a)
    cols_a, conv_b, sums = stage_conv_one(conv_a, sums_a, aff_a, inner, live, k_one, table, nb)
    far_in = gather_far(after(second_in, sums), nch)
    far_two = gather_far(after(flat_two, sums), nch)
    sums_b = sync(sums)
    w_skip = gather_rest(weight_skip, far_skip, nch, sums)
    conv_s, sums_s = stage_skip(slabs, w_skip, live, nb)
    w_out = gather_rest(weight_out, far_out, nch, sums)
    sums_b, (sums_s, w_out) = slot(sums_b, [sums_s, w_out])
    act_b, conv_c, sums = stage_expand(conv_b, sums_b, aff_b, inner, live, w_out, table, nb, sums_s)
    far_sout = gather_far(after(second_out, sums), nch)
    sums_c = sync(sums)
    k_two = gather_rest(flat_two, far_two, nch, sums)
    s_in = gather_rest(second_in, far_in, nch, sums)
    sums_c, (s_in,) = slot(sums_c, [s_in])
    first, first_low, conv_d, sums = stage_join(conv_c, sums_c, aff_c, conv_s, aff_s, live, s_in, table, nb)
    cot = to_subnets(cotangent, small_in, groups, nch, sums)
    sums_d = sync(sums)
    sums_d, (k_two,) = slot(sums_d, [k_two])
    cols_d, conv_e, sums = stage_conv_two(conv_d, sums_d, aff_d, inner, live, k_two, table, nb)
    sums_e = sync(sums)
    s_out = gather_rest(second_out, far_sout, nch, sums)
    sums_e, (s_out,) = slot(sums_e, [s_out])
    act_e, conv_f, sums = stage_expand(conv_e, sums_e, aff_e, inner, live, s_out, table, nb)
    sums_f = sync(sums)
    sums_f, (cot,) = slot(sums_f, [cot])
    result, grad_sum, sums = stage_result(conv_f, sums_f, aff_f, first, cot, live, table, nb)
    grads_f = sync(sums)
    result = small_out(from_subnets(result, groups, nch), subnets)

    low_f, gy_e, sums = stage_back_f(
        grad_sum, conv_f, sums_f, grads_f, aff_f, live, s_out, conv_e, sums_e, aff_e, inner, table, nb
    )
    grads_e = sync(sums)
    d_sout = Reduce(nb, nch, (act_e, low_f))
    grads_e, x = slot(grads_e, d_sout.first())
    d_sout.near(x)
    low_e, gy_d, sums = stage_back_two(
        gy_e, conv_e, sums_e, grads_e, aff_e, k_two, conv_d, sums_d, aff_d, inner, table, nb
    )
    grads_d = sync(sums)
    d_two = Reduce(nb, nch, (cols_d, low_e), lead=(9,))
    grads_d, x, y, (result,) = slot(grads_d, d_sout.second(), d_two.first(), [result])
    d_sout.far(x)
    d_two.near(y)
    low_d, grad_one, sums = stage_back_join(
        gy_d, conv_d, sums_d, grads_d, aff_d, inner, s_in, cot, grad_sum, conv_c, sums_c, aff_c, conv_s,
        aff_s, live, table, nb,
    )
    grads_j = sync(sums)
    d_sin = Reduce(nb, nch, (first_low, low_d))
    grads_j, y, z = slot(grads_j, d_two.second(), d_sin.first())
    d_two.far(y)
    d_sin.near(z)
    low_c, low_s, gy_b, sums = stage_back_first(
        grad_one, grads_j, conv_c, sums_c, aff_c, conv_s, aff_s, live, w_out, conv_b, sums_b, aff_b, inner,
        table, nb,
    )
    grads_b = sync(sums)
    d_both = Reduce(nb, nch, (act_b, low_c), (slabs, low_s))
    skip_grad = stage_back_skip(low_s, w_skip)
    grads_b, x, y, d_sout.terms = slot(grads_b, d_sin.second(), d_both.first(), d_sout.terms)
    d_sin.far(x)
    d_both.near(y)
    low_b, gy_a, sums = stage_back_one(
        gy_b, conv_b, sums_b, grads_b, aff_b, k_one, conv_a, sums_a, aff_a, inner, table, nb
    )
    grads_a = sync(sums)
    d_one = Reduce(nb, nch, (cols_a, low_b), lead=(9,))
    grads_a, y, z, (skip_grad,), d_two.terms, d_sin.terms = slot(
        grads_a, d_one.first(), d_both.second(), [skip_grad], d_two.terms, d_sin.terms
    )
    d_one.near(y)
    d_both.far(z)
    early = BatchSum([d_sout, d_two, d_sin], nb, nch)
    early.along_x()
    grads_a, y = slot(grads_a, d_one.second())
    d_one.far(y)
    low_a, grad_in = stage_back_in(gy_a, conv_a, sums_a, grads_a, aff_a, w_in, skip_grad, inner, table, nch)
    d_in = Reduce(nb, nch, (slabs, low_a))
    inputs_grad = rows_out(from_subnets(grad_in, groups, nch), subnets)
    second_out_grad, kernel_two_grad, second_in_grad = early.along_z(low_a)
    d_in.direct()
    middle = BatchSum([d_both], nb, nch)
    middle.along_x(low_a)
    weight_out_grad, weight_skip_grad = middle.along_z()
    late = BatchSum([d_one, d_in], nb, nch)
    late.along_x()
    kernel_one_grad, weight_in_grad = late.along_z()

    def pair(sums, parts, which):
        total = jnp.sum(sums, axis=0).reshape(-1, parts, MID)
        both = jnp.stack([total[:, which].reshape(-1), total[:, 0].reshape(-1)])
        return both.reshape(2, nch, -1)

    norm_parts = [
        pair(grads_a, 2, 1), pair(grads_b, 2, 1), pair(grads_j, 3, 1), pair(grads_j, 3, 2), pair(grads_d, 2, 1),
        pair(grads_e, 2, 1), pair(grads_f, 2, 1),
    ]
    joined = jnp.moveaxis(jnp.concatenate(norm_parts, axis=2), 1, 0)
    mine = jnp.sum(lax.all_to_all(joined, "chan", 0, 0), axis=0) / groups
    norm_grads = []
    at = 0
    for part in norm_parts:
        norm_grads.append(mine[:, at : at + part.shape[2]])
        at += part.shape[2]

    shape = (3, 3, MID // nb, MID // nch)
    return (
        result, inputs_grad, weight_in_grad, kernel_one_grad.reshape(shape), weight_out_grad, weight_skip_grad,
        second_in_grad, kernel_two_grad.reshape(shape), second_out_grad, *norm_grads,
    )


def solution(mesh):
    nb, nch = mesh.shape["batch"], mesh.shape["chan"]
    maps = P(None, "batch", None, None, "chan")
    cols = P(None, "chan")
    taps = P(None, None, None, "chan")
    in_specs = (maps, cols, taps, cols, cols, cols, taps, cols) + (cols,) * 7 + (P(), P(), P(), maps)
    both = P("batch", "chan")
    split = P(None, None, "batch", "chan")
    out_specs = (maps, maps, both, split, both, both, both, split, both) + (cols,) * 7

    def run(*args):
        return body(*args, nb=nb, nch=nch)

    return jax.shard_map(run, mesh=mesh, in_specs=in_specs, out_specs=out_specs, check_vma=False)
```

```python
import jax
import jax.numpy as jnp
from jax import lax
from jax.experimental import pallas as pl
from jax.experimental.pallas import tpu as pltpu
from jax.sharding import PartitionSpec as P

EPS = 1e-05
F32 = jnp.float32
BF = jnp.bfloat16
MID = 512
Q = 4
R = 392
NT = (((1,), (1,)), ((), ()))
TN = (((0,), (0,)), ((), ()))
VMEM_LIMIT = 60 * 1024 * 1024


def call(body, grid, ins, outs, scratch=(), flops=0, moved=0):
    in_specs = []
    for item in ins:
        if item[1] is None:
            in_specs.append(pl.BlockSpec(memory_space=pltpu.SMEM))
        else:
            in_specs.append(pl.BlockSpec(item[1], item[2]))
    return pl.pallas_call(
        body,
        grid=grid,
        in_specs=in_specs,
        out_specs=[pl.BlockSpec(item[2], item[3]) for item in outs],
        out_shape=[jax.ShapeDtypeStruct(item[0], item[1]) for item in outs],
        scratch_shapes=list(scratch),
        compiler_params=pltpu.CompilerParams(vmem_limit_bytes=VMEM_LIMIT),
        cost_estimate=pl.CostEstimate(flops=int(flops), bytes_accessed=int(moved), transcendentals=0),
    )(*[item[0] for item in ins])


def whole(array):
    zeros = (0,) * array.ndim
    return (array, array.shape, lambda i: zeros)


def bands():
    return [slice(56 * h, 56 * h + 56) for h in range(7)]


def tall(value):
    return value.reshape(7, 8, value.shape[-1])


def dot(left, right, dims=(((1,), (0,)), ((), ()))):
    return lax.dot_general(left, right, dims, preferred_element_type=F32)


def mean_inv(sums, pixels):
    total = jnp.sum(sums, axis=0)
    mean = total[:, :MID] / pixels
    var = jnp.maximum(total[:, MID : 2 * MID] / pixels - mean * mean, 0.0)
    return mean, lax.rsqrt(var + EPS)


def forward_coef(sums, affine, mask, pixels):
    mean, inv = mean_inv(sums, pixels)
    scale = affine[0:1] * inv
    return mask * scale, mask * (affine[1:2] - mean * scale), mean, inv


def backward_coef(sums, grad_sums, which, affine, mask, pixels):
    mean, inv = mean_inv(sums, pixels)
    total = jnp.sum(grad_sums, axis=0)
    first = total[:, :MID] / pixels
    second = total[:, which * MID : (which + 1) * MID] / pixels
    scale = affine[0:1] * inv
    slope = -scale * second * inv
    return mask * scale, mask * slope, mask * (-scale * first - slope * mean)


def silu(u):
    return u * jax.nn.sigmoid(u)


def silu_both(u):
    s = jax.nn.sigmoid(u)
    return u * s, s * (1.0 + u * (1.0 - s))


def silu_slope(u):
    s = jax.nn.sigmoid(u)
    return s * (1.0 + u * (1.0 - s))


def fold(acc, value):
    return acc + jnp.sum(tall(value), axis=0)


def put_sums(ref, parts):
    row = jnp.concatenate([jnp.sum(part, axis=0, keepdims=True) for part in parts], axis=1)
    ref[...] = jnp.broadcast_to(row[None], ref.shape)


def value_sums(out_ref, pieces, live):
    first = jnp.zeros((8, MID), F32)
    second = jnp.zeros((8, MID), F32)
    for value in pieces:
        first = fold(first, value)
        second = fold(second, value * value)
    put_sums(out_ref, [first * live, second * live])


def rows_in(inputs):
    subnets, images, size, _, width = inputs.shape
    cut = inputs.reshape(subnets, images, size // 2, 2, size // 2, 2, width)
    return jnp.transpose(cut, (0, 3, 5, 2, 4, 1, 6)).reshape(subnets, 4, R, width)


def rows_out(rows, subnets):
    cut = rows.reshape(subnets, 2, 2, 7, 7, 8, rows.shape[3])
    return jnp.transpose(cut, (0, 5, 3, 1, 4, 2, 6)).reshape(subnets, 8, 14, 14, rows.shape[3])


def small_in(maps):
    return jnp.transpose(maps, (0, 2, 3, 1, 4)).reshape(maps.shape[0], R, maps.shape[4])


def small_out(rows, subnets):
    return jnp.transpose(rows.reshape(subnets, 7, 7, 8, rows.shape[2]), (0, 3, 1, 2, 4))


def lanes(ref):
    return jnp.concatenate([ref[j] for j in range(ref.shape[0])], axis=1)


def stage_a(slabs, weight, live, nb):
    nch, width = slabs.shape[0], slabs.shape[3]
    cin = nch * width

    def body(x_ref, w_ref, live_ref, a_ref, s_ref, sums):
        p = pl.program_id(0)
        x = jnp.concatenate([x_ref[k, 0] for k in range(nch)], axis=1)
        w = lanes(w_ref)
        value = dot(x, w)
        a_ref[0] = value

        @pl.when(p == 0)
        def _():
            sums[...] = jnp.zeros_like(sums)

        first = jnp.zeros((8, MID), F32)
        second = jnp.zeros((8, MID), F32)
        for band in bands():
            piece = value[band]
            first = fold(first, piece)
            second = fold(second, piece * piece)
        sums[0] += first
        sums[1] += second

        @pl.when(p == 3)
        def _():
            put_sums(s_ref, [sums[0] * live_ref[...], sums[1] * live_ref[...]])

    return call(
        body,
        (4,),
        [(slabs, (nch, 1, R, width), lambda i: (0, i, 0, 0)), whole(weight), whole(live)],
        [
            ((4, R, MID), F32, (1, R, MID), lambda i: (i, 0, 0)),
            ((nb, 1, 2 * MID), F32, (nb, 1, 2 * MID), lambda i: (0, 0, 0)),
        ],
        [pltpu.VMEM((2, 8, MID), F32)],
        flops=2 * 4 * R * cin * MID,
        moved=4 * R * (2 * cin + 4 * MID) + 2 * cin * MID,
    )


def stage_skip(slabs, weight, live, nb):
    nch, width = slabs.shape[0], slabs.shape[3]
    cin = nch * width

    def body(x_ref, w_ref, live_ref, o_ref, s_ref):
        x = jnp.concatenate([x_ref[k, 0] for k in range(nch)], axis=1)
        value = dot(x, w_ref[0])
        o_ref[...] = value
        value_sums(s_ref, [value[band] for band in bands()], live_ref[...])

    return call(
        body,
        (Q,),
        [
            (slabs, (nch, 1, R, width), lambda i: (0, 0, 0, 0)),
            (weight, (1, cin, MID), lambda i: (i, 0, 0)),
            whole(live),
        ],
        [
            ((R, Q * MID), F32, (R, MID), lambda i: (0, i)),
            ((nb, 1, Q * 2 * MID), F32, (nb, 1, 2 * MID), lambda i: (0, 0, i)),
        ],
        flops=2 * R * cin * Q * MID,
        moved=2 * R * cin + Q * MID * (2 * cin + 4 * R),
    )


def stage_conv_one(conv_a, sums_a, affine, inner, live, kernel, table, nb):
    def body(t_ref, a_ref, s_ref, g_ref, inner_ref, live_ref, k_ref, cols_ref, b_ref, o_ref, pad, acc):
        i = pl.program_id(0)

        @pl.when(i == 0)
        def _():
            scale, shift, _, _ = forward_coef(s_ref[...], g_ref[...], inner_ref[...], t_ref[0])
            pad[1, :, 0] = jnp.zeros((2, 8, 8, MID), F32)
            pad[:, 1, :, 0] = jnp.zeros((2, 8, 8, MID), F32)
            for p in range(4):
                for h, band in enumerate(bands()):
                    u = tall(a_ref[p, band]) * scale + shift
                    pad[p // 2, p % 2, h + 1, 1:8] = silu(u)

        hp = jnp.where(i == 1, 0, 1)
        h0 = jnp.minimum(i, 1)
        taps = []
        for dw in range(3):
            wp = 0 if dw == 1 else 1
            w0 = 0 if dw == 0 else 1
            tap = pad[hp, wp, pl.ds(h0, 7), w0 : w0 + 7].reshape(R, MID).astype(BF)
            cols_ref[:, dw * MID : (dw + 1) * MID] = tap
            taps.append(tap)
        value = sum(dot(taps[dw], jnp.concatenate([k_ref[j, dw] for j in range(Q)], axis=1)) for dw in range(3))

        @pl.when(i == 0)
        def _():
            acc[...] = value

        @pl.when(i > 0)
        def _():
            acc[...] += value

        @pl.when(i == 2)
        def _():
            low = acc[...].astype(BF).astype(F32)
            b_ref[...] = low
            value_sums(o_ref, [low[band] for band in bands()], live_ref[...])

    return call(
        body,
        (3,),
        [
            (table, None),
            whole(conv_a),
            whole(sums_a),
            whole(affine),
            whole(inner),
            whole(live),
            (kernel, (Q, 3, MID, MID // Q), lambda i: (0, i, 0, 0)),
        ],
        [
            ((R, 9 * MID), BF, (R, 3 * MID), lambda i: (0, i)),
            ((R, MID), F32, (R, MID), lambda i: (0, 0)),
            ((nb, 1, 2 * MID), F32, (nb, 1, 2 * MID), lambda i: (0, 0, 0)),
        ],
        [pltpu.VMEM((2, 2, 8, 8, 8, MID), F32), pltpu.VMEM((R, MID), F32)],
        flops=2 * R * 9 * MID * MID,
        moved=4 * 4 * R * MID + 2 * R * 9 * MID + 2 * 9 * MID * MID,
    )


def stage_conv_two(conv_d, sums_d, affine, inner, live, kernel, table, nb):
    def body(t_ref, d_ref, s_ref, g_ref, inner_ref, live_ref, k_ref, cols_ref, e_ref, o_ref, pad, acc):
        i = pl.program_id(0)

        @pl.when(i == 0)
        def _():
            scale, shift, _, _ = forward_coef(s_ref[...], g_ref[...], inner_ref[...], t_ref[1])
            pad[...] = jnp.zeros_like(pad)
            for h, band in enumerate(bands()):
                u = tall(d_ref[band]) * scale + shift
                pad[h + 1, 1:8] = silu(u)

        taps = []
        for dw in range(3):
            tap = pad[pl.ds(i, 7), dw : dw + 7].reshape(R, MID).astype(BF)
            cols_ref[:, dw * MID : (dw + 1) * MID] = tap
            taps.append(tap)
        value = sum(dot(taps[dw], jnp.concatenate([k_ref[j, dw] for j in range(Q)], axis=1)) for dw in range(3))

        @pl.when(i == 0)
        def _():
            acc[...] = value

        @pl.when(i > 0)
        def _():
            acc[...] += value

        @pl.when(i == 2)
        def _():
            low = acc[...].astype(BF).astype(F32)
            e_ref[...] = low
            value_sums(o_ref, [low[band] for band in bands()], live_ref[...])

    return call(
        body,
        (3,),
        [
            (table, None),
            whole(conv_d),
            whole(sums_d),
            whole(affine),
            whole(inner),
            whole(live),
            (kernel, (Q, 3, MID, MID // Q), lambda i: (0, i, 0, 0)),
        ],
        [
            ((R, 9 * MID), BF, (R, 3 * MID), lambda i: (0, i)),
            ((R, MID), F32, (R, MID), lambda i: (0, 0)),
            ((nb, 1, 2 * MID), F32, (nb, 1, 2 * MID), lambda i: (0, 0, 0)),
        ],
        [pltpu.VMEM((9, 9, 8, MID), F32), pltpu.VMEM((R, MID), F32)],
        flops=2 * R * 9 * MID * MID,
        moved=4 * R * MID + 2 * R * 9 * MID + 2 * 9 * MID * MID,
    )


def stage_expand(conv, sums, affine, inner, live, weight, table, nb, beside=None):
    parts = 2 if beside is None else 4

    def body(t_ref, b_ref, s_ref, g_ref, inner_ref, live_ref, w_ref, *refs):
        act_ref, o_ref, sum_ref, wide = refs[-4:]
        i = pl.program_id(0)

        @pl.when(i == 0)
        def _():
            scale, shift, _, _ = forward_coef(s_ref[...], g_ref[...], inner_ref[...], t_ref[1])
            for band in bands():
                u = tall(b_ref[band]) * scale + shift
                wide[band] = silu(u).reshape(56, MID)
            act_ref[...] = wide[...].astype(BF)

        value = dot(act_ref[...], w_ref[0])
        o_ref[...] = value
        value_sums(sum_ref.at[:, :, : 2 * MID], [value[band] for band in bands()], live_ref[...])
        if beside is not None:
            sum_ref[:, :, 2 * MID :] = refs[0][...]

    return call(
        body,
        (Q,),
        [
            (table, None),
            whole(conv),
            whole(sums),
            whole(affine),
            whole(inner),
            whole(live),
            (weight, (1, MID, MID), lambda i: (i, 0, 0)),
        ]
        + ([] if beside is None else [sum_chunk(beside)]),
        [
            ((R, MID), BF, (R, MID), lambda i: (0, 0)),
            ((R, Q * MID), F32, (R, MID), lambda i: (0, i)),
            ((nb, 1, Q * parts * MID), F32, (nb, 1, parts * MID), lambda i: (0, 0, i)),
        ],
        [pltpu.VMEM((R, MID), F32)],
        flops=2 * R * MID * Q * MID,
        moved=4 * R * MID * (Q + 1) + 2 * MID * MID * Q,
    )


def chunk(array, parts=1):
    return (array, (array.shape[0], parts * MID), lambda i: (0, i))


def sum_chunk(array, parts=2):
    return (array, (array.shape[0], 1, parts * MID), lambda i: (0, 0, i))


def stage_join(conv_c, sums_c, affine_c, conv_s, affine_s, live, weight, table, nb):
    def body(t_ref, c_ref, sc_ref, gc_ref, v_ref, gv_ref, live_ref, w_ref, f_ref, low_ref, d_ref, o_ref, acc):
        i = pl.program_id(0)
        live = live_ref[...]
        scale_c, shift_c, _, _ = forward_coef(sc_ref[...], gc_ref[...], live, t_ref[1])
        scale_s, shift_s, _, _ = forward_coef(sc_ref[:, :, 2 * MID :], gv_ref[...], live, t_ref[1])
        shift = shift_c + shift_s
        for band in bands():
            u = tall(c_ref[band]) * scale_c + tall(v_ref[band]) * scale_s + shift
            f_ref[band] = silu(u).reshape(56, MID)
        low = f_ref[...].astype(BF)
        low_ref[...] = low
        value = dot(low, lanes(w_ref))

        @pl.when(i == 0)
        def _():
            acc[...] = value

        @pl.when(i > 0)
        def _():
            acc[...] += value

        @pl.when(i == Q - 1)
        def _():
            total = acc[...]
            d_ref[...] = total
            value_sums(o_ref, [total[band] for band in bands()], live)

    return call(
        body,
        (Q,),
        [
            (table, None),
            chunk(conv_c),
            sum_chunk(sums_c, 4),
            chunk(affine_c),
            chunk(conv_s),
            chunk(affine_s),
            whole(live),
            (weight, (Q, MID, MID // Q), lambda i: (0, i, 0)),
        ],
        [
            ((R, Q * MID), F32, (R, MID), lambda i: (0, i)),
            ((R, Q * MID), BF, (R, MID), lambda i: (0, i)),
            ((R, MID), F32, (R, MID), lambda i: (0, 0)),
            ((nb, 1, 2 * MID), F32, (nb, 1, 2 * MID), lambda i: (0, 0, 0)),
        ],
        [pltpu.VMEM((R, MID), F32)],
        flops=2 * R * MID * Q * MID,
        moved=14 * R * MID * Q + 2 * MID * MID * Q,
    )


def stage_result(conv_f, sums_f, affine, first, cotangent, live, table, nb):
    nch, width = cotangent.shape[0], cotangent.shape[2]
    per = nch // Q

    def body(t_ref, f_ref, s_ref, g_ref, y_ref, ct_ref, live_ref, r_ref, gs_ref, o_ref, wide):
        live = live_ref[...]
        on = t_ref[2]
        scale, shift, mean, inv = forward_coef(s_ref[...], g_ref[...], live, t_ref[1])
        ct = jnp.concatenate([ct_ref[k] for k in range(per)], axis=1).astype(F32)
        first_sum = jnp.zeros((8, MID), F32)
        second_sum = jnp.zeros((8, MID), F32)
        for band in bands():
            v = tall(f_ref[band])
            y = tall(y_ref[band])
            u = v * scale + shift + y
            second, slope = silu_both(u)
            wide[band] = (y + on * (second - y)).reshape(56, MID)
            grad = on * tall(ct[band]) * slope
            gs_ref[band] = grad.reshape(56, MID)
            first_sum = first_sum + jnp.sum(grad, axis=0)
            second_sum = second_sum + jnp.sum(grad * (v - mean), axis=0)
        result = wide[...].astype(BF)
        for k in range(per):
            r_ref[k] = result[:, k * width : (k + 1) * width]
        put_sums(o_ref, [first_sum * live, second_sum * live * inv])

    return call(
        body,
        (Q,),
        [
            (table, None),
            chunk(conv_f),
            sum_chunk(sums_f),
            chunk(affine),
            chunk(first),
            (cotangent, (per, R, width), lambda i: (i, 0, 0)),
            whole(live),
        ],
        [
            ((nch, R, width), BF, (per, R, width), lambda i: (i, 0, 0)),
            ((R, Q * MID), F32, (R, MID), lambda i: (0, i)),
            ((nb, 1, Q * 2 * MID), F32, (nb, 1, 2 * MID), lambda i: (0, 0, i)),
        ],
        [pltpu.VMEM((R, MID), F32)],
        moved=16 * R * Q * MID,
    )


def finish_inner(grad, conv_ref, sums, affine, mask, pixels, out_put, sum_ref):
    scale, shift, mean, inv = forward_coef(sums, affine, mask, pixels)
    first = jnp.zeros((8, MID), F32)
    second = jnp.zeros((8, MID), F32)
    for band in bands():
        v = tall(conv_ref[band])
        gy = mask * (tall(grad[band]) * silu_slope(v * scale + shift))
        out_put(band, gy.reshape(56, MID))
        first = first + jnp.sum(gy, axis=0)
        second = second + jnp.sum(gy * (v - mean), axis=0)
    put_sums(sum_ref, [first, second * inv])


def stage_back_f(gs, conv_f, sums_f, grad_f, affine_f, live, weight, conv_e, sums_e, affine_e, inner, table, nb):
    def body(
        t_ref, gs_ref, f_ref, sf_ref, gf_ref, af_ref, live_ref, w_ref, e_ref, se_ref, ae_ref, inner_ref,
        low_ref, gy_ref, o_ref, acc, wide,
    ):
        i = pl.program_id(0)
        a, b, c = backward_coef(sf_ref[...], gf_ref[...], 1, af_ref[...], live_ref[...], t_ref[1])
        for band in bands():
            wide[band] = (tall(gs_ref[band]) * a + tall(f_ref[band]) * b + c).reshape(56, MID)
        low = wide[...].astype(BF)
        low_ref[...] = low
        value = dot(low, w_ref[0], NT)

        @pl.when(i == 0)
        def _():
            acc[...] = value

        @pl.when(i > 0)
        def _():
            acc[...] += value

        @pl.when(i == Q - 1)
        def _():
            def put(band, piece):
                gy_ref[band] = piece

            finish_inner(acc, e_ref, se_ref[...], ae_ref[...], inner_ref[...], t_ref[1], put, o_ref)

    return call(
        body,
        (Q,),
        [
            (table, None),
            chunk(gs),
            chunk(conv_f),
            sum_chunk(sums_f),
            sum_chunk(grad_f),
            chunk(affine_f),
            whole(live),
            (weight, (1, MID, MID), lambda i: (i, 0, 0)),
            whole(conv_e),
            whole(sums_e),
            whole(affine_e),
            whole(inner),
        ],
        [
            ((R, Q * MID), BF, (R, MID), lambda i: (0, i)),
            ((R, MID), F32, (R, MID), lambda i: (0, 0)),
            ((nb, 1, 2 * MID), F32, (nb, 1, 2 * MID), lambda i: (0, 0, 0)),
        ],
        [pltpu.VMEM((R, MID), F32), pltpu.VMEM((R, MID), F32)],
        flops=2 * R * MID * Q * MID,
        moved=10 * R * MID * Q + 2 * MID * MID * Q,
    )


def stage_back_two(gy_e, conv_e, sums_e, grad_e, affine_e, kernel, conv_d, sums_d, affine_d, inner, table, nb):
    def body(
        t_ref, gy_ref, e_ref, se_ref, ge_ref, ae_ref, k_ref, d_ref, sd_ref, ad_ref, inner_ref,
        low_ref, out_ref, o_ref, pad, acc, wide,
    ):
        i = pl.program_id(0)

        @pl.when(i == 0)
        def _():
            a, b, c = backward_coef(se_ref[...], ge_ref[...], 1, ae_ref[...], inner_ref[...], t_ref[1])
            pad[...] = jnp.zeros_like(pad)
            for h, band in enumerate(bands()):
                value = tall(gy_ref[band]) * a + tall(e_ref[band]) * b + c
                wide[band] = value.reshape(56, MID)
                pad[h + 1, 1:8] = value
            low_ref[...] = wide[...].astype(BF)

        total = None
        for dw in range(3):
            tap = pad[pl.ds(2 - i, 7), 2 - dw : 9 - dw].reshape(R, MID).astype(BF)
            part = dot(tap, jnp.concatenate([k_ref[j, dw] for j in range(Q)], axis=1), NT)
            total = part if total is None else total + part

        @pl.when(i == 0)
        def _():
            acc[...] = total

        @pl.when(i > 0)
        def _():
            acc[...] += total

        @pl.when(i == 2)
        def _():
            low = acc[...].astype(BF).astype(F32)

            def put(band, piece):
                out_ref[band] = piece

            finish_inner(low, d_ref, sd_ref[...], ad_ref[...], inner_ref[...], t_ref[1], put, o_ref)

    return call(
        body,
        (3,),
        [
            (table, None),
            whole(gy_e),
            whole(conv_e),
            whole(sums_e),
            whole(grad_e),
            whole(affine_e),
            (kernel, (Q, 3, MID, MID // Q), lambda i: (0, i, 0, 0)),
            whole(conv_d),
            whole(sums_d),
            whole(affine_d),
            whole(inner),
        ],
        [
            ((R, MID), BF, (R, MID), lambda i: (0, 0)),
            ((R, MID), F32, (R, MID), lambda i: (0, 0)),
            ((nb, 1, 2 * MID), F32, (nb, 1, 2 * MID), lambda i: (0, 0, 0)),
        ],
        [pltpu.VMEM((9, 9, 8, MID), F32), pltpu.VMEM((R, MID), F32), pltpu.VMEM((R, MID), F32)],
        flops=2 * R * 9 * MID * MID,
        moved=16 * R * MID + 2 * 9 * MID * MID,
    )


def stage_back_join(
    gy_d, conv_d, sums_d, grad_d, affine_d, inner, weight, cotangent, gs, conv_c, sums_c, affine_c, conv_s,
    affine_s, live, table, nb,
):
    nch, width = cotangent.shape[0], cotangent.shape[2]
    per = nch // Q

    def body(
        t_ref, gy_ref, d_ref, sd_ref, gd_ref, ad_ref, inner_ref, w_ref, ct_ref, gs_ref, c_ref, sc_ref, ac_ref, v_ref,
        av_ref, live_ref, low_ref, out_ref, o_ref, wide,
    ):
        i = pl.program_id(0)
        live = live_ref[...]

        @pl.when(i == 0)
        def _():
            a, b, c = backward_coef(sd_ref[...], gd_ref[...], 1, ad_ref[...], inner_ref[...], t_ref[1])
            for band in bands():
                wide[band] = (tall(gy_ref[band]) * a + tall(d_ref[band]) * b + c).reshape(56, MID)
            low_ref[...] = wide[...].astype(BF)

        back = dot(low_ref[...], lanes(w_ref), NT)
        ct = jnp.concatenate([ct_ref[k] for k in range(per)], axis=1).astype(F32)
        scale_c, shift_c, mean_c, inv_c = forward_coef(sc_ref[...], ac_ref[...], live, t_ref[1])
        scale_s, shift_s, mean_s, inv_s = forward_coef(sc_ref[:, :, 2 * MID :], av_ref[...], live, t_ref[1])
        shift = shift_c + shift_s
        off = 1.0 - t_ref[2]
        one = jnp.zeros((8, MID), F32)
        two = jnp.zeros((8, MID), F32)
        three = jnp.zeros((8, MID), F32)
        for band in bands():
            c = tall(c_ref[band])
            v = tall(v_ref[band])
            u = c * scale_c + v * scale_s + shift
            grad = off * tall(ct[band]) + tall(gs_ref[band]) + tall(back[band])
            grad = live * (grad * silu_slope(u))
            out_ref[band] = grad.reshape(56, MID)
            one = one + jnp.sum(grad, axis=0)
            two = two + jnp.sum(grad * (c - mean_c), axis=0)
            three = three + jnp.sum(grad * (v - mean_s), axis=0)
        put_sums(o_ref, [one, two * inv_c, three * inv_s])

    return call(
        body,
        (Q,),
        [
            (table, None),
            whole(gy_d),
            whole(conv_d),
            whole(sums_d),
            whole(grad_d),
            whole(affine_d),
            whole(inner),
            (weight, (Q, MID, MID // Q), lambda i: (0, i, 0)),
            (cotangent, (per, R, width), lambda i: (i, 0, 0)),
            chunk(gs),
            chunk(conv_c),
            sum_chunk(sums_c, 4),
            chunk(affine_c),
            chunk(conv_s),
            chunk(affine_s),
            whole(live),
        ],
        [
            ((R, MID), BF, (R, MID), lambda i: (0, 0)),
            ((R, Q * MID), F32, (R, MID), lambda i: (0, i)),
            ((nb, 1, Q * 3 * MID), F32, (nb, 1, 3 * MID), lambda i: (0, 0, i)),
        ],
        [pltpu.VMEM((R, MID), F32)],
        flops=2 * R * MID * Q * MID,
        moved=18 * R * MID * Q + 2 * MID * MID * Q,
    )


def stage_back_first(
    grad, sums_g, conv_c, sums_c, affine_c, conv_s, affine_s, live, weight, conv_b, sums_b, affine_b, inner,
    table, nb,
):
    def body(
        t_ref, g_ref, sg_ref, c_ref, sc_ref, ac_ref, v_ref, av_ref, live_ref, w_ref, b_ref, sb_ref, ab_ref,
        inner_ref, lowc_ref, lows_ref, out_ref, o_ref, acc, wide,
    ):
        i = pl.program_id(0)
        live = live_ref[...]
        a, b, c = backward_coef(sc_ref[:, :, 2 * MID :], sg_ref[...], 2, av_ref[...], live, t_ref[1])
        for band in bands():
            wide[band] = (tall(g_ref[band]) * a + tall(v_ref[band]) * b + c).reshape(56, MID)
        lows_ref[...] = wide[...].astype(BF)
        a, b, c = backward_coef(sc_ref[...], sg_ref[...], 1, ac_ref[...], live, t_ref[1])
        for band in bands():
            wide[band] = (tall(g_ref[band]) * a + tall(c_ref[band]) * b + c).reshape(56, MID)
        low = wide[...].astype(BF)
        lowc_ref[...] = low
        value = dot(low, w_ref[0], NT)

        @pl.when(i == 0)
        def _():
            acc[...] = value

        @pl.when(i > 0)
        def _():
            acc[...] += value

        @pl.when(i == Q - 1)
        def _():
            def put(band, piece):
                out_ref[band] = piece

            finish_inner(acc, b_ref, sb_ref[...], ab_ref[...], inner_ref[...], t_ref[1], put, o_ref)

    return call(
        body,
        (Q,),
        [
            (table, None),
            chunk(grad),
            sum_chunk(sums_g, 3),
            chunk(conv_c),
            sum_chunk(sums_c, 4),
            chunk(affine_c),
            chunk(conv_s),
            chunk(affine_s),
            whole(live),
            (weight, (1, MID, MID), lambda i: (i, 0, 0)),
            whole(conv_b),
            whole(sums_b),
            whole(affine_b),
            whole(inner),
        ],
        [
            ((R, Q * MID), BF, (R, MID), lambda i: (0, i)),
            ((R, Q * MID), BF, (R, MID), lambda i: (0, i)),
            ((R, MID), F32, (R, MID), lambda i: (0, 0)),
            ((nb, 1, 2 * MID), F32, (nb, 1, 2 * MID), lambda i: (0, 0, 0)),
        ],
        [pltpu.VMEM((R, MID), F32), pltpu.VMEM((R, MID), F32)],
        flops=2 * R * MID * Q * MID,
        moved=16 * R * MID * Q + 2 * MID * MID * Q,
    )


def stage_back_skip(low, weight):
    cin = weight.shape[1]

    def body(g_ref, w_ref, o_ref):
        i = pl.program_id(0)
        value = dot(g_ref[...], w_ref[0], NT)

        @pl.when(i == 0)
        def _():
            o_ref[...] = value

        @pl.when(i > 0)
        def _():
            o_ref[...] += value

    return call(
        body,
        (Q,),
        [chunk(low), (weight, (1, cin, MID), lambda i: (i, 0, 0))],
        [((R, cin), F32, (R, cin), lambda i: (0, 0))],
        flops=2 * R * cin * Q * MID,
        moved=4 * R * cin + 2 * R * Q * MID + 2 * cin * Q * MID,
    )[0]


def stage_back_one(gy_b, conv_b, sums_b, grad_b, affine_b, kernel, conv_a, sums_a, affine_a, inner, table, nb):
    def body(
        t_ref, gy_ref, b_ref, sb_ref, gb_ref, ab_ref, k_ref, a_ref, sa_ref, aa_ref, inner_ref,
        low_ref, out_ref, o_ref, pad, acc, wide,
    ):
        i = pl.program_id(0)

        @pl.when(i == 0)
        def _():
            a, b, c = backward_coef(sb_ref[...], gb_ref[...], 1, ab_ref[...], inner_ref[...], t_ref[1])
            pad[7] = jnp.zeros((8, 8, MID), F32)
            pad[:, 7] = jnp.zeros((8, 8, MID), F32)
            for h, band in enumerate(bands()):
                value = tall(gy_ref[band]) * a + tall(b_ref[band]) * b + c
                wide[band] = value.reshape(56, MID)
                pad[h, 0:7] = value
            low_ref[...] = wide[...].astype(BF)

        h0 = jnp.where(i == 0, 1, 0)
        near = pad[pl.ds(h0, 7), 0:7].reshape(R, MID).astype(BF)
        far = pad[pl.ds(h0, 7), 1:8].reshape(R, MID).astype(BF)
        k = [jnp.concatenate([k_ref[j, dw] for j in range(Q)], axis=1) for dw in range(3)]
        even = dot(near, k[1], NT)
        odd = dot(far, k[0], NT) + dot(near, k[2], NT)

        @pl.when(i == 0)
        def _():
            acc[2] = even
            acc[3] = odd

        @pl.when(i == 1)
        def _():
            acc[0] = even
            acc[1] = odd

        @pl.when(i == 2)
        def _():
            acc[2] += even
            acc[3] += odd
            mask = inner_ref[...]
            scale, shift, mean, inv = forward_coef(sa_ref[...], aa_ref[...], mask, t_ref[0])
            first = jnp.zeros((8, MID), F32)
            second = jnp.zeros((8, MID), F32)
            for p in range(4):
                wide[...] = acc[p].astype(BF).astype(F32)
                for band in bands():
                    v = tall(a_ref[p, band])
                    gy = mask * (tall(wide[band]) * silu_slope(v * scale + shift))
                    out_ref[p, band] = gy.reshape(56, MID)
                    first = first + jnp.sum(gy, axis=0)
                    second = second + jnp.sum(gy * (v - mean), axis=0)
            put_sums(o_ref, [first, second * inv])

    return call(
        body,
        (3,),
        [
            (table, None),
            whole(gy_b),
            whole(conv_b),
            whole(sums_b),
            whole(grad_b),
            whole(affine_b),
            (kernel, (Q, 3, MID, MID // Q), lambda i: (0, i, 0, 0)),
            whole(conv_a),
            whole(sums_a),
            whole(affine_a),
            whole(inner),
        ],
        [
            ((R, MID), BF, (R, MID), lambda i: (0, 0)),
            ((4, R, MID), F32, (4, R, MID), lambda i: (0, 0, 0)),
            ((nb, 1, 2 * MID), F32, (nb, 1, 2 * MID), lambda i: (0, 0, 0)),
        ],
        [pltpu.VMEM((8, 8, 8, MID), F32), pltpu.VMEM((4, R, MID), F32), pltpu.VMEM((R, MID), F32)],
        flops=2 * R * 9 * MID * MID,
        moved=32 * R * MID + 2 * 9 * MID * MID,
    )


def stage_back_in(gy_a, conv_a, sums_a, grad_a, affine_a, weight, skip_grad, inner, table, nch):
    cin = weight.shape[1]
    width = cin // nch

    def body(t_ref, gy_ref, a_ref, sa_ref, ga_ref, aa_ref, w_ref, s_ref, inner_ref, low_ref, out_ref, wide):
        i = pl.program_id(0)
        a, b, c = backward_coef(sa_ref[...], ga_ref[...], 1, aa_ref[...], inner_ref[...], t_ref[0])
        for band in bands():
            wide[band] = (tall(gy_ref[0, band]) * a + tall(a_ref[0, band]) * b + c).reshape(56, MID)
        low = wide[...].astype(BF)
        low_ref[0] = low
        value = dot(low, lanes(w_ref), NT)

        @pl.when(i == 0)
        def _():
            both = (value + s_ref[...]).astype(BF)
            for k in range(nch):
                out_ref[k, 0] = both[:, k * width : (k + 1) * width]

        @pl.when(i > 0)
        def _():
            both = value.astype(BF)
            for k in range(nch):
                out_ref[k, 0] = both[:, k * width : (k + 1) * width]

    return call(
        body,
        (4,),
        [
            (table, None),
            (gy_a, (1, R, MID), lambda i: (i, 0, 0)),
            (conv_a, (1, R, MID), lambda i: (i, 0, 0)),
            whole(sums_a),
            whole(grad_a),
            whole(affine_a),
            whole(weight),
            whole(skip_grad),
            whole(inner),
        ],
        [
            ((4, R, MID), BF, (1, R, MID), lambda i: (i, 0, 0)),
            ((nch, 4, R, width), BF, (nch, 1, R, width), lambda i: (0, i, 0, 0)),
        ],
        [pltpu.VMEM((R, MID), F32)],
        flops=2 * 4 * R * cin * MID,
        moved=4 * R * (10 * MID + 2 * cin) + 2 * cin * MID + 4 * R * cin,
    )


def after(value, *others):
    return lax.optimization_barrier((value,) + others)[0]


NEAR = [(i, i ^ 1) for i in range(Q)]
FAR = [(i, i ^ 2) for i in range(Q)]


def gather_far(part, nch):
    return lax.ppermute(part, "chan", FAR) if nch == Q else None


def gather_rest(part, other, nch, *when):
    if nch == Q:
        c = lax.axis_index("chan")
        part, other = lax.optimization_barrier((part, other) + when)[:2]
        parts = [part, lax.ppermute(part, "chan", NEAR), other, lax.ppermute(other, "chan", NEAR)]
        return place(parts, c)
    full = lax.all_gather(part, "chan", axis=part.ndim - 1, tiled=True)
    cut = full.reshape(full.shape[:-1] + (Q, full.shape[-1] // Q))
    return jnp.moveaxis(cut, -2, 0)


def place(parts, c):
    shape = parts[0].shape
    cuts = shape[0] if len(shape) == 3 else (2 if shape[0] % 32 == 0 else 1)
    rows = shape[0] // cuts

    def body(c_ref, *refs):
        ins, out, held, in_sems, out_sems = refs[:Q], refs[Q], refs[Q + 1], refs[Q + 2], refs[Q + 3]
        into, away = [], []
        for i in range(cuts):
            for k in range(Q):
                span = pl.ds(i * rows, rows)
                into.append(pltpu.make_async_copy(ins[k].at[span], held.at[k, span], in_sems.at[k, i]))
                goal = out.at[jnp.bitwise_xor(c_ref[0], k), span]
                away.append(pltpu.make_async_copy(held.at[k, span], goal, out_sems.at[k, i]))
        for copy in into:
            copy.start()
        for copy, leave in zip(into, away):
            copy.wait()
            leave.start()
        for leave in away:
            leave.wait()

    return pl.pallas_call(
        body,
        in_specs=[pl.BlockSpec(memory_space=pltpu.SMEM)] + [pl.BlockSpec(memory_space=pl.ANY)] * Q,
        out_specs=pl.BlockSpec(memory_space=pl.ANY),
        out_shape=jax.ShapeDtypeStruct((Q,) + shape, parts[0].dtype),
        scratch_shapes=[
            pltpu.VMEM((Q,) + shape, parts[0].dtype),
            pltpu.SemaphoreType.DMA((Q, cuts)),
            pltpu.SemaphoreType.DMA((Q, cuts)),
        ],
        compiler_params=pltpu.CompilerParams(vmem_limit_bytes=VMEM_LIMIT),
        cost_estimate=pl.CostEstimate(flops=0, bytes_accessed=4 * Q * parts[0].size, transcendentals=0),
    )(c.reshape(1).astype(jnp.int32), *parts)


def exchange(pick, nch):
    c = lax.axis_index("chan")
    parts = [pick(c)]
    for k in (3, 2, 1):
        parts.insert(1, lax.ppermute(pick(jnp.bitwise_xor(c, k)), "chan", [(i, i ^ k) for i in range(Q)]))
    return place(parts, c)


def to_subnets(maps, order, groups, nch, *tokens):
    if groups == 1:

        def pick(member):
            part = order(lax.dynamic_index_in_dim(maps, member, 0, keepdims=True))[0]
            return after(part, *tokens) if tokens else part

        return exchange(pick, nch)
    blocks = order(maps)
    images = 8 // groups
    shape = blocks.shape
    cut = blocks.reshape(shape[:-2] + (49, groups, images, shape[-1]))
    cut = jnp.moveaxis(cut, -3, 1)
    cut = jnp.pad(cut, [(0, 0)] * (cut.ndim - 2) + [(0, 8 - images), (0, 0)])
    blocks = cut.reshape((shape[0] * groups,) + shape[1:])
    return lax.all_to_all(blocks, "chan", 0, 0)


def from_subnets(blocks, groups, nch):
    if groups == 1:
        return exchange(lambda member: lax.dynamic_index_in_dim(blocks, member, 0, keepdims=False), nch)
    back = lax.all_to_all(blocks, "chan", 0, 0)
    images = 8 // groups
    shape = back.shape
    cut = back.reshape((shape[0] // groups, groups) + shape[1:-2] + (49, 8, shape[-1]))[..., :images, :]
    cut = jnp.moveaxis(cut, 1, -3)
    return cut.reshape((shape[0] // groups,) + shape[1:-2] + (R, shape[-1]))


def sum_pairs(one, two):
    cut = [part.reshape(part.shape[0], 1, Q, -1) for part in (one, two)]
    return jnp.concatenate(cut, axis=3).reshape(one.shape[0], 1, -1)


def make_sync(groups, nch):
    def sync(sums):
        got = lax.all_to_all(sums, "batch", 0, 0)
        if groups > 1:
            pairs = [[g * groups + k for k in range(groups)] for g in range(nch // groups)]
            got = lax.psum(got, "chan", axis_index_groups=pairs)
        return got

    return sync


def weight_product(pairs, columns, plus, width, apart):
    every = columns is None
    depths = [left.shape[1] if left.ndim == 2 else left.shape[0] * left.shape[3] for left, _ in pairs]
    depth = sum(depths)
    if len(pairs) > 1 or pairs[0][0].ndim == 4:
        step = min(256, pairs[-1][0].shape[-1])
    else:
        step = {4608: 1536, 2048: 1024}.get(depth, 512)
    starts = [sum(depths[:m]) // step for m in range(len(pairs) + 1)]

    def local(i, m):
        return jnp.clip(i - starts[m], 0, starts[m + 1] - starts[m] - 1)

    args, specs = [], []
    for m, (left, grad) in enumerate(pairs):
        phases, rows = grad.shape[0], grad.shape[1]
        args.append(left)
        if left.ndim == 2:
            specs.append(pl.BlockSpec((rows, step), lambda i, c, m=m: (0, local(i, m))))
        else:
            specs.append(pl.BlockSpec((1, phases, rows, step), lambda i, c, m=m: (local(i, m), 0, 0, 0)))
        if every:
            args.append(grad)
            specs.append(pl.BlockSpec(grad.shape, lambda i, c: (0, 0, 0)))
        else:
            for k in range(2):
                args.append(grad)
                specs.append(pl.BlockSpec((phases, rows, width), lambda i, c, k=k: (0, 0, c[k])))
    each = 2 if every else 3
    pair = pl.BlockSpec((2, step, width), lambda i, c: (0, i, 0))
    if plus is not None:
        args.append(plus)
        specs.append(pair)

    def one(m, refs, more, outs):
        left, grad = pairs[m]
        l_ref = refs[0]
        value = None
        for p in range(grad.shape[0]):
            right = refs[1][p] if every else jnp.concatenate([refs[1][p], refs[2][p]], axis=1)
            piece = dot(l_ref[...] if left.ndim == 2 else l_ref[0, p], right, TN)
            value = piece if value is None else value + piece
        for k in range(Q if every else 2):
            part = value[:, k * width : (k + 1) * width]
            if more is not None:
                part = part + more[k].astype(F32)
            if apart:
                outs[k][...] = part.astype(BF)
            else:
                outs[0][k] = part.astype(BF)

    def body(c_ref, *refs):
        ins, outs = refs[: len(args)], refs[len(args) :]
        more = ins[-1] if plus is not None else None
        if len(pairs) == 1:
            one(0, ins, more, outs)
            return
        i = pl.program_id(0)
        for m in range(len(pairs)):

            @pl.when(jnp.logical_and(i >= starts[m], i < starts[m + 1]))
            def _(m=m):
                one(m, ins[each * m : each * m + each], more, outs)

    single = pl.BlockSpec((step, width), lambda i, c: (i, 0))
    block = jax.ShapeDtypeStruct((depth, width), BF)
    if every:
        out_specs = pl.BlockSpec((Q, step, width), lambda i, c: (0, i, 0))
        out_shape = jax.ShapeDtypeStruct((Q, depth, width), BF)
    elif apart:
        out_specs, out_shape = [single, single], [block, block]
    else:
        out_specs, out_shape = pair, jax.ShapeDtypeStruct((2, depth, width), BF)
    flops = sum(4 * left.size * width for left, _ in pairs)
    return pl.pallas_call(
        body,
        grid_spec=pltpu.PrefetchScalarGridSpec(
            num_scalar_prefetch=1, grid=(depth // step,), in_specs=specs, out_specs=out_specs
        ),
        out_shape=out_shape,
        compiler_params=pltpu.CompilerParams(vmem_limit_bytes=VMEM_LIMIT),
        cost_estimate=pl.CostEstimate(flops=0, bytes_accessed=0, transcendentals=0),
    )(jnp.zeros((1,), jnp.int32) if every else columns, *args)


class Reduce:
    def __init__(self, nb, nch, *pairs, lead=()):
        self.nb, self.nch, self.lead = nb, nch, lead
        self.pairs = [(left, grad if grad.ndim == 3 else grad[None]) for left, grad in pairs]
        self.width = self.pairs[0][1].shape[2] // nch
        self.depths = [left.shape[1] if left.ndim == 2 else left.shape[0] * left.shape[3] for left, _ in pairs]
        self.depth = sum(self.depths)
        self.quick = nch == Q

    def first(self):
        if not self.quick:
            parts = []
            for (left, grad), depth in zip(self.pairs, self.depths):
                if left.ndim == 4:
                    left = jnp.transpose(left[:, : grad.shape[0]], (1, 2, 0, 3)).reshape(-1, depth)
                parts.append(dot(left, grad.reshape(-1, grad.shape[2]), TN).astype(BF))
            full = jnp.concatenate(parts, axis=0)
            self.terms = [lax.psum_scatter(full, "chan", scatter_dimension=1, tiled=True)]
            return []
        c = lax.axis_index("chan").astype(jnp.int32)
        self.value = weight_product(self.pairs, jnp.stack([c ^ 1, c ^ 3]), None, self.width, False)
        return [self.value]

    def near(self, held=None):
        if self.quick:
            self.value = lax.ppermute(held[0], "chan", NEAR)

    def second(self):
        if not self.quick:
            return []
        c = lax.axis_index("chan").astype(jnp.int32)
        out = weight_product(self.pairs, jnp.stack([c, c ^ 2]), self.value, self.width, True)
        return list(out)

    def far(self, held=None):
        if self.quick:
            self.terms = [held[0], lax.ppermute(held[1], "chan", FAR)]

    def pieces(self, together=True):
        outs = []
        for terms in [self.terms] if together else [[term] for term in self.terms]:
            at = 0
            for depth in self.depths:
                rows = depth // self.nb
                outs.append((terms, self.lead, at // rows, rows, self.width))
                at += depth
        return outs


def total_rows(piece):
    _, _, _, rows, width = piece
    return rows * (width // 128)


def half_sum(pieces, which, gots=None):
    args, specs = [], []
    for terms, lead, first, rows, width in pieces:
        for term in terms:
            if lead:
                args.append(term.reshape(lead + (8, rows // lead[0], width)))
                block = lead + (1, rows // lead[0], width)
                specs.append(pl.BlockSpec(block, lambda i, c: (0, 2 * i + c[0], 0, 0)))
            else:
                args.append(term)
                specs.append(pl.BlockSpec((rows, width), lambda i, c, first=first: (first + 2 * i + c[0], 0)))
    count = len(args)
    for got in gots or []:
        args.append(got)
        specs.append(pl.BlockSpec((1,) + got.shape[1:], lambda i, c: (i, 0, 0)))
    height = sum(total_rows(piece) for piece in pieces)

    def body(c_ref, *refs):
        out = refs[-1]
        parts = []
        at = 0
        for terms, lead, _, rows, width in pieces:
            total = None
            for ref in refs[at : at + len(terms)]:
                part = ref[...].reshape(rows, width).astype(F32)
                total = part if total is None else total + part
            at += len(terms)
            parts += [total[:, 128 * k : 128 * k + 128] for k in range(width // 128)]
        value = jnp.concatenate(parts, axis=0) if len(parts) > 1 else parts[0]
        if gots:
            more = [ref[0].astype(F32) for ref in refs[count : count + len(gots)]]
            value = value + (jnp.concatenate(more, axis=0) if len(more) > 1 else more[0])
        out[0] = value.astype(BF)

    return pl.pallas_call(
        body,
        grid_spec=pltpu.PrefetchScalarGridSpec(
            num_scalar_prefetch=1,
            grid=(4,),
            in_specs=specs,
            out_specs=pl.BlockSpec((1, height, 128), lambda i, c: (i, 0, 0)),
        ),
        out_shape=jax.ShapeDtypeStruct((4, height, 128), BF),
        compiler_params=pltpu.CompilerParams(vmem_limit_bytes=VMEM_LIMIT),
        cost_estimate=pl.CostEstimate(flops=0, bytes_accessed=0, transcendentals=0),
    )(which.reshape(1).astype(jnp.int32), *args)


def split_total(total, pieces):
    outs = []
    at = 0
    for piece in pieces:
        rows, width = piece[3], piece[4]
        part = total[at : at + total_rows(piece)]
        at += total_rows(piece)
        if width > 128:
            part = jnp.transpose(part.reshape(width // 128, rows, 128), (1, 0, 2)).reshape(rows, width)
        outs.append(part)
    return outs


def along_x(send):
    return lax.ppermute(send, "batch", [(i, i ^ 1) for i in range(8)])


def along_z(keep):
    lines = [[2 * k + x for k in range(4)] for x in range(2)]
    return lax.all_to_all(keep, "batch", 0, 0, axis_index_groups=lines)


def along_z_parts(keep, z):
    parts = [lax.dynamic_index_in_dim(keep, z, 0, keepdims=False)]
    for k in (3, 2, 1):
        block = lax.dynamic_index_in_dim(keep, jnp.bitwise_xor(z, k), 0, keepdims=False)
        parts.append(lax.ppermute(block, "batch", [(i, i ^ (2 * k)) for i in range(8)]))
    return parts


def batch_scatter(member, nb):
    total = member.terms[0]
    outs = []
    at = 0
    for depth in member.depths:
        part = total[at : at + depth]
        at += depth
        if member.lead:
            part = jnp.moveaxis(part.reshape(member.lead + (nb, -1, member.width)), 1, 0)
        part = part.reshape(nb, depth // nb, member.width)
        outs.append(lax.psum_scatter(part, "batch", scatter_dimension=0, tiled=True)[0].astype(F32))
    return outs


def slot(value, *groups):
    flat = [array for group in groups for array in group]
    held = lax.optimization_barrier((value, *flat))
    out = []
    at = 1
    for group in groups:
        out.append(list(held[at : at + len(group)]))
        at += len(group)
    return [held[0]] + out


def body(
    inputs, weight_in, kernel_one, weight_out, weight_skip, second_in, kernel_two, second_out, norm_reduce,
    norm_kernel, norm_expand, norm_skip, later_reduce, later_kernel, later_expand, widths, depths, counts, cotangent,
    *, nb, nch,
):
    subnets, per = inputs.shape[0], inputs.shape[1]
    groups = nch // subnets
    images = per // groups
    chan = lax.axis_index("chan")
    member, half = chan // groups, chan % groups
    slots = jnp.arange(8, dtype=jnp.int32)
    ids = lax.axis_index("batch") * per + half * images + slots
    count = counts[member]
    live_image = jnp.logical_and(slots < images, ids < count).astype(F32)[:, None]
    live = jnp.broadcast_to(live_image, (8, MID))
    inner = live * (jnp.arange(MID, dtype=jnp.int32) < widths[member]).astype(F32)[None, :]
    high, low = inputs.shape[2], cotangent.shape[2]
    table = jnp.stack(
        [
            count.astype(F32) * (high * high),
            count.astype(F32) * (low * low),
            (depths[member] == 2).astype(F32),
        ]
    )
    sync = make_sync(groups, nch)

    small = (norm_reduce, norm_kernel, later_reduce, later_kernel)
    large = (norm_expand, norm_skip, later_expand)
    joined = jnp.concatenate(small + large, axis=1)
    spread = lax.all_to_all(jnp.broadcast_to(joined[None], (nch,) + joined.shape), "chan", 0, 0)
    at = 0
    full = []
    for part in small + large:
        piece = lax.slice_in_dim(spread, at, at + part.shape[1], axis=2)
        full.append(jnp.moveaxis(piece, 0, 1).reshape(2, -1))
        at += part.shape[1]
    flat_one = kernel_one.reshape((9,) + kernel_one.shape[2:])
    flat_two = kernel_two.reshape((9,) + kernel_two.shape[2:])
    far = gather_far(weight_in, nch)
    slabs = to_subnets(inputs, rows_in, groups, nch, *([far] if nch == Q else []))
    slabs, full = slot(slabs, full)
    aff_a, aff_b, aff_d, aff_e, aff_c, aff_s, aff_f = full
    w_in = gather_rest(weight_in, far, nch)
    far_one = gather_far(after(flat_one, slabs), nch)
    far_out = gather_far(after(weight_out, w_in), nch)

    conv_a, sums = stage_a(slabs, w_in, live, nb)
    far_in = gather_far(after(second_in, sums), nch)
    far_skip = gather_far(after(weight_skip, sums), nch)
    sums_a = sync(sums)
    k_one = gather_rest(flat_one, far_one, nch, sums_a)
    cols_a, conv_b, sums = stage_conv_one(conv_a, sums_a, aff_a, inner, live, k_one, table, nb)
    w_out = gather_rest(weight_out, far_out, nch, sums)
    s_in = gather_rest(second_in, far_in, nch, sums)
    sums_b = sync(sums)
    sums_b, (w_out, s_in) = slot(sums_b, [w_out, s_in])
    act_b, conv_c, sums = stage_expand(conv_b, sums_b, aff_b, inner, live, w_out, table, nb)
    far_two = gather_far(after(flat_two, sums), nch)
    w_skip = gather_rest(weight_skip, far_skip, nch, sums)
    sums_c = sync(sums)
    conv_s, sums = stage_skip(slabs, w_skip, live, nb)
    sums_s = sync(sums)
    sums_c = sum_pairs(sums_c, sums_s)
    first, first_low, conv_d, sums = stage_join(conv_c, sums_c, aff_c, conv_s, aff_s, live, s_in, table, nb)
    far_sout = gather_far(after(second_out, sums), nch)
    k_two = gather_rest(flat_two, far_two, nch, sums)
    sums_d = sync(sums)
    sums_d, (k_two,) = slot(sums_d, [k_two])
    cols_d, conv_e, sums = stage_conv_two(conv_d, sums_d, aff_d, inner, live, k_two, table, nb)
    cot = to_subnets(cotangent, small_in, groups, nch, sums)
    s_out = gather_rest(second_out, far_sout, nch, sums)
    sums_e = sync(sums)
    sums_e, (s_out,) = slot(sums_e, [s_out])
    act_e, conv_f, sums = stage_expand(conv_e, sums_e, aff_e, inner, live, s_out, table, nb)
    sums_f = sync(sums)
    sums_f, (cot,) = slot(sums_f, [cot])
    result, grad_sum, sums = stage_result(conv_f, sums_f, aff_f, first, cot, live, table, nb)
    grads_f = sync(sums)
    result = small_out(from_subnets(result, groups, nch), subnets)

    low_f, gy_e, sums = stage_back_f(
        grad_sum, conv_f, sums_f, grads_f, aff_f, live, s_out, conv_e, sums_e, aff_e, inner, table, nb
    )
    grads_e = sync(sums)
    quick = nch == Q and nb == 8
    b_index = lax.axis_index("batch")
    x_index, z_index = b_index % 2, b_index // 2

    d_sout = Reduce(nb, nch, (act_e, low_f))
    grads_e, x = slot(grads_e, d_sout.first())
    d_sout.near(x)
    low_e, gy_d, sums = stage_back_two(
        gy_e, conv_e, sums_e, grads_e, aff_e, k_two, conv_d, sums_d, aff_d, inner, table, nb
    )
    grads_d = sync(sums)
    d_two = Reduce(nb, nch, (cols_d, low_e), lead=(9,))
    grads_d, x, y, (result,) = slot(grads_d, d_sout.second(), d_two.first(), [result])
    d_sout.far(x)
    d_two.near(y)
    low_d, grad_one, sums = stage_back_join(
        gy_d, conv_d, sums_d, grads_d, aff_d, inner, s_in, cot, grad_sum, conv_c, sums_c, aff_c, conv_s,
        aff_s, live, table, nb,
    )
    grads_j = sync(sums)
    d_sin = Reduce(nb, nch, (first_low, low_d))
    grads_j, y, z, d_sout.terms = slot(grads_j, d_two.second(), d_sin.first(), d_sout.terms)
    d_two.far(y)
    d_sin.near(z)
    low_c, low_s, gy_b, sums = stage_back_first(
        grad_one, grads_j, conv_c, sums_c, aff_c, conv_s, aff_s, live, w_out, conv_b, sums_b, aff_b, inner,
        table, nb,
    )
    grads_b = sync(sums)
    d_both = Reduce(nb, nch, (act_b, low_c), (slabs, low_s))
    skip_grad = stage_back_skip(low_s, w_skip)
    grads_b, x, y, d_two.terms = slot(grads_b, d_sin.second(), d_both.first(), d_two.terms)
    d_sin.far(x)
    d_both.near(y)
    early = []
    send = []
    if quick:
        early = d_sout.pieces() + d_two.pieces()
        send = [half_sum(early, 1 - x_index)]
    grads_b, send = slot(grads_b, send)
    got = along_x(send[0]) if quick else None
    low_b, gy_a, sums = stage_back_one(
        gy_b, conv_b, sums_b, grads_b, aff_b, k_one, conv_a, sums_a, aff_a, inner, table, nb
    )
    grads_a = sync(sums)
    d_one = Reduce(nb, nch, (cols_a, low_b), lead=(9,))
    kept = [half_sum(early, x_index, [got])] if quick else []
    grads_a, y, z, (skip_grad,), kept, d_sin.terms = slot(
        grads_a, d_one.first(), d_both.second(), [skip_grad], kept, d_sin.terms
    )
    d_one.near(y)
    d_both.far(z)
    ones = d_one.second()
    if quick:
        d_one.terms = ones
        one_pieces = d_one.pieces(False)
        ones = [half_sum(one_pieces, 1 - x_index)]
    grads_a, ones = slot(grads_a, ones)
    if quick:
        one_got = along_x(ones[0])
    else:
        d_one.far(ones)
    low_a, grad_in = stage_back_in(gy_a, conv_a, sums_a, grads_a, aff_a, w_in, skip_grad, inner, table, nch)
    d_in = Reduce(nb, nch, (slabs, low_a))
    if quick:
        grad_in = lax.all_to_all(grad_in, "chan", 0, 0)
    else:
        grad_in = from_subnets(grad_in, groups, nch)
    x = d_in.first()
    d_in.near(x)
    ins = d_in.second()
    if quick:
        early_parts = along_z_parts(after(kept[0], low_a), z_index)
        d_in.terms = ins
        in_pieces = d_in.pieces(False)
        one_kept = after(half_sum(one_pieces, x_index, [one_got]), low_a)
        held = lax.optimization_barrier(tuple(d_both.terms) + (one_kept,))
        d_both.terms, one_kept = list(held[:2]), held[2]
        one_parts = along_z_parts(one_kept, z_index)
        middle = d_sin.pieces() + d_both.pieces()
        middle_got = along_x(half_sum(middle, 1 - x_index))
        in_got = along_x(half_sum(in_pieces, 1 - x_index))
        middle_parts = along_z_parts(half_sum(middle + in_pieces, x_index, [middle_got, in_got]), z_index)
        outs = []
        for parts, pieces in ((early_parts, early), (one_parts, one_pieces), (middle_parts, middle + in_pieces)):
            total = parts[0].astype(F32)
            for part in parts[1:]:
                total = total + part.astype(F32)
            outs += split_total(total, pieces)
        (
            second_out_grad, kernel_two_grad, one_own, one_far, second_in_grad, weight_out_grad, weight_skip_grad,
            in_own, in_far,
        ) = outs
        across = lax.ppermute(jnp.concatenate([one_far, in_far], axis=0).astype(BF), "chan", FAR).astype(F32)
        kernel_one_grad = one_own + across[: one_own.shape[0]]
        weight_in_grad = in_own + across[one_own.shape[0] :]
    else:
        d_in.far(ins)
        if nch == Q:
            for member in (d_sout, d_two, d_sin, d_both, d_one, d_in):
                member.terms = [(member.terms[0].astype(F32) + member.terms[1].astype(F32)).astype(BF)]
        (second_out_grad,), (kernel_two_grad,) = batch_scatter(d_sout, nb), batch_scatter(d_two, nb)
        (second_in_grad,), (kernel_one_grad,) = batch_scatter(d_sin, nb), batch_scatter(d_one, nb)
        (weight_out_grad, weight_skip_grad), (weight_in_grad,) = batch_scatter(d_both, nb), batch_scatter(d_in, nb)
    inputs_grad = rows_out(grad_in, subnets)

    def pair(sums, parts, which):
        total = jnp.sum(sums, axis=0).reshape(-1, parts, MID)
        both = jnp.stack([total[:, which].reshape(-1), total[:, 0].reshape(-1)])
        return both.reshape(2, nch, -1)

    norm_parts = [
        pair(grads_a, 2, 1), pair(grads_b, 2, 1), pair(grads_j, 3, 1), pair(grads_j, 3, 2), pair(grads_d, 2, 1),
        pair(grads_e, 2, 1), pair(grads_f, 2, 1),
    ]
    joined = after(jnp.moveaxis(jnp.concatenate(norm_parts, axis=2), 1, 0), inputs_grad)
    mine = jnp.sum(lax.all_to_all(joined, "chan", 0, 0), axis=0) / groups
    norm_grads = []
    at = 0
    for part in norm_parts:
        norm_grads.append(mine[:, at : at + part.shape[2]])
        at += part.shape[2]

    shape = (3, 3, MID // nb, MID // nch)
    return (
        result, inputs_grad, weight_in_grad, kernel_one_grad.reshape(shape), weight_out_grad, weight_skip_grad,
        second_in_grad, kernel_two_grad.reshape(shape), second_out_grad, *norm_grads,
    )


def solution(mesh):
    nb, nch = mesh.shape["batch"], mesh.shape["chan"]
    maps = P(None, "batch", None, None, "chan")
    cols = P(None, "chan")
    taps = P(None, None, None, "chan")
    in_specs = (maps, cols, taps, cols, cols, cols, taps, cols) + (cols,) * 7 + (P(), P(), P(), maps)
    both = P("batch", "chan")
    split = P(None, None, "batch", "chan")
    out_specs = (maps, maps, both, split, both, both, both, split, both) + (cols,) * 7

    def run(*args):
        return body(*args, nb=nb, nch=nch)

    return jax.shard_map(run, mesh=mesh, in_specs=in_specs, out_specs=out_specs, check_vma=False)
```

```python
import jax
import jax.numpy as jnp
from jax import lax
from jax.experimental import pallas as pl
from jax.experimental.pallas import tpu as pltpu
from jax.sharding import PartitionSpec as P

EPS = 1e-05
F32 = jnp.float32
BF = jnp.bfloat16
MID = 512
Q = 4
R = 392
NT = (((1,), (1,)), ((), ()))
TN = (((0,), (0,)), ((), ()))
VMEM_LIMIT = 53 * 1024 * 1024


def call(body, grid, ins, outs, scratch=(), flops=0, moved=0):
    in_specs = []
    for item in ins:
        if item[1] is None:
            in_specs.append(pl.BlockSpec(memory_space=pltpu.SMEM))
        else:
            in_specs.append(pl.BlockSpec(item[1], item[2]))
    return pl.pallas_call(
        body,
        grid=grid,
        in_specs=in_specs,
        out_specs=[pl.BlockSpec(item[2], item[3]) for item in outs],
        out_shape=[jax.ShapeDtypeStruct(item[0], item[1]) for item in outs],
        scratch_shapes=list(scratch),
        compiler_params=pltpu.CompilerParams(vmem_limit_bytes=VMEM_LIMIT),
        cost_estimate=pl.CostEstimate(flops=int(flops * 0.25), bytes_accessed=int(moved * 0.25), transcendentals=0),
    )(*[item[0] for item in ins])


def whole(array):
    zeros = (0,) * array.ndim
    return (array, array.shape, lambda i: zeros)


def bands():
    return [slice(56 * h, 56 * h + 56) for h in range(7)]


def tall(value):
    return value.reshape(7, 8, value.shape[-1])


def dot(left, right, dims=(((1,), (0,)), ((), ()))):
    return lax.dot_general(left, right, dims, preferred_element_type=F32)


def mean_inv(sums, pixels):
    total = jnp.sum(sums, axis=0)
    mean = total[:, :MID] / pixels
    var = jnp.maximum(total[:, MID : 2 * MID] / pixels - mean * mean, 0.0)
    return mean, lax.rsqrt(var + EPS)


def forward_coef(sums, affine, mask, pixels):
    mean, inv = mean_inv(sums, pixels)
    scale = affine[0:1] * inv
    return mask * scale, mask * (affine[1:2] - mean * scale), mean, inv


def backward_coef(sums, grad_sums, which, affine, mask, pixels):
    mean, inv = mean_inv(sums, pixels)
    total = jnp.sum(grad_sums, axis=0)
    first = total[:, :MID] / pixels
    second = total[:, which * MID : (which + 1) * MID] / pixels
    scale = affine[0:1] * inv
    slope = -scale * second * inv
    return mask * scale, mask * slope, mask * (-scale * first - slope * mean)


def silu(u):
    return u * jax.nn.sigmoid(u)


def silu_both(u):
    s = jax.nn.sigmoid(u)
    return u * s, s * (1.0 + u * (1.0 - s))


def silu_slope(u):
    s = jax.nn.sigmoid(u)
    return s * (1.0 + u * (1.0 - s))


def fold(acc, value):
    return acc + jnp.sum(tall(value), axis=0)


def put_sums(ref, parts):
    row = jnp.concatenate([jnp.sum(part, axis=0, keepdims=True) for part in parts], axis=1)
    ref[...] = jnp.broadcast_to(row[None], ref.shape)


def value_sums(out_ref, pieces, live):
    first = jnp.zeros((8, MID), F32)
    second = jnp.zeros((8, MID), F32)
    for value in pieces:
        first = fold(first, value)
        second = fold(second, value * value)
    put_sums(out_ref, [first * live, second * live])


def rows_in(inputs):
    subnets, images, size, _, width = inputs.shape
    cut = inputs.reshape(subnets, images, size // 2, 2, size // 2, 2, width)
    return jnp.transpose(cut, (0, 3, 5, 2, 4, 1, 6)).reshape(subnets, 4, R, width)


def rows_out(rows, subnets):
    cut = rows.reshape(subnets, 2, 2, 7, 7, 8, rows.shape[3])
    return jnp.transpose(cut, (0, 5, 3, 1, 4, 2, 6)).reshape(subnets, 8, 14, 14, rows.shape[3])


def small_in(maps):
    return jnp.transpose(maps, (0, 2, 3, 1, 4)).reshape(maps.shape[0], R, maps.shape[4])


def small_out(rows, subnets):
    return jnp.transpose(rows.reshape(subnets, 7, 7, 8, rows.shape[2]), (0, 3, 1, 2, 4))


def lanes(ref):
    return jnp.concatenate([ref[j] for j in range(ref.shape[0])], axis=1)


def stage_a(slabs, weight, live, nb):
    nch, width = slabs.shape[0], slabs.shape[3]
    cin = nch * width

    def body(x_ref, w_ref, live_ref, a_ref, s_ref, sums):
        p = pl.program_id(0)
        x = jnp.concatenate([x_ref[k, 0] for k in range(nch)], axis=1)
        w = lanes(w_ref)
        value = dot(x, w)
        a_ref[0] = value

        @pl.when(p == 0)
        def _():
            sums[...] = jnp.zeros_like(sums)

        first = jnp.zeros((8, MID), F32)
        second = jnp.zeros((8, MID), F32)
        for band in bands():
            piece = value[band]
            first = fold(first, piece)
            second = fold(second, piece * piece)
        sums[0] += first
        sums[1] += second

        @pl.when(p == 3)
        def _():
            put_sums(s_ref, [sums[0] * live_ref[...], sums[1] * live_ref[...]])

    return call(
        body,
        (4,),
        [(slabs, (nch, 1, R, width), lambda i: (0, i, 0, 0)), whole(weight), whole(live)],
        [
            ((4, R, MID), F32, (1, R, MID), lambda i: (i, 0, 0)),
            ((nb, 1, 2 * MID), F32, (nb, 1, 2 * MID), lambda i: (0, 0, 0)),
        ],
        [pltpu.VMEM((2, 8, MID), F32)],
        flops=2 * 4 * R * cin * MID,
        moved=4 * R * (2 * cin + 4 * MID) + 2 * cin * MID,
    )


def stage_skip(slabs, weight, live, nb):
    nch, width = slabs.shape[0], slabs.shape[3]
    cin = nch * width

    def body(x_ref, w_ref, live_ref, o_ref, s_ref):
        x = jnp.concatenate([x_ref[k, 0] for k in range(nch)], axis=1)
        value = dot(x, w_ref[0])
        o_ref[...] = value
        value_sums(s_ref, [value[band] for band in bands()], live_ref[...])

    return call(
        body,
        (Q,),
        [
            (slabs, (nch, 1, R, width), lambda i: (0, 0, 0, 0)),
            (weight, (1, cin, MID), lambda i: (i, 0, 0)),
            whole(live),
        ],
        [
            ((R, Q * MID), F32, (R, MID), lambda i: (0, i)),
            ((nb, 1, Q * 2 * MID), F32, (nb, 1, 2 * MID), lambda i: (0, 0, i)),
        ],
        flops=2 * R * cin * Q * MID,
        moved=2 * R * cin + Q * MID * (2 * cin + 4 * R),
    )


def stage_conv_one(conv_a, sums_a, affine, inner, live, kernel, table, nb):
    def body(t_ref, a_ref, s_ref, g_ref, inner_ref, live_ref, k_ref, cols_ref, b_ref, o_ref, pad, acc):
        i = pl.program_id(0)

        @pl.when(i == 0)
        def _():
            scale, shift, _, _ = forward_coef(s_ref[...], g_ref[...], inner_ref[...], t_ref[0])
            pad[1, :, 0] = jnp.zeros((2, 8, 8, MID), F32)
            pad[:, 1, :, 0] = jnp.zeros((2, 8, 8, MID), F32)
            for p in range(4):
                for h, band in enumerate(bands()):
                    u = tall(a_ref[p, band]) * scale + shift
                    pad[p // 2, p % 2, h + 1, 1:8] = silu(u)

        hp = jnp.where(i == 1, 0, 1)
        h0 = jnp.minimum(i, 1)
        taps = []
        for dw in range(3):
            wp = 0 if dw == 1 else 1
            w0 = 0 if dw == 0 else 1
            tap = pad[hp, wp, pl.ds(h0, 7), w0 : w0 + 7].reshape(R, MID).astype(BF)
            cols_ref[:, dw * MID : (dw + 1) * MID] = tap
            taps.append(tap)
        value = sum(dot(taps[dw], jnp.concatenate([k_ref[j, dw] for j in range(Q)], axis=1)) for dw in range(3))

        @pl.when(i == 0)
        def _():
            acc[...] = value

        @pl.when(i > 0)
        def _():
            acc[...] += value

        @pl.when(i == 2)
        def _():
            low = acc[...].astype(BF).astype(F32)
            b_ref[...] = low
            value_sums(o_ref, [low[band] for band in bands()], live_ref[...])

    return call(
        body,
        (3,),
        [
            (table, None),
            whole(conv_a),
            whole(sums_a),
            whole(affine),
            whole(inner),
            whole(live),
            (kernel, (Q, 3, MID, MID // Q), lambda i: (0, i, 0, 0)),
        ],
        [
            ((R, 9 * MID), BF, (R, 3 * MID), lambda i: (0, i)),
            ((R, MID), F32, (R, MID), lambda i: (0, 0)),
            ((nb, 1, 2 * MID), F32, (nb, 1, 2 * MID), lambda i: (0, 0, 0)),
        ],
        [pltpu.VMEM((2, 2, 8, 8, 8, MID), F32), pltpu.VMEM((R, MID), F32)],
        flops=2 * R * 9 * MID * MID,
        moved=4 * 4 * R * MID + 2 * R * 9 * MID + 2 * 9 * MID * MID,
    )


def stage_conv_two(conv_d, sums_d, affine, inner, live, kernel, table, nb):
    def body(t_ref, d_ref, s_ref, g_ref, inner_ref, live_ref, k_ref, cols_ref, e_ref, o_ref, pad, acc):
        i = pl.program_id(0)

        @pl.when(i == 0)
        def _():
            scale, shift, _, _ = forward_coef(s_ref[...], g_ref[...], inner_ref[...], t_ref[1])
            pad[...] = jnp.zeros_like(pad)
            for h, band in enumerate(bands()):
                u = tall(d_ref[band]) * scale + shift
                pad[h + 1, 1:8] = silu(u)

        taps = []
        for dw in range(3):
            tap = pad[pl.ds(i, 7), dw : dw + 7].reshape(R, MID).astype(BF)
            cols_ref[:, dw * MID : (dw + 1) * MID] = tap
            taps.append(tap)
        value = sum(dot(taps[dw], jnp.concatenate([k_ref[j, dw] for j in range(Q)], axis=1)) for dw in range(3))

        @pl.when(i == 0)
        def _():
            acc[...] = value

        @pl.when(i > 0)
        def _():
            acc[...] += value

        @pl.when(i == 2)
        def _():
            low = acc[...].astype(BF).astype(F32)
            e_ref[...] = low
            value_sums(o_ref, [low[band] for band in bands()], live_ref[...])

    return call(
        body,
        (3,),
        [
            (table, None),
            whole(conv_d),
            whole(sums_d),
            whole(affine),
            whole(inner),
            whole(live),
            (kernel, (Q, 3, MID, MID // Q), lambda i: (0, i, 0, 0)),
        ],
        [
            ((R, 9 * MID), BF, (R, 3 * MID), lambda i: (0, i)),
            ((R, MID), F32, (R, MID), lambda i: (0, 0)),
            ((nb, 1, 2 * MID), F32, (nb, 1, 2 * MID), lambda i: (0, 0, 0)),
        ],
        [pltpu.VMEM((9, 9, 8, MID), F32), pltpu.VMEM((R, MID), F32)],
        flops=2 * R * 9 * MID * MID,
        moved=4 * R * MID + 2 * R * 9 * MID + 2 * 9 * MID * MID,
    )


def stage_expand(conv, sums, affine, inner, live, weight, table, nb, beside=None):
    parts = 2 if beside is None else 4

    def body(t_ref, b_ref, s_ref, g_ref, inner_ref, live_ref, w_ref, *refs):
        act_ref, o_ref, sum_ref, wide = refs[-4:]
        i = pl.program_id(0)

        @pl.when(i == 0)
        def _():
            scale, shift, _, _ = forward_coef(s_ref[...], g_ref[...], inner_ref[...], t_ref[1])
            for band in bands():
                u = tall(b_ref[band]) * scale + shift
                wide[band] = silu(u).reshape(56, MID)
            act_ref[...] = wide[...].astype(BF)

        value = dot(act_ref[...], w_ref[0])
        o_ref[...] = value
        value_sums(sum_ref.at[:, :, : 2 * MID], [value[band] for band in bands()], live_ref[...])
        if beside is not None:
            sum_ref[:, :, 2 * MID :] = refs[0][...]

    return call(
        body,
        (Q,),
        [
            (table, None),
            whole(conv),
            whole(sums),
            whole(affine),
            whole(inner),
            whole(live),
            (weight, (1, MID, MID), lambda i: (i, 0, 0)),
        ]
        + ([] if beside is None else [sum_chunk(beside)]),
        [
            ((R, MID), BF, (R, MID), lambda i: (0, 0)),
            ((R, Q * MID), F32, (R, MID), lambda i: (0, i)),
            ((nb, 1, Q * parts * MID), F32, (nb, 1, parts * MID), lambda i: (0, 0, i)),
        ],
        [pltpu.VMEM((R, MID), F32)],
        flops=2 * R * MID * Q * MID,
        moved=4 * R * MID * (Q + 1) + 2 * MID * MID * Q,
    )


def chunk(array, parts=1):
    return (array, (array.shape[0], parts * MID), lambda i: (0, i))


def sum_chunk(array, parts=2):
    return (array, (array.shape[0], 1, parts * MID), lambda i: (0, 0, i))


def stage_join(conv_c, sums_c, affine_c, conv_s, affine_s, live, weight, table, nb):
    def body(t_ref, c_ref, sc_ref, gc_ref, v_ref, gv_ref, live_ref, w_ref, f_ref, low_ref, d_ref, o_ref, acc):
        i = pl.program_id(0)
        live = live_ref[...]
        scale_c, shift_c, _, _ = forward_coef(sc_ref[...], gc_ref[...], live, t_ref[1])
        scale_s, shift_s, _, _ = forward_coef(sc_ref[:, :, 2 * MID :], gv_ref[...], live, t_ref[1])
        shift = shift_c + shift_s
        for band in bands():
            u = tall(c_ref[band]) * scale_c + tall(v_ref[band]) * scale_s + shift
            f_ref[band] = silu(u).reshape(56, MID)
        low = f_ref[...].astype(BF)
        low_ref[...] = low
        value = dot(low, lanes(w_ref))

        @pl.when(i == 0)
        def _():
            acc[...] = value

        @pl.when(i > 0)
        def _():
            acc[...] += value

        @pl.when(i == Q - 1)
        def _():
            total = acc[...]
            d_ref[...] = total
            value_sums(o_ref, [total[band] for band in bands()], live)

    return call(
        body,
        (Q,),
        [
            (table, None),
            chunk(conv_c),
            sum_chunk(sums_c, 4),
            chunk(affine_c),
            chunk(conv_s),
            chunk(affine_s),
            whole(live),
            (weight, (Q, MID, MID // Q), lambda i: (0, i, 0)),
        ],
        [
            ((R, Q * MID), F32, (R, MID), lambda i: (0, i)),
            ((R, Q * MID), BF, (R, MID), lambda i: (0, i)),
            ((R, MID), F32, (R, MID), lambda i: (0, 0)),
            ((nb, 1, 2 * MID), F32, (nb, 1, 2 * MID), lambda i: (0, 0, 0)),
        ],
        [pltpu.VMEM((R, MID), F32)],
        flops=2 * R * MID * Q * MID,
        moved=14 * R * MID * Q + 2 * MID * MID * Q,
    )


def stage_result(conv_f, sums_f, affine, first, cotangent, live, table, nb):
    nch, width = cotangent.shape[0], cotangent.shape[2]
    per = nch // Q

    def body(t_ref, f_ref, s_ref, g_ref, y_ref, ct_ref, live_ref, r_ref, gs_ref, o_ref, wide):
        live = live_ref[...]
        on = t_ref[2]
        scale, shift, mean, inv = forward_coef(s_ref[...], g_ref[...], live, t_ref[1])
        ct = jnp.concatenate([ct_ref[k] for k in range(per)], axis=1).astype(F32)
        first_sum = jnp.zeros((8, MID), F32)
        second_sum = jnp.zeros((8, MID), F32)
        for band in bands():
            v = tall(f_ref[band])
            y = tall(y_ref[band])
            u = v * scale + shift + y
            second, slope = silu_both(u)
            wide[band] = (y + on * (second - y)).reshape(56, MID)
            grad = on * tall(ct[band]) * slope
            gs_ref[band] = grad.reshape(56, MID)
            first_sum = first_sum + jnp.sum(grad, axis=0)
            second_sum = second_sum + jnp.sum(grad * (v - mean), axis=0)
        result = wide[...].astype(BF)
        for k in range(per):
            r_ref[k] = result[:, k * width : (k + 1) * width]
        put_sums(o_ref, [first_sum * live, second_sum * live * inv])

    return call(
        body,
        (Q,),
        [
            (table, None),
            chunk(conv_f),
            sum_chunk(sums_f),
            chunk(affine),
            chunk(first),
            (cotangent, (per, R, width), lambda i: (i, 0, 0)),
            whole(live),
        ],
        [
            ((nch, R, width), BF, (per, R, width), lambda i: (i, 0, 0)),
            ((R, Q * MID), F32, (R, MID), lambda i: (0, i)),
            ((nb, 1, Q * 2 * MID), F32, (nb, 1, 2 * MID), lambda i: (0, 0, i)),
        ],
        [pltpu.VMEM((R, MID), F32)],
        moved=16 * R * Q * MID,
    )


def finish_inner(grad, conv_ref, sums, affine, mask, pixels, out_put, sum_ref):
    scale, shift, mean, inv = forward_coef(sums, affine, mask, pixels)
    first = jnp.zeros((8, MID), F32)
    second = jnp.zeros((8, MID), F32)
    for band in bands():
        v = tall(conv_ref[band])
        gy = mask * (tall(grad[band]) * silu_slope(v * scale + shift))
        out_put(band, gy.reshape(56, MID))
        first = first + jnp.sum(gy, axis=0)
        second = second + jnp.sum(gy * (v - mean), axis=0)
    put_sums(sum_ref, [first, second * inv])


def stage_back_f(gs, conv_f, sums_f, grad_f, affine_f, live, weight, conv_e, sums_e, affine_e, inner, table, nb):
    def body(
        t_ref, gs_ref, f_ref, sf_ref, gf_ref, af_ref, live_ref, w_ref, e_ref, se_ref, ae_ref, inner_ref,
        low_ref, gy_ref, o_ref, acc, wide,
    ):
        i = pl.program_id(0)
        a, b, c = backward_coef(sf_ref[...], gf_ref[...], 1, af_ref[...], live_ref[...], t_ref[1])
        for band in bands():
            wide[band] = (tall(gs_ref[band]) * a + tall(f_ref[band]) * b + c).reshape(56, MID)
        low = wide[...].astype(BF)
        low_ref[...] = low
        value = dot(low, w_ref[0], NT)

        @pl.when(i == 0)
        def _():
            acc[...] = value

        @pl.when(i > 0)
        def _():
            acc[...] += value

        @pl.when(i == Q - 1)
        def _():
            def put(band, piece):
                gy_ref[band] = piece

            finish_inner(acc, e_ref, se_ref[...], ae_ref[...], inner_ref[...], t_ref[1], put, o_ref)

    return call(
        body,
        (Q,),
        [
            (table, None),
            chunk(gs),
            chunk(conv_f),
            sum_chunk(sums_f),
            sum_chunk(grad_f),
            chunk(affine_f),
            whole(live),
            (weight, (1, MID, MID), lambda i: (i, 0, 0)),
            whole(conv_e),
            whole(sums_e),
            whole(affine_e),
            whole(inner),
        ],
        [
            ((R, Q * MID), BF, (R, MID), lambda i: (0, i)),
            ((R, MID), F32, (R, MID), lambda i: (0, 0)),
            ((nb, 1, 2 * MID), F32, (nb, 1, 2 * MID), lambda i: (0, 0, 0)),
        ],
        [pltpu.VMEM((R, MID), F32), pltpu.VMEM((R, MID), F32)],
        flops=2 * R * MID * Q * MID,
        moved=10 * R * MID * Q + 2 * MID * MID * Q,
    )


def stage_back_two(gy_e, conv_e, sums_e, grad_e, affine_e, kernel, conv_d, sums_d, affine_d, inner, table, nb):
    def body(
        t_ref, gy_ref, e_ref, se_ref, ge_ref, ae_ref, k_ref, d_ref, sd_ref, ad_ref, inner_ref,
        low_ref, out_ref, o_ref, pad, acc, wide,
    ):
        i = pl.program_id(0)

        @pl.when(i == 0)
        def _():
            a, b, c = backward_coef(se_ref[...], ge_ref[...], 1, ae_ref[...], inner_ref[...], t_ref[1])
            pad[...] = jnp.zeros_like(pad)
            for h, band in enumerate(bands()):
                value = tall(gy_ref[band]) * a + tall(e_ref[band]) * b + c
                wide[band] = value.reshape(56, MID)
                pad[h + 1, 1:8] = value
            low_ref[...] = wide[...].astype(BF)

        total = None
        for dw in range(3):
            tap = pad[pl.ds(2 - i, 7), 2 - dw : 9 - dw].reshape(R, MID).astype(BF)
            part = dot(tap, jnp.concatenate([k_ref[j, dw] for j in range(Q)], axis=1), NT)
            total = part if total is None else total + part

        @pl.when(i == 0)
        def _():
            acc[...] = total

        @pl.when(i > 0)
        def _():
            acc[...] += total

        @pl.when(i == 2)
        def _():
            low = acc[...].astype(BF).astype(F32)

            def put(band, piece):
                out_ref[band] = piece

            finish_inner(low, d_ref, sd_ref[...], ad_ref[...], inner_ref[...], t_ref[1], put, o_ref)

    return call(
        body,
        (3,),
        [
            (table, None),
            whole(gy_e),
            whole(conv_e),
            whole(sums_e),
            whole(grad_e),
            whole(affine_e),
            (kernel, (Q, 3, MID, MID // Q), lambda i: (0, i, 0, 0)),
            whole(conv_d),
            whole(sums_d),
            whole(affine_d),
            whole(inner),
        ],
        [
            ((R, MID), BF, (R, MID), lambda i: (0, 0)),
            ((R, MID), F32, (R, MID), lambda i: (0, 0)),
            ((nb, 1, 2 * MID), F32, (nb, 1, 2 * MID), lambda i: (0, 0, 0)),
        ],
        [pltpu.VMEM((9, 9, 8, MID), F32), pltpu.VMEM((R, MID), F32), pltpu.VMEM((R, MID), F32)],
        flops=2 * R * 9 * MID * MID,
        moved=16 * R * MID + 2 * 9 * MID * MID,
    )


def stage_back_join(
    gy_d, conv_d, sums_d, grad_d, affine_d, inner, weight, cotangent, gs, conv_c, sums_c, affine_c, conv_s,
    affine_s, live, table, nb,
):
    nch, width = cotangent.shape[0], cotangent.shape[2]
    per = nch // Q

    def body(
        t_ref, gy_ref, d_ref, sd_ref, gd_ref, ad_ref, inner_ref, w_ref, ct_ref, gs_ref, c_ref, sc_ref, ac_ref, v_ref,
        av_ref, live_ref, low_ref, out_ref, o_ref, wide,
    ):
        i = pl.program_id(0)
        live = live_ref[...]

        @pl.when(i == 0)
        def _():
            a, b, c = backward_coef(sd_ref[...], gd_ref[...], 1, ad_ref[...], inner_ref[...], t_ref[1])
            for band in bands():
                wide[band] = (tall(gy_ref[band]) * a + tall(d_ref[band]) * b + c).reshape(56, MID)
            low_ref[...] = wide[...].astype(BF)

        back = dot(low_ref[...], lanes(w_ref), NT)
        ct = jnp.concatenate([ct_ref[k] for k in range(per)], axis=1).astype(F32)
        scale_c, shift_c, mean_c, inv_c = forward_coef(sc_ref[...], ac_ref[...], live, t_ref[1])
        scale_s, shift_s, mean_s, inv_s = forward_coef(sc_ref[:, :, 2 * MID :], av_ref[...], live, t_ref[1])
        shift = shift_c + shift_s
        off = 1.0 - t_ref[2]
        one = jnp.zeros((8, MID), F32)
        two = jnp.zeros((8, MID), F32)
        three = jnp.zeros((8, MID), F32)
        for band in bands():
            c = tall(c_ref[band])
            v = tall(v_ref[band])
            u = c * scale_c + v * scale_s + shift
            grad = off * tall(ct[band]) + tall(gs_ref[band]) + tall(back[band])
            grad = live * (grad * silu_slope(u))
            out_ref[band] = grad.reshape(56, MID)
            one = one + jnp.sum(grad, axis=0)
            two = two + jnp.sum(grad * (c - mean_c), axis=0)
            three = three + jnp.sum(grad * (v - mean_s), axis=0)
        put_sums(o_ref, [one, two * inv_c, three * inv_s])

    return call(
        body,
        (Q,),
        [
            (table, None),
            whole(gy_d),
            whole(conv_d),
            whole(sums_d),
            whole(grad_d),
            whole(affine_d),
            whole(inner),
            (weight, (Q, MID, MID // Q), lambda i: (0, i, 0)),
            (cotangent, (per, R, width), lambda i: (i, 0, 0)),
            chunk(gs),
            chunk(conv_c),
            sum_chunk(sums_c, 4),
            chunk(affine_c),
            chunk(conv_s),
            chunk(affine_s),
            whole(live),
        ],
        [
            ((R, MID), BF, (R, MID), lambda i: (0, 0)),
            ((R, Q * MID), F32, (R, MID), lambda i: (0, i)),
            ((nb, 1, Q * 3 * MID), F32, (nb, 1, 3 * MID), lambda i: (0, 0, i)),
        ],
        [pltpu.VMEM((R, MID), F32)],
        flops=2 * R * MID * Q * MID,
        moved=18 * R * MID * Q + 2 * MID * MID * Q,
    )


def stage_back_first(
    grad, sums_g, conv_c, sums_c, affine_c, conv_s, affine_s, live, weight, conv_b, sums_b, affine_b, inner,
    table, nb,
):
    def body(
        t_ref, g_ref, sg_ref, c_ref, sc_ref, ac_ref, v_ref, av_ref, live_ref, w_ref, b_ref, sb_ref, ab_ref,
        inner_ref, lowc_ref, lows_ref, out_ref, o_ref, acc, wide,
    ):
        i = pl.program_id(0)
        live = live_ref[...]
        a, b, c = backward_coef(sc_ref[:, :, 2 * MID :], sg_ref[...], 2, av_ref[...], live, t_ref[1])
        for band in bands():
            wide[band] = (tall(g_ref[band]) * a + tall(v_ref[band]) * b + c).reshape(56, MID)
        lows_ref[...] = wide[...].astype(BF)
        a, b, c = backward_coef(sc_ref[...], sg_ref[...], 1, ac_ref[...], live, t_ref[1])
        for band in bands():
            wide[band] = (tall(g_ref[band]) * a + tall(c_ref[band]) * b + c).reshape(56, MID)
        low = wide[...].astype(BF)
        lowc_ref[...] = low
        value = dot(low, w_ref[0], NT)

        @pl.when(i == 0)
        def _():
            acc[...] = value

        @pl.when(i > 0)
        def _():
            acc[...] += value

        @pl.when(i == Q - 1)
        def _():
            def put(band, piece):
                out_ref[band] = piece

            finish_inner(acc, b_ref, sb_ref[...], ab_ref[...], inner_ref[...], t_ref[1], put, o_ref)

    return call(
        body,
        (Q,),
        [
            (table, None),
            chunk(grad),
            sum_chunk(sums_g, 3),
            chunk(conv_c),
            sum_chunk(sums_c, 4),
            chunk(affine_c),
            chunk(conv_s),
            chunk(affine_s),
            whole(live),
            (weight, (1, MID, MID), lambda i: (i, 0, 0)),
            whole(conv_b),
            whole(sums_b),
            whole(affine_b),
            whole(inner),
        ],
        [
            ((R, Q * MID), BF, (R, MID), lambda i: (0, i)),
            ((R, Q * MID), BF, (R, MID), lambda i: (0, i)),
            ((R, MID), F32, (R, MID), lambda i: (0, 0)),
            ((nb, 1, 2 * MID), F32, (nb, 1, 2 * MID), lambda i: (0, 0, 0)),
        ],
        [pltpu.VMEM((R, MID), F32), pltpu.VMEM((R, MID), F32)],
        flops=2 * R * MID * Q * MID,
        moved=16 * R * MID * Q + 2 * MID * MID * Q,
    )


def stage_back_skip(low, weight):
    cin = weight.shape[1]

    def body(g_ref, w_ref, o_ref):
        i = pl.program_id(0)
        value = dot(g_ref[...], w_ref[0], NT)

        @pl.when(i == 0)
        def _():
            o_ref[...] = value

        @pl.when(i > 0)
        def _():
            o_ref[...] += value

    return call(
        body,
        (Q,),
        [chunk(low), (weight, (1, cin, MID), lambda i: (i, 0, 0))],
        [((R, cin), F32, (R, cin), lambda i: (0, 0))],
        flops=2 * R * cin * Q * MID,
        moved=4 * R * cin + 2 * R * Q * MID + 2 * cin * Q * MID,
    )[0]


def stage_back_one(gy_b, conv_b, sums_b, grad_b, affine_b, kernel, conv_a, sums_a, affine_a, inner, table, nb):
    def body(
        t_ref, gy_ref, b_ref, sb_ref, gb_ref, ab_ref, k_ref, a_ref, sa_ref, aa_ref, inner_ref,
        low_ref, out_ref, o_ref, pad, acc, wide,
    ):
        i = pl.program_id(0)

        @pl.when(i == 0)
        def _():
            a, b, c = backward_coef(sb_ref[...], gb_ref[...], 1, ab_ref[...], inner_ref[...], t_ref[1])
            pad[7] = jnp.zeros((8, 8, MID), F32)
            pad[:, 7] = jnp.zeros((8, 8, MID), F32)
            for h, band in enumerate(bands()):
                value = tall(gy_ref[band]) * a + tall(b_ref[band]) * b + c
                wide[band] = value.reshape(56, MID)
                pad[h, 0:7] = value
            low_ref[...] = wide[...].astype(BF)

        h0 = jnp.where(i == 0, 1, 0)
        near = pad[pl.ds(h0, 7), 0:7].reshape(R, MID).astype(BF)
        far = pad[pl.ds(h0, 7), 1:8].reshape(R, MID).astype(BF)
        k = [jnp.concatenate([k_ref[j, dw] for j in range(Q)], axis=1) for dw in range(3)]
        even = dot(near, k[1], NT)
        odd = dot(far, k[0], NT) + dot(near, k[2], NT)

        @pl.when(i == 0)
        def _():
            acc[2] = even
            acc[3] = odd

        @pl.when(i == 1)
        def _():
            acc[0] = even
            acc[1] = odd

        @pl.when(i == 2)
        def _():
            acc[2] += even
            acc[3] += odd
            mask = inner_ref[...]
            scale, shift, mean, inv = forward_coef(sa_ref[...], aa_ref[...], mask, t_ref[0])
            first = jnp.zeros((8, MID), F32)
            second = jnp.zeros((8, MID), F32)
            for p in range(4):
                wide[...] = acc[p].astype(BF).astype(F32)
                for band in bands():
                    v = tall(a_ref[p, band])
                    gy = mask * (tall(wide[band]) * silu_slope(v * scale + shift))
                    out_ref[p, band] = gy.reshape(56, MID)
                    first = first + jnp.sum(gy, axis=0)
                    second = second + jnp.sum(gy * (v - mean), axis=0)
            put_sums(o_ref, [first, second * inv])

    return call(
        body,
        (3,),
        [
            (table, None),
            whole(gy_b),
            whole(conv_b),
            whole(sums_b),
            whole(grad_b),
            whole(affine_b),
            (kernel, (Q, 3, MID, MID // Q), lambda i: (0, i, 0, 0)),
            whole(conv_a),
            whole(sums_a),
            whole(affine_a),
            whole(inner),
        ],
        [
            ((R, MID), BF, (R, MID), lambda i: (0, 0)),
            ((4, R, MID), F32, (4, R, MID), lambda i: (0, 0, 0)),
            ((nb, 1, 2 * MID), F32, (nb, 1, 2 * MID), lambda i: (0, 0, 0)),
        ],
        [pltpu.VMEM((8, 8, 8, MID), F32), pltpu.VMEM((4, R, MID), F32), pltpu.VMEM((R, MID), F32)],
        flops=2 * R * 9 * MID * MID,
        moved=32 * R * MID + 2 * 9 * MID * MID,
    )


def stage_back_in(gy_a, conv_a, sums_a, grad_a, affine_a, weight, skip_grad, inner, table, nch):
    cin = weight.shape[1]
    width = cin // nch

    def body(t_ref, gy_ref, a_ref, sa_ref, ga_ref, aa_ref, w_ref, s_ref, inner_ref, low_ref, out_ref, wide):
        i = pl.program_id(0)
        a, b, c = backward_coef(sa_ref[...], ga_ref[...], 1, aa_ref[...], inner_ref[...], t_ref[0])
        for band in bands():
            wide[band] = (tall(gy_ref[0, band]) * a + tall(a_ref[0, band]) * b + c).reshape(56, MID)
        low = wide[...].astype(BF)
        low_ref[0] = low
        value = dot(low, lanes(w_ref), NT)

        @pl.when(i == 0)
        def _():
            both = (value + s_ref[...]).astype(BF)
            for k in range(nch):
                out_ref[k, 0] = both[:, k * width : (k + 1) * width]

        @pl.when(i > 0)
        def _():
            both = value.astype(BF)
            for k in range(nch):
                out_ref[k, 0] = both[:, k * width : (k + 1) * width]

    return call(
        body,
        (4,),
        [
            (table, None),
            (gy_a, (1, R, MID), lambda i: (i, 0, 0)),
            (conv_a, (1, R, MID), lambda i: (i, 0, 0)),
            whole(sums_a),
            whole(grad_a),
            whole(affine_a),
            whole(weight),
            whole(skip_grad),
            whole(inner),
        ],
        [
            ((4, R, MID), BF, (1, R, MID), lambda i: (i, 0, 0)),
            ((nch, 4, R, width), BF, (nch, 1, R, width), lambda i: (0, i, 0, 0)),
        ],
        [pltpu.VMEM((R, MID), F32)],
        flops=2 * 4 * R * cin * MID,
        moved=4 * R * (10 * MID + 2 * cin) + 2 * cin * MID + 4 * R * cin,
    )


def after(value, *others):
    return lax.optimization_barrier((value,) + others)[0]


NEAR = [(i, i ^ 1) for i in range(Q)]
FAR = [(i, i ^ 2) for i in range(Q)]


def gather_far(part, nch):
    return lax.ppermute(part, "chan", FAR) if nch == Q else None


def gather_rest(part, other, nch, *when):
    if nch == Q:
        c = lax.axis_index("chan")
        part, other = lax.optimization_barrier((part, other) + when)[:2]
        parts = [part, lax.ppermute(part, "chan", NEAR), other, lax.ppermute(other, "chan", NEAR)]
        return place(parts, c)
    full = lax.all_gather(part, "chan", axis=part.ndim - 1, tiled=True)
    cut = full.reshape(full.shape[:-1] + (Q, full.shape[-1] // Q))
    return jnp.moveaxis(cut, -2, 0)


def place(parts, c):
    shape = parts[0].shape
    cuts = shape[0] if len(shape) == 3 else (2 if shape[0] % 32 == 0 else 1)
    rows = shape[0] // cuts

    def body(c_ref, *refs):
        ins, out, held, in_sems, out_sems = refs[:Q], refs[Q], refs[Q + 1], refs[Q + 2], refs[Q + 3]
        into, away = [], []
        for i in range(cuts):
            for k in range(Q):
                span = pl.ds(i * rows, rows)
                into.append(pltpu.make_async_copy(ins[k].at[span], held.at[k, span], in_sems.at[k, i]))
                goal = out.at[jnp.bitwise_xor(c_ref[0], k), span]
                away.append(pltpu.make_async_copy(held.at[k, span], goal, out_sems.at[k, i]))
        for copy in into:
            copy.start()
        for copy, leave in zip(into, away):
            copy.wait()
            leave.start()
        for leave in away:
            leave.wait()

    return pl.pallas_call(
        body,
        in_specs=[pl.BlockSpec(memory_space=pltpu.SMEM)] + [pl.BlockSpec(memory_space=pl.ANY)] * Q,
        out_specs=pl.BlockSpec(memory_space=pl.ANY),
        out_shape=jax.ShapeDtypeStruct((Q,) + shape, parts[0].dtype),
        scratch_shapes=[
            pltpu.VMEM((Q,) + shape, parts[0].dtype),
            pltpu.SemaphoreType.DMA((Q, cuts)),
            pltpu.SemaphoreType.DMA((Q, cuts)),
        ],
        compiler_params=pltpu.CompilerParams(vmem_limit_bytes=VMEM_LIMIT),
        cost_estimate=pl.CostEstimate(flops=0, bytes_accessed=4 * Q * parts[0].size, transcendentals=0),
    )(c.reshape(1).astype(jnp.int32), *parts)


def exchange(pick, nch):
    c = lax.axis_index("chan")
    parts = [pick(c)]
    for k in (3, 2, 1):
        parts.insert(1, lax.ppermute(pick(jnp.bitwise_xor(c, k)), "chan", [(i, i ^ k) for i in range(Q)]))
    return place(parts, c)


def to_subnets(maps, order, groups, nch, *tokens):
    if groups == 1:

        def pick(member):
            part = order(lax.dynamic_index_in_dim(maps, member, 0, keepdims=True))[0]
            return after(part, *tokens) if tokens else part

        return exchange(pick, nch)
    blocks = order(maps)
    images = 8 // groups
    shape = blocks.shape
    cut = blocks.reshape(shape[:-2] + (49, groups, images, shape[-1]))
    cut = jnp.moveaxis(cut, -3, 1)
    cut = jnp.pad(cut, [(0, 0)] * (cut.ndim - 2) + [(0, 8 - images), (0, 0)])
    blocks = cut.reshape((shape[0] * groups,) + shape[1:])
    return lax.all_to_all(blocks, "chan", 0, 0)


def from_subnets(blocks, groups, nch):
    if groups == 1:
        return exchange(lambda member: lax.dynamic_index_in_dim(blocks, member, 0, keepdims=False), nch)
    back = lax.all_to_all(blocks, "chan", 0, 0)
    images = 8 // groups
    shape = back.shape
    cut = back.reshape((shape[0] // groups, groups) + shape[1:-2] + (49, 8, shape[-1]))[..., :images, :]
    cut = jnp.moveaxis(cut, 1, -3)
    return cut.reshape((shape[0] // groups,) + shape[1:-2] + (R, shape[-1]))


def sum_pairs(one, two):
    cut = [part.reshape(part.shape[0], 1, Q, -1) for part in (one, two)]
    return jnp.concatenate(cut, axis=3).reshape(one.shape[0], 1, -1)


def make_sync(groups, nch):
    def sync(sums):
        got = lax.all_to_all(sums, "batch", 0, 0)
        if groups > 1:
            pairs = [[g * groups + k for k in range(groups)] for g in range(nch // groups)]
            got = lax.psum(got, "chan", axis_index_groups=pairs)
        return got

    return sync


def weight_product(pairs, columns, plus, width, apart):
    every = columns is None
    depths = [left.shape[1] if left.ndim == 2 else left.shape[0] * left.shape[3] for left, _ in pairs]
    depth = sum(depths)
    if len(pairs) > 1 or pairs[0][0].ndim == 4:
        step = min(256, pairs[-1][0].shape[-1])
    else:
        step = {4608: 1536, 2048: 1024}.get(depth, 512)
    starts = [sum(depths[:m]) // step for m in range(len(pairs) + 1)]

    def local(i, m):
        return jnp.clip(i - starts[m], 0, starts[m + 1] - starts[m] - 1)

    args, specs = [], []
    for m, (left, grad) in enumerate(pairs):
        phases, rows = grad.shape[0], grad.shape[1]
        args.append(left)
        if left.ndim == 2:
            specs.append(pl.BlockSpec((rows, step), lambda i, c, m=m: (0, local(i, m))))
        else:
            specs.append(pl.BlockSpec((1, phases, rows, step), lambda i, c, m=m: (local(i, m), 0, 0, 0)))
        if every:
            args.append(grad)
            specs.append(pl.BlockSpec(grad.shape, lambda i, c: (0, 0, 0)))
        else:
            for k in range(2):
                args.append(grad)
                specs.append(pl.BlockSpec((phases, rows, width), lambda i, c, k=k: (0, 0, c[k])))
    each = 2 if every else 3
    pair = pl.BlockSpec((2, step, width), lambda i, c: (0, i, 0))
    if plus is not None:
        args.append(plus)
        specs.append(pair)

    def one(m, refs, more, outs):
        left, grad = pairs[m]
        l_ref = refs[0]
        value = None
        for p in range(grad.shape[0]):
            right = refs[1][p] if every else jnp.concatenate([refs[1][p], refs[2][p]], axis=1)
            piece = dot(l_ref[...] if left.ndim == 2 else l_ref[0, p], right, TN)
            value = piece if value is None else value + piece
        for k in range(Q if every else 2):
            part = value[:, k * width : (k + 1) * width]
            if more is not None:
                part = part + more[k].astype(F32)
            if apart:
                outs[k][...] = part.astype(BF)
            else:
                outs[0][k] = part.astype(BF)

    def body(c_ref, *refs):
        ins, outs = refs[: len(args)], refs[len(args) :]
        more = ins[-1] if plus is not None else None
        if len(pairs) == 1:
            one(0, ins, more, outs)
            return
        i = pl.program_id(0)
        for m in range(len(pairs)):

            @pl.when(jnp.logical_and(i >= starts[m], i < starts[m + 1]))
            def _(m=m):
                one(m, ins[each * m : each * m + each], more, outs)

    single = pl.BlockSpec((step, width), lambda i, c: (i, 0))
    block = jax.ShapeDtypeStruct((depth, width), BF)
    if every:
        out_specs = pl.BlockSpec((Q, step, width), lambda i, c: (0, i, 0))
        out_shape = jax.ShapeDtypeStruct((Q, depth, width), BF)
    elif apart:
        out_specs, out_shape = [single, single], [block, block]
    else:
        out_specs, out_shape = pair, jax.ShapeDtypeStruct((2, depth, width), BF)
    flops = sum(4 * left.size * width for left, _ in pairs)
    return pl.pallas_call(
        body,
        grid_spec=pltpu.PrefetchScalarGridSpec(
            num_scalar_prefetch=1, grid=(depth // step,), in_specs=specs, out_specs=out_specs
        ),
        out_shape=out_shape,
        compiler_params=pltpu.CompilerParams(vmem_limit_bytes=VMEM_LIMIT),
        cost_estimate=pl.CostEstimate(flops=0, bytes_accessed=0, transcendentals=0),
    )(jnp.zeros((1,), jnp.int32) if every else columns, *args)


class Reduce:
    def __init__(self, nb, nch, *pairs, lead=()):
        self.nb, self.nch, self.lead = nb, nch, lead
        self.pairs = [(left, grad if grad.ndim == 3 else grad[None]) for left, grad in pairs]
        self.width = self.pairs[0][1].shape[2] // nch
        self.depths = [left.shape[1] if left.ndim == 2 else left.shape[0] * left.shape[3] for left, _ in pairs]
        self.depth = sum(self.depths)
        self.quick = nch == Q

    def first(self):
        if not self.quick:
            parts = []
            for (left, grad), depth in zip(self.pairs, self.depths):
                if left.ndim == 4:
                    left = jnp.transpose(left[:, : grad.shape[0]], (1, 2, 0, 3)).reshape(-1, depth)
                parts.append(dot(left, grad.reshape(-1, grad.shape[2]), TN).astype(BF))
            full = jnp.concatenate(parts, axis=0)
            self.terms = [lax.psum_scatter(full, "chan", scatter_dimension=1, tiled=True)]
            return []
        c = lax.axis_index("chan").astype(jnp.int32)
        self.value = weight_product(self.pairs, jnp.stack([c ^ 1, c ^ 3]), None, self.width, False)
        return [self.value]

    def near(self, held=None):
        if self.quick:
            self.value = lax.ppermute(held[0], "chan", NEAR)

    def second(self):
        if not self.quick:
            return []
        c = lax.axis_index("chan").astype(jnp.int32)
        out = weight_product(self.pairs, jnp.stack([c, c ^ 2]), self.value, self.width, True)
        return list(out)

    def far(self, held=None):
        if self.quick:
            self.terms = [held[0], lax.ppermute(held[1], "chan", FAR)]

    def pieces(self, together=True):
        outs = []
        for terms in [self.terms] if together else [[term] for term in self.terms]:
            at = 0
            for depth in self.depths:
                rows = depth // self.nb
                outs.append((terms, self.lead, at // rows, rows, self.width))
                at += depth
        return outs


def total_rows(piece):
    _, _, _, rows, width = piece
    return rows * (width // 128)


def half_sum(pieces, which, gots=None):
    args, specs = [], []
    for terms, lead, first, rows, width in pieces:
        for term in terms:
            if lead:
                args.append(term.reshape(lead + (8, rows // lead[0], width)))
                block = lead + (1, rows // lead[0], width)
                specs.append(pl.BlockSpec(block, lambda i, c: (0, 2 * i + c[0], 0, 0)))
            else:
                args.append(term)
                specs.append(pl.BlockSpec((rows, width), lambda i, c, first=first: (first + 2 * i + c[0], 0)))
    count = len(args)
    for got in gots or []:
        args.append(got)
        specs.append(pl.BlockSpec((1,) + got.shape[1:], lambda i, c: (i, 0, 0)))
    height = sum(total_rows(piece) for piece in pieces)

    def body(c_ref, *refs):
        out = refs[-1]
        parts = []
        at = 0
        for terms, lead, _, rows, width in pieces:
            total = None
            for ref in refs[at : at + len(terms)]:
                part = ref[...].reshape(rows, width).astype(F32)
                total = part if total is None else total + part
            at += len(terms)
            parts += [total[:, 128 * k : 128 * k + 128] for k in range(width // 128)]
        value = jnp.concatenate(parts, axis=0) if len(parts) > 1 else parts[0]
        if gots:
            more = [ref[0].astype(F32) for ref in refs[count : count + len(gots)]]
            value = value + (jnp.concatenate(more, axis=0) if len(more) > 1 else more[0])
        out[0] = value.astype(BF)

    return pl.pallas_call(
        body,
        grid_spec=pltpu.PrefetchScalarGridSpec(
            num_scalar_prefetch=1,
            grid=(4,),
            in_specs=specs,
            out_specs=pl.BlockSpec((1, height, 128), lambda i, c: (i, 0, 0)),
        ),
        out_shape=jax.ShapeDtypeStruct((4, height, 128), BF),
        compiler_params=pltpu.CompilerParams(vmem_limit_bytes=VMEM_LIMIT),
        cost_estimate=pl.CostEstimate(flops=0, bytes_accessed=0, transcendentals=0),
    )(which.reshape(1).astype(jnp.int32), *args)


def split_total(total, pieces):
    outs = []
    at = 0
    for piece in pieces:
        rows, width = piece[3], piece[4]
        part = total[at : at + total_rows(piece)]
        at += total_rows(piece)
        if width > 128:
            part = jnp.transpose(part.reshape(width // 128, rows, 128), (1, 0, 2)).reshape(rows, width)
        outs.append(part)
    return outs


def along_x(send):
    return lax.ppermute(send, "batch", [(i, i ^ 1) for i in range(8)])


def along_z(keep):
    lines = [[2 * k + x for k in range(4)] for x in range(2)]
    return lax.all_to_all(keep, "batch", 0, 0, axis_index_groups=lines)


def along_z_parts(keep, z):
    parts = [lax.dynamic_index_in_dim(keep, z, 0, keepdims=False)]
    for k in (3, 2, 1):
        block = lax.dynamic_index_in_dim(keep, jnp.bitwise_xor(z, k), 0, keepdims=False)
        parts.append(lax.ppermute(block, "batch", [(i, i ^ (2 * k)) for i in range(8)]))
    return parts


def batch_scatter(member, nb):
    total = member.terms[0]
    outs = []
    at = 0
    for depth in member.depths:
        part = total[at : at + depth]
        at += depth
        if member.lead:
            part = jnp.moveaxis(part.reshape(member.lead + (nb, -1, member.width)), 1, 0)
        part = part.reshape(nb, depth // nb, member.width)
        outs.append(lax.psum_scatter(part, "batch", scatter_dimension=0, tiled=True)[0].astype(F32))
    return outs


def slot(value, *groups):
    flat = [array for group in groups for array in group]
    held = lax.optimization_barrier((value, *flat))
    out = []
    at = 1
    for group in groups:
        out.append(list(held[at : at + len(group)]))
        at += len(group)
    return [held[0]] + out


def body(
    inputs, weight_in, kernel_one, weight_out, weight_skip, second_in, kernel_two, second_out, norm_reduce,
    norm_kernel, norm_expand, norm_skip, later_reduce, later_kernel, later_expand, widths, depths, counts, cotangent,
    *, nb, nch,
):
    subnets, per = inputs.shape[0], inputs.shape[1]
    groups = nch // subnets
    images = per // groups
    chan = lax.axis_index("chan")
    member, half = chan // groups, chan % groups
    slots = jnp.arange(8, dtype=jnp.int32)
    ids = lax.axis_index("batch") * per + half * images + slots
    count = counts[member]
    live_image = jnp.logical_and(slots < images, ids < count).astype(F32)[:, None]
    live = jnp.broadcast_to(live_image, (8, MID))
    inner = live * (jnp.arange(MID, dtype=jnp.int32) < widths[member]).astype(F32)[None, :]
    high, low = inputs.shape[2], cotangent.shape[2]
    table = jnp.stack(
        [
            count.astype(F32) * (high * high),
            count.astype(F32) * (low * low),
            (depths[member] == 2).astype(F32),
        ]
    )
    sync = make_sync(groups, nch)

    small = (norm_reduce, norm_kernel, later_reduce, later_kernel)
    large = (norm_expand, norm_skip, later_expand)
    joined = jnp.concatenate(small + large, axis=1)
    spread = lax.all_to_all(jnp.broadcast_to(joined[None], (nch,) + joined.shape), "chan", 0, 0)
    at = 0
    full = []
    for part in small + large:
        piece = lax.slice_in_dim(spread, at, at + part.shape[1], axis=2)
        full.append(jnp.moveaxis(piece, 0, 1).reshape(2, -1))
        at += part.shape[1]
    flat_one = kernel_one.reshape((9,) + kernel_one.shape[2:])
    flat_two = kernel_two.reshape((9,) + kernel_two.shape[2:])
    far = gather_far(weight_in, nch)
    slabs = to_subnets(inputs, rows_in, groups, nch, *([far] if nch == Q else []))
    slabs, full = slot(slabs, full)
    aff_a, aff_b, aff_d, aff_e, aff_c, aff_s, aff_f = full
    w_in = gather_rest(weight_in, far, nch)
    far_one = gather_far(after(flat_one, slabs), nch)
    far_out = gather_far(after(weight_out, w_in), nch)

    conv_a, sums = stage_a(slabs, w_in, live, nb)
    far_in = gather_far(after(second_in, sums), nch)
    far_skip = gather_far(after(weight_skip, sums), nch)
    sums_a = sync(sums)
    k_one = gather_rest(flat_one, far_one, nch, sums_a)
    cols_a, conv_b, sums = stage_conv_one(conv_a, sums_a, aff_a, inner, live, k_one, table, nb)
    w_out = gather_rest(weight_out, far_out, nch, sums)
    s_in = gather_rest(second_in, far_in, nch, sums)
    sums_b = sync(sums)
    sums_b, (w_out, s_in) = slot(sums_b, [w_out, s_in])
    act_b, conv_c, sums = stage_expand(conv_b, sums_b, aff_b, inner, live, w_out, table, nb)
    far_two = gather_far(after(flat_two, sums), nch)
    w_skip = gather_rest(weight_skip, far_skip, nch, sums)
    sums_c = sync(sums)
    conv_s, sums = stage_skip(slabs, w_skip, live, nb)
    sums_s = sync(sums)
    sums_c = sum_pairs(sums_c, sums_s)
    first, first_low, conv_d, sums = stage_join(conv_c, sums_c, aff_c, conv_s, aff_s, live, s_in, table, nb)
    far_sout = gather_far(after(second_out, sums), nch)
    k_two = gather_rest(flat_two, far_two, nch, sums)
    sums_d = sync(sums)
    sums_d, (k_two,) = slot(sums_d, [k_two])
    cols_d, conv_e, sums = stage_conv_two(conv_d, sums_d, aff_d, inner, live, k_two, table, nb)
    cot = to_subnets(cotangent, small_in, groups, nch, sums)
    s_out = gather_rest(second_out, far_sout, nch, sums)
    sums_e = sync(sums)
    sums_e, (s_out,) = slot(sums_e, [s_out])
    act_e, conv_f, sums = stage_expand(conv_e, sums_e, aff_e, inner, live, s_out, table, nb)
    sums_f = sync(sums)
    sums_f, (cot,) = slot(sums_f, [cot])
    result, grad_sum, sums = stage_result(conv_f, sums_f, aff_f, first, cot, live, table, nb)
    grads_f = sync(sums)
    result = small_out(from_subnets(result, groups, nch), subnets)

    low_f, gy_e, sums = stage_back_f(
        grad_sum, conv_f, sums_f, grads_f, aff_f, live, s_out, conv_e, sums_e, aff_e, inner, table, nb
    )
    grads_e = sync(sums)
    quick = nch == Q and nb == 8
    b_index = lax.axis_index("batch")
    x_index, z_index = b_index % 2, b_index // 2

    d_sout = Reduce(nb, nch, (act_e, low_f))
    grads_e, x = slot(grads_e, d_sout.first())
    d_sout.near(x)
    low_e, gy_d, sums = stage_back_two(
        gy_e, conv_e, sums_e, grads_e, aff_e, k_two, conv_d, sums_d, aff_d, inner, table, nb
    )
    grads_d = sync(sums)
    d_two = Reduce(nb, nch, (cols_d, low_e), lead=(9,))
    grads_d, x, y, (result,) = slot(grads_d, d_sout.second(), d_two.first(), [result])
    d_sout.far(x)
    d_two.near(y)
    low_d, grad_one, sums = stage_back_join(
        gy_d, conv_d, sums_d, grads_d, aff_d, inner, s_in, cot, grad_sum, conv_c, sums_c, aff_c, conv_s,
        aff_s, live, table, nb,
    )
    grads_j = sync(sums)
    d_sin = Reduce(nb, nch, (first_low, low_d))
    grads_j, y, z, d_sout.terms = slot(grads_j, d_two.second(), d_sin.first(), d_sout.terms)
    d_two.far(y)
    d_sin.near(z)
    low_c, low_s, gy_b, sums = stage_back_first(
        grad_one, grads_j, conv_c, sums_c, aff_c, conv_s, aff_s, live, w_out, conv_b, sums_b, aff_b, inner,
        table, nb,
    )
    grads_b = sync(sums)
    d_both = Reduce(nb, nch, (act_b, low_c), (slabs, low_s))
    skip_grad = stage_back_skip(low_s, w_skip)
    grads_b, x, y, d_two.terms = slot(grads_b, d_sin.second(), d_both.first(), d_two.terms)
    d_sin.far(x)
    d_both.near(y)
    early = []
    send = []
    if quick:
        early = d_sout.pieces() + d_two.pieces()
        send = [half_sum(early, 1 - x_index)]
    grads_b, send = slot(grads_b, send)
    got = along_x(send[0]) if quick else None
    low_b, gy_a, sums = stage_back_one(
        gy_b, conv_b, sums_b, grads_b, aff_b, k_one, conv_a, sums_a, aff_a, inner, table, nb
    )
    grads_a = sync(sums)
    d_one = Reduce(nb, nch, (cols_a, low_b), lead=(9,))
    kept = [half_sum(early, x_index, [got])] if quick else []
    grads_a, y, z, (skip_grad,), kept, d_sin.terms = slot(
        grads_a, d_one.first(), d_both.second(), [skip_grad], kept, d_sin.terms
    )
    d_one.near(y)
    d_both.far(z)
    ones = d_one.second()
    if quick:
        d_one.terms = ones
        one_pieces = d_one.pieces(False)
        ones = [half_sum(one_pieces, 1 - x_index)]
    grads_a, ones = slot(grads_a, ones)
    if quick:
        one_got = along_x(ones[0])
    else:
        d_one.far(ones)
    low_a, grad_in = stage_back_in(gy_a, conv_a, sums_a, grads_a, aff_a, w_in, skip_grad, inner, table, nch)
    d_in = Reduce(nb, nch, (slabs, low_a))
    if quick:
        grad_in = lax.all_to_all(grad_in, "chan", 0, 0)
    else:
        grad_in = from_subnets(grad_in, groups, nch)
    x = d_in.first()
    d_in.near(x)
    ins = d_in.second()
    if quick:
        early_parts = along_z_parts(after(kept[0], low_a), z_index)
        d_in.terms = ins
        in_pieces = d_in.pieces(False)
        one_kept = after(half_sum(one_pieces, x_index, [one_got]), low_a)
        held = lax.optimization_barrier(tuple(d_both.terms) + (one_kept,))
        d_both.terms, one_kept = list(held[:2]), held[2]
        one_parts = along_z_parts(one_kept, z_index)
        middle = d_sin.pieces() + d_both.pieces()
        middle_got = along_x(half_sum(middle, 1 - x_index))
        in_got = along_x(half_sum(in_pieces, 1 - x_index))
        middle_parts = along_z_parts(half_sum(middle + in_pieces, x_index, [middle_got, in_got]), z_index)
        outs = []
        for parts, pieces in ((early_parts, early), (one_parts, one_pieces), (middle_parts, middle + in_pieces)):
            total = parts[0].astype(F32)
            for part in parts[1:]:
                total = total + part.astype(F32)
            outs += split_total(total, pieces)
        (
            second_out_grad, kernel_two_grad, one_own, one_far, second_in_grad, weight_out_grad, weight_skip_grad,
            in_own, in_far,
        ) = outs
        across = lax.ppermute(jnp.concatenate([one_far, in_far], axis=0).astype(BF), "chan", FAR).astype(F32)
        kernel_one_grad = one_own + across[: one_own.shape[0]]
        weight_in_grad = in_own + across[one_own.shape[0] :]
    else:
        d_in.far(ins)
        if nch == Q:
            for member in (d_sout, d_two, d_sin, d_both, d_one, d_in):
                member.terms = [(member.terms[0].astype(F32) + member.terms[1].astype(F32)).astype(BF)]
        (second_out_grad,), (kernel_two_grad,) = batch_scatter(d_sout, nb), batch_scatter(d_two, nb)
        (second_in_grad,), (kernel_one_grad,) = batch_scatter(d_sin, nb), batch_scatter(d_one, nb)
        (weight_out_grad, weight_skip_grad), (weight_in_grad,) = batch_scatter(d_both, nb), batch_scatter(d_in, nb)
    inputs_grad = rows_out(grad_in, subnets)

    def pair(sums, parts, which):
        total = jnp.sum(sums, axis=0).reshape(-1, parts, MID)
        both = jnp.stack([total[:, which].reshape(-1), total[:, 0].reshape(-1)])
        return both.reshape(2, nch, -1)

    norm_parts = [
        pair(grads_a, 2, 1), pair(grads_b, 2, 1), pair(grads_j, 3, 1), pair(grads_j, 3, 2), pair(grads_d, 2, 1),
        pair(grads_e, 2, 1), pair(grads_f, 2, 1),
    ]
    joined = after(jnp.moveaxis(jnp.concatenate(norm_parts, axis=2), 1, 0), grad_in)
    mine = jnp.sum(lax.all_to_all(joined, "chan", 0, 0), axis=0) / groups
    norm_grads = []
    at = 0
    for part in norm_parts:
        norm_grads.append(mine[:, at : at + part.shape[2]])
        at += part.shape[2]

    shape = (3, 3, MID // nb, MID // nch)
    return (
        result, inputs_grad, weight_in_grad, kernel_one_grad.reshape(shape), weight_out_grad, weight_skip_grad,
        second_in_grad, kernel_two_grad.reshape(shape), second_out_grad, *norm_grads,
    )


def solution(mesh):
    nb, nch = mesh.shape["batch"], mesh.shape["chan"]
    maps = P(None, "batch", None, None, "chan")
    cols = P(None, "chan")
    taps = P(None, None, None, "chan")
    in_specs = (maps, cols, taps, cols, cols, cols, taps, cols) + (cols,) * 7 + (P(), P(), P(), maps)
    both = P("batch", "chan")
    split = P(None, None, "batch", "chan")
    out_specs = (maps, maps, both, split, both, both, both, split, both) + (cols,) * 7

    def run(*args):
        return body(*args, nb=nb, nch=nch)

    return jax.shard_map(run, mesh=mesh, in_specs=in_specs, out_specs=out_specs, check_vma=False)
```
